256 devices in a mesh: rep: 4 (over x_hi, core), lat: 8 (over x_lo, y), lon: 8 (over z).
Axes of the slice: x: 4 (x_hi: 2, x_lo: 2; x = x_hi * 2 + x_lo), y: 4, z: 8, core: 2. Of those that a mesh axis runs over, the one named last changes fastest.
Arguments:
- tokens: bfloat16 [4, 8, 48, 96, 192], P('rep', None, 'lat', 'lon'), may hold values from -6 to 6
- cotangent: bfloat16 [4, 8, 48, 96, 192], P('rep', None, 'lat', 'lon'), may hold values from -6 to 6
- gain_a: float32 [192], replicated, may hold values from 0.1 to 1.9
- qkv_a: bfloat16 [192, 576], replicated, may hold values from -0.4375 to 0.4375
- out_a: bfloat16 [192, 192], replicated, may hold values from -0.4375 to 0.4375
- bias_a: float32 [6, 144, 144], replicated, may hold values from -6 to 330
- gain_b: float32 [192], replicated, may hold values from 0.1 to 1.9
- qkv_b: bfloat16 [192, 576], replicated, may hold values from -0.4375 to 0.4375
- out_b: bfloat16 [192, 192], replicated, may hold values from -0.4375 to 0.4375
- bias_b: float32 [6, 144, 144], replicated, may hold values from -6 to 330
Outputs:
- d_tokens: bfloat16 [4, 8, 48, 96, 192], P('rep', None, 'lat', 'lon')
- gain_grad_a: float32 [192], replicated
- qkv_grad_a: float32 [192, 576], replicated
- out_grad_a: float32 [192, 192], replicated
- bias_grad_a: float32 [6, 144, 144], replicated
- gain_grad_b: float32 [192], replicated
- qkv_grad_b: float32 [192, 576], replicated
- out_grad_b: float32 [192, 192], replicated
- bias_grad_b: float32 [6, 144, 144], replicated
The draws below stay inside these ranges and needn't reach their ends.
All inputs are finite; a program needn't handle non-finite values.
Results may differ from the reference program's by a relative error of at most 0.028.
Values may be sent and summed in bfloat16 or wider, within the bound.
A program may use at most 64 MiB of HBM per device.

```python
import jax
import jax.numpy as jnp
from jax import lax

C = 192
HEADS = 6
LEVELS = 8
WZ = 2
WLAT = 6
WLON = 12
WT = 144
SZ = 1
SLAT = 3
SLON = 6
BATCH = 4
LAT = 48
LON = 96


def draw_bias_a(key, part):
    key = jax.random.fold_in(key, 11)
    return jnp.clip(jax.random.normal(key, (HEADS, WT, WT), jnp.float32), -6.0, 6.0)


def draw_bias_b(key, part):
    key = jax.random.fold_in(key, 12)
    return jnp.clip(jax.random.normal(key, (HEADS, WT, WT), jnp.float32), -6.0, 6.0)


def shard_levels(stream_key, shape, cuts, smallest, high):
    factor_of = 1.0
    for axis_at, parts in cuts:
        steps = jax.random.uniform(jax.random.fold_in(jax.random.fold_in(stream_key, 6), axis_at), (parts,), jnp.float32, smallest / len(cuts), high / len(cuts))
        factor_of = factor_of * jnp.repeat(jnp.exp(steps), shape[axis_at] // parts).reshape((-1,) + (1,) * (len(shape) - 1 - axis_at))
    return factor_of


def gaussian(own_key, shape, scale, limit, shards=(), kind=jnp.bfloat16):
    result = scale * jax.random.normal(own_key, shape, jnp.float32)
    if shards:
        result = result * shard_levels(own_key, shape, shards, -0.22, 0.18)
    return jnp.clip(result, -limit, limit).astype(kind)


def setup_inputs(seed: int = 0) -> dict:
    splits = jax.random.split(jax.random.key(seed), 11)
    tokens = gaussian(splits[0], (BATCH, LEVELS, LAT, LON, C), 1.0, 6.0, ((0, 4), (2, 8), (3, 8)))
    cotangent = gaussian(splits[1], (BATCH, LEVELS, LAT, LON, C), 1.0, 6.0, ((0, 4), (2, 8), (3, 8)))
    gain_a = jnp.clip(1.0 + 0.18 * jax.random.normal(splits[2], (C,), jnp.float32), 0.1, 1.9)
    qkv_a = gaussian(splits[3], (C, 3 * C), C ** -0.5, 0.4375)
    out_a = gaussian(splits[4], (C, C), C ** -0.5, 0.4375)
    bias_a = draw_bias_a(jax.random.fold_in(splits[10], 71), 0)
    gain_b = jnp.clip(1.0 + 0.18 * jax.random.normal(splits[6], (C,), jnp.float32), 0.1, 1.9)
    qkv_b = gaussian(splits[7], (C, 3 * C), C ** -0.5, 0.4375)
    out_b = gaussian(splits[8], (C, C), C ** -0.5, 0.4375)
    bias_b = draw_bias_b(jax.random.fold_in(splits[10], 71), 0)
    return dict(tokens=tokens, cotangent=cotangent, gain_a=gain_a, qkv_a=qkv_a, out_a=out_a, bias_a=bias_a, gain_b=gain_b, qkv_b=qkv_b, out_b=out_b, bias_b=bias_b)


def to_windows(grid, wz, wl, wo):
    b, z, l, o, c = grid.shape
    boxed = grid.reshape(b, z // wz, wz, l // wl, wl, o // wo, wo, c)
    boxed = boxed.transpose(0, 1, 3, 5, 2, 4, 6, 7)
    return boxed.reshape(-1, wz * wl * wo, c)

def from_windows(windows_in, full_shape, wz, wl, wo):
    b, z, l, o, c = full_shape
    boxed = windows_in.reshape(b, z // wz, l // wl, o // wo, wz, wl, wo, c)
    boxed = boxed.transpose(0, 1, 4, 2, 5, 3, 6, 7)
    return boxed.reshape(b, z, l, o, c)

def attend_forward(block_in, labels, gain, w_qkv, w_out, bias):
    count, window_len, width = block_in.shape
    heads = bias.shape[0]
    head_width = width // heads
    factor = head_width ** (-0.5)
    flat = block_in.reshape(-1, width).astype(jnp.float32)
    center = flat - lax.optimization_barrier(jnp.mean(flat, axis=-1, keepdims=True))
    inv_std = lax.rsqrt(lax.optimization_barrier(jnp.mean(center * center, axis=-1, keepdims=True)) + 1e-05)
    unit = center * inv_std
    normed = (unit * gain).astype(jnp.bfloat16)
    qkv = jnp.dot(normed, w_qkv, preferred_element_type=jnp.float32).astype(jnp.bfloat16)
    qkv = qkv.reshape(count, window_len, 3, heads, head_width).transpose(2, 0, 3, 1, 4)
    query, key, value = (qkv[0], qkv[1], qkv[2])
    scores = jnp.einsum('nhad,nhbd->nhab', query.astype(jnp.float32), key.astype(jnp.float32)) * factor + bias
    if labels is not None:
        allowed = labels[:, None, :, None] == labels[:, None, None, :]
        scores = jnp.where(allowed, scores, -1e+30)
    probs = jax.nn.softmax(scores, axis=-1)
    probs_bf = probs.astype(jnp.bfloat16)
    attended = jnp.einsum('nhab,nhbd->nhad', probs_bf.astype(jnp.float32), value.astype(jnp.float32)).astype(jnp.bfloat16)
    attended = attended.transpose(0, 2, 1, 3).reshape(-1, width)
    mixed = jnp.dot(attended, w_out, preferred_element_type=jnp.float32)
    block_out = (flat + mixed).astype(jnp.bfloat16).reshape(count, window_len, width)
    return (block_out, (unit, inv_std, normed, query, key, value, probs, probs_bf, attended))

def attend_backward(cache, incoming, gain, w_qkv, w_out):
    unit, inv_std, normed, query, key, value, probs, probs_bf, attended = cache
    count, heads, window_len, head_width = query.shape
    width = heads * head_width
    factor = head_width ** (-0.5)
    flat_in = incoming.reshape(-1, width)
    out_grad = jnp.dot(attended.T, flat_in, preferred_element_type=jnp.float32)
    d_attended = jnp.dot(flat_in, w_out.T, preferred_element_type=jnp.float32).astype(jnp.bfloat16)
    d_attended = d_attended.reshape(count, window_len, heads, head_width).transpose(0, 2, 1, 3)
    d_probs = jnp.einsum('nhad,nhbd->nhab', d_attended.astype(jnp.float32), value.astype(jnp.float32))
    d_value = jnp.einsum('nhab,nhad->nhbd', probs_bf.astype(jnp.float32), d_attended.astype(jnp.float32)).astype(jnp.bfloat16)
    d_scores = probs * (d_probs - lax.optimization_barrier(jnp.sum(probs * d_probs, axis=-1, keepdims=True)))
    bias_grad = lax.optimization_barrier(jnp.sum(d_scores, axis=0))
    d_scaled = (d_scores * factor).astype(jnp.bfloat16)
    d_query = jnp.einsum('nhab,nhbd->nhad', d_scaled.astype(jnp.float32), key.astype(jnp.float32)).astype(jnp.bfloat16)
    d_key = jnp.einsum('nhab,nhad->nhbd', d_scaled.astype(jnp.float32), query.astype(jnp.float32)).astype(jnp.bfloat16)
    d_qkv = jnp.stack([d_query, d_key, d_value], axis=0).transpose(1, 3, 0, 2, 4).reshape(-1, 3 * width)
    qkv_grad = jnp.dot(normed.T, d_qkv, preferred_element_type=jnp.float32)
    d_normed = jnp.dot(d_qkv, w_qkv.T, preferred_element_type=jnp.float32)
    gain_grad = lax.optimization_barrier(jnp.sum(d_normed * unit, axis=0))
    d_hat = d_normed * gain
    d_input = flat_in.astype(jnp.float32) + inv_std * (d_hat - lax.optimization_barrier(jnp.mean(d_hat, axis=-1, keepdims=True)) - unit * lax.optimization_barrier(jnp.mean(d_hat * unit, axis=-1, keepdims=True)))
    return (d_input.reshape(count, window_len, width), (gain_grad, qkv_grad, out_grad, bias_grad))

def reference(tokens, cotangent, gain_a, qkv_a, out_a, bias_a, gain_b, qkv_b, out_b, bias_b):
    full_shape = tokens.shape
    group = LAT // WLAT * (LON // WLON)

    def blocks(grid):
        windows_in = to_windows(grid, WZ, WLAT, WLON)
        return windows_in.reshape(-1, group, windows_in.shape[1], windows_in.shape[2])

    def grid_of(blocked):
        return from_windows(blocked.reshape(-1, blocked.shape[2], blocked.shape[3]), full_shape, WZ, WLAT, WLON)

    def forward_regular(block_in):
        return attend_forward(block_in, None, gain_a, qkv_a, out_a, bias_a)[0]
    middle = grid_of(lax.map(forward_regular, blocks(tokens)))
    rolled = jnp.roll(middle, (-SZ, -SLAT, -SLON), axis=(1, 2, 3))
    rolled_cot = jnp.roll(cotangent, (-SZ, -SLAT, -SLON), axis=(1, 2, 3))
    level_index = jnp.arange(LEVELS, dtype=jnp.int32)[:, None, None]
    row_index = jnp.arange(LAT, dtype=jnp.int32)[None, :, None]
    labels = 2 * (level_index >= LEVELS - SZ).astype(jnp.int32) + (row_index >= LAT - SLAT).astype(jnp.int32)
    labels = jnp.broadcast_to(labels, (full_shape[0], LEVELS, LAT, LON))[..., None]
    label_blocks = blocks(labels)[..., 0]
    zeros = (jnp.zeros((C,), jnp.float32), jnp.zeros((C, 3 * C), jnp.float32), jnp.zeros((C, C), jnp.float32), jnp.zeros((HEADS, WT, WT), jnp.float32))

    def step_shifted(totals, items):
        block_in, block_cot, block_lab = items
        cache = attend_forward(block_in, block_lab, gain_b, qkv_b, out_b, bias_b)[1]
        d_input, grads = attend_backward(cache, block_cot, gain_b, qkv_b, out_b)
        return (tuple((total + grad for total, grad in zip(totals, grads))), d_input.astype(jnp.bfloat16))
    totals_b, d_rolled = lax.scan(step_shifted, zeros, (blocks(rolled), blocks(rolled_cot), label_blocks))
    d_middle = jnp.roll(grid_of(d_rolled), (SZ, SLAT, SLON), axis=(1, 2, 3))

    def step_regular(totals, items):
        block_in, block_cot = items
        cache = attend_forward(block_in, None, gain_a, qkv_a, out_a, bias_a)[1]
        d_input, grads = attend_backward(cache, block_cot, gain_a, qkv_a, out_a)
        return (tuple((total + grad for total, grad in zip(totals, grads))), d_input.astype(jnp.bfloat16))
    totals_a, d_blocks = lax.scan(step_regular, zeros, (blocks(tokens), blocks(d_middle)))
    d_tokens = grid_of(d_blocks)
    return (d_tokens, totals_a[0], totals_a[1], totals_a[2], totals_a[3], totals_b[0], totals_b[1], totals_b[2], totals_b[3])
```

```python
import functools

import jax
import jax.numpy as jnp
import numpy as np
from jax import lax
from jax.experimental import pallas as pl
from jax.experimental.pallas import tpu as pltpu
from jax.sharding import PartitionSpec as P

MESH = pl.DeviceIdType.MESH
C = 192
HEADS = 6
HEAD = 32
WT = 144
LEVELS = 8
WINDOWS = 4
TOK = WT * WINDOWS
FACTOR = HEAD ** (-0.5)
F32 = jnp.float32
BF16 = jnp.bfloat16
PIECE = 144
SPOTS = 16
HALF = PIECE * SPOTS
VMEM_LIMIT = 48 * 1024 * 1024


def nt(left, right):
    return lax.dot_general(left, right, (((1,), (1,)), ((), ())), preferred_element_type=F32)


def tn(left, right):
    return lax.dot_general(left, right, (((0,), (0,)), ((), ())), preferred_element_type=F32)


def nn(left, right):
    return lax.dot_general(left, right, (((1,), (0,)), ((), ())), preferred_element_type=F32)


def routes():
    slot_of_token = np.zeros(TOK, np.int32)
    place_of_slot = np.zeros(TOK, np.int32)
    for z in range(8):
        for i in range(6):
            for j in range(12):
                token = z * 72 + i * 12 + j
                zr, ir, jr = (z - 1) % 8, (i + 3) % 6, (j + 6) % 12
                quarter = 2 * (ir >= 3) + (jr >= 6)
                slot = quarter * WT + zr * 18 + (ir % 3) * 6 + jr % 6
                slot_of_token[token] = slot
                place_of_slot[slot] = zr * 72 + ir * 12 + jr
    return np.stack(
        [slot_of_token, place_of_slot, np.argsort(place_of_slot), np.argsort(slot_of_token)]
    ).astype(np.int32)


def head_mask(h, dtype):
    lane = lax.broadcasted_iota(jnp.int32, (1, C), 1)
    return jnp.where((lane >= h * HEAD) & (lane < (h + 1) * HEAD), 1.0, 0.0).astype(dtype)


def window_forward(w, x, gain, wq, wk, wv, bias, extra, save):
    unit_s, inv_s, normed_s, q_s, k_s, v_s, p_s, att_s = save
    rows = pl.ds(pl.multiple_of(w * WT, WT), WT)
    xf = x.astype(F32)
    center = xf - jnp.mean(xf, axis=-1, keepdims=True)
    inv = lax.rsqrt(jnp.mean(center * center, axis=-1, keepdims=True) + 1e-05)
    unit = center * inv
    normed = (unit * gain).astype(BF16)
    unit_s[rows, :] = unit
    inv_s[rows, :] = inv
    normed_s[rows, :] = normed
    q = nn(normed, wq).astype(BF16)
    k = nn(normed, wk).astype(BF16)
    v = nn(normed, wv).astype(BF16)
    q_s[rows, :] = q
    k_s[rows, :] = k
    v_s[rows, :] = v
    att = jnp.zeros((WT, C), F32)
    for h in range(HEADS):
        m = head_mask(h, BF16)
        s = nt(q * m, k) * FACTOR + bias[h]
        if extra is not None:
            s = s + extra
        e = jnp.exp(s - jnp.max(s, axis=-1, keepdims=True))
        p = (e * (1.0 / jnp.sum(e, axis=-1, keepdims=True))).astype(BF16)
        p_s[w * HEADS + h] = p
        att = att + nn(p, v * m)
    att = att.astype(BF16)
    att_s[rows, :] = att
    return xf, att


def window_backward(w, g, gain, wq, wk, wv, wo, save, grads):
    unit_s, inv_s, normed_s, q_s, k_s, v_s, p_s, att_s = save
    gq_s, gk_s, gv_s, go_s, gb_s, gg_s = grads
    rows = pl.ds(pl.multiple_of(w * WT, WT), WT)
    go_s[...] += tn(att_s[rows, :], g)
    da = nt(g, wo).astype(BF16)
    q = q_s[rows, :]
    k = k_s[rows, :]
    v = v_s[rows, :]
    dq = jnp.zeros((WT, C), F32)
    dk = jnp.zeros((WT, C), F32)
    dv = jnp.zeros((WT, C), F32)
    for h in range(HEADS):
        m = head_mask(h, BF16)
        dah = da * m
        p = p_s[w * HEADS + h]
        dp = nt(dah, v)
        pf = p.astype(F32)
        t = pf * dp
        ds = t - pf * jnp.sum(t, axis=-1, keepdims=True)
        gb_s[h] += ds
        dsb = (ds * FACTOR).astype(BF16)
        dv = dv + tn(p, dah)
        dq = dq + nn(dsb, k * m)
        dk = dk + tn(dsb, q * m)
    dq = dq.astype(BF16)
    dk = dk.astype(BF16)
    dv = dv.astype(BF16)
    normed = normed_s[rows, :]
    gq_s[...] += tn(normed, dq)
    gk_s[...] += tn(normed, dk)
    gv_s[...] += tn(normed, dv)
    dn = nt(dq, wq) + nt(dk, wk) + nt(dv, wv)
    unit = unit_s[rows, :]
    gg_s[...] += jnp.sum(dn * unit, axis=0, keepdims=True)
    dh = dn * gain
    d_in = g.astype(F32) + inv_s[rows, :] * (
        dh
        - jnp.mean(dh, axis=-1, keepdims=True)
        - unit * jnp.mean(dh * unit, axis=-1, keepdims=True)
    )
    return d_in.astype(BF16)


def pack(out, base, grads):
    gq_s, gk_s, gv_s, go_s, gb_s, gg_s = grads
    at = base
    for ref in (gq_s, gk_s, gv_s, go_s):
        out[at : at + C, :] = ref[:, :128].astype(BF16)
        at += C
    for one, two in ((gq_s, gk_s), (gv_s, go_s)):
        out[at : at + C, :] = jnp.concatenate([one[:, 128:], two[:, 128:]], axis=1).astype(BF16)
        at += C
    for h in range(HEADS):
        out[at : at + WT, :] = gb_s[h, :, :128].astype(BF16)
        at += WT
    tails = [gb_s[h, :, 128:] for h in range(HEADS)] + [jnp.zeros((WT, 32), F32)]
    out[at : at + WT, :] = jnp.concatenate(tails, axis=1).astype(BF16)
    at += WT
    gg = gg_s[...]
    second = jnp.concatenate([gg[:, 128:], jnp.zeros((1, 64), F32)], axis=1)
    tile = jnp.concatenate([gg[:, :128], second, jnp.zeros((14, 128), F32)], axis=0)
    out[at : at + 16, :] = tile.astype(BF16)
    at += 16
    out[at : base + HALF, :] = jnp.zeros((base + HALF - at, 128), BF16)


def layer_kernel(
    lats,
    lons,
    tok_ref,
    cot_ref,
    gain_a,
    qkv_a,
    out_a,
    bias_a,
    gain_b,
    qkv_b,
    out_b,
    bias_b,
    route_ref,
    dtok_ref,
    grads_ref,
    save_a,
    save_b,
    grad_a,
    grad_b,
    mat_s,
    extra_s,
    mid_s,
    send_s,
    recv_s,
    x_b,
    g_b,
    send_sem,
    recv_sem,
):
    lat = lax.axis_index("lat")
    lon = lax.axis_index("lon")

    def shifted(dlat, dlon):
        return {"lat": lax.rem(lat + dlat + lats, lats), "lon": lax.rem(lon + dlon + lons, lons)}

    before = [shifted(0, -1), shifted(-1, 0), shifted(-1, -1)]
    after = [shifted(0, 1), shifted(1, 0), shifted(1, 1)]

    def quarters(leg, targets):
        copies = []
        for n, target in enumerate(targets):
            rows = pl.ds((n + 1) * WT, WT)
            copies.append(
                pltpu.make_async_remote_copy(
                    src_ref=send_s.at[leg, rows],
                    dst_ref=recv_s.at[leg, rows],
                    send_sem=send_sem.at[leg * 3 + n],
                    recv_sem=recv_sem.at[leg * 3 + n],
                    device_id=target,
                    device_id_type=MESH,
                )
            )
        return copies

    barrier = pltpu.get_barrier_semaphore()
    for other in before + after:
        pl.semaphore_signal(barrier, inc=1, device_id=other, device_id_type=MESH)

    row_iota = lax.broadcasted_iota(jnp.int32, (TOK, TOK), 0)
    for n in range(4):
        mat_s[n] = jnp.where(row_iota == route_ref[n : n + 1, :], 1.0, 0.0).astype(BF16)

    send_s[0] = nn(mat_s[0], cot_ref[...]).astype(BF16)
    pl.semaphore_wait(barrier, 6)
    legs = [quarters(0, before), quarters(1, before), quarters(2, after)]
    for copy in legs[0]:
        copy.start()
    recv_s[0, 0:WT] = send_s[0, 0:WT]

    for grads in (grad_a, grad_b):
        for ref in grads:
            ref[...] = jnp.zeros_like(ref)

    def label(shape, axis, level):
        at = lax.broadcasted_iota(jnp.int32, shape, axis)
        upper = jnp.where(at >= 72, 1, 0)
        inside = at - 72 * upper
        late = jnp.where(inside >= 36, 1, 0) * jnp.where(lat == lats - 1, 1, 0)
        return late + 2 * upper if level else late

    for n in range(2):
        same = label((WT, WT), 0, n) == label((WT, WT), 1, n)
        extra_s[n] = jnp.where(same, 0.0, -1e30)

    ga = gain_a[...]
    wo = out_a[...]
    wqa, wka, wva = (qkv_a[:, n * C : (n + 1) * C] for n in range(3))

    def regular(w, carry):
        rows = pl.ds(pl.multiple_of(w * WT, WT), WT)
        xf, att = window_forward(w, tok_ref[rows, :], ga, wqa, wka, wva, bias_a, None, save_a)
        mid_s[rows, :] = (xf + nn(att, wo)).astype(BF16)
        return carry

    lax.fori_loop(0, WINDOWS, regular, 0)

    send_s[1] = nn(mat_s[0], mid_s[...]).astype(BF16)
    for copy in legs[1]:
        copy.start()
    recv_s[1, 0:WT] = send_s[1, 0:WT]
    for copy in legs[0]:
        copy.wait()
    g_b[...] = nn(mat_s[1], recv_s[0]).astype(BF16)
    for copy in legs[1]:
        copy.wait()
    x_b[...] = nn(mat_s[1], recv_s[1]).astype(BF16)

    gb = gain_b[...]
    wob = out_b[...]
    wqb, wkb, wvb = (qkv_b[:, n * C : (n + 1) * C] for n in range(3))

    def shifted_block(w, carry):
        rows = pl.ds(pl.multiple_of(w * WT, WT), WT)
        extra = extra_s[lax.div(w, WINDOWS - 1)]
        window_forward(w, x_b[rows, :], gb, wqb, wkb, wvb, bias_b, extra, save_b)
        x_b[rows, :] = window_backward(w, g_b[rows, :], gb, wqb, wkb, wvb, wob, save_b, grad_b)
        return carry

    lax.fori_loop(0, WINDOWS, shifted_block, 0)

    send_s[2] = nn(mat_s[2], x_b[...]).astype(BF16)
    for copy in legs[2]:
        copy.start()
    recv_s[2, 0:WT] = send_s[2, 0:WT]
    pack(grads_ref, HALF, grad_b)
    for copy in legs[2]:
        copy.wait()
    mid_s[...] = nn(mat_s[3], recv_s[2]).astype(BF16)

    def regular_back(w, carry):
        rows = pl.ds(pl.multiple_of(w * WT, WT), WT)
        dtok_ref[rows, :] = window_backward(w, mid_s[rows, :], ga, wqa, wka, wva, wo, save_a, grad_a)
        return carry

    lax.fori_loop(0, WINDOWS, regular_back, 0)
    pack(grads_ref, 0, grad_a)


def sum_kernel(
    in_ref,
    out_ref,
    core_s,
    part_s,
    plane_s,
    line_s,
    core_send,
    core_recv,
    plane_send,
    plane_recv,
    line_send,
    line_recv,
    back_send,
    back_recv,
    last_send,
    last_recv,
):
    rep = lax.axis_index("rep")
    lat = lax.axis_index("lat")
    lon = lax.axis_index("lon")
    x_hi, core = rep // 2, rep % 2
    x_lo, y = lat // 4, lat % 4
    me = (x_hi * 2 + x_lo) * 4 + y
    partner = {"rep": x_hi * 2 + (1 - core)}

    def spot(index):
        x, yy = index // 4, index % 4
        return {"rep": (x // 2) * 2 + core, "lat": (x % 2) * 4 + yy}

    barrier = pltpu.get_barrier_semaphore()
    pl.semaphore_signal(barrier, inc=1, device_id=partner, device_id_type=MESH)

    def greet_plane(k, carry):
        pl.semaphore_signal(
            barrier, inc=1, device_id=spot(lax.rem(me + k, SPOTS)), device_id_type=MESH
        )
        return carry

    def greet_line(k, carry):
        pl.semaphore_signal(
            barrier, inc=1, device_id={"lon": lax.rem(lon + k, 8)}, device_id_type=MESH
        )
        return carry

    lax.fori_loop(1, SPOTS, greet_plane, 0)
    lax.fori_loop(1, 8, greet_line, 0)
    pl.semaphore_wait(barrier, 1 + SPOTS - 1 + 7)

    def core_copy(k):
        j = lax.rem(me + k, SPOTS)
        return pltpu.make_async_remote_copy(
            src_ref=in_ref.at[1 - core, j],
            dst_ref=core_s.at[k],
            send_sem=core_send.at[k],
            recv_sem=core_recv.at[k],
            device_id=partner,
            device_id_type=MESH,
        )

    def plane_copy(k):
        return pltpu.make_async_remote_copy(
            src_ref=part_s.at[k],
            dst_ref=plane_s.at[k],
            send_sem=plane_send.at[k],
            recv_sem=plane_recv.at[k],
            device_id=spot(lax.rem(me + k, SPOTS)),
            device_id_type=MESH,
        )

    def start_core(k, carry):
        core_copy(k).start()
        return carry

    lax.fori_loop(1, SPOTS, start_core, 0)
    core_copy(0).start()

    def merge_core(k):
        core_copy(k).wait()
        j = lax.rem(me + k, SPOTS)
        return in_ref[core, j].astype(F32) + core_s[k].astype(F32)

    def start_plane(k, carry):
        part_s[k] = merge_core(k).astype(BF16)
        plane_copy(k).start()
        return carry

    lax.fori_loop(1, SPOTS, start_plane, 0)

    def add_plane(k, total):
        plane_copy(k).wait()
        return total + plane_s[k].astype(F32)

    total = lax.fori_loop(1, SPOTS, add_plane, merge_core(0))
    line_s[lon] = total.astype(BF16)

    def line_copy(k):
        return pltpu.make_async_remote_copy(
            src_ref=line_s.at[lon],
            dst_ref=line_s.at[lon],
            send_sem=line_send.at[k],
            recv_sem=line_recv.at[k],
            device_id={"lon": lax.rem(lon + k, 8)},
            device_id_type=MESH,
        )

    def start_line(k, carry):
        line_copy(k).start()
        return carry

    def wait_line(k, carry):
        line_copy(k).wait_send()
        pltpu.make_async_remote_copy(
            src_ref=line_s.at[lax.rem(lon + 8 - k, 8)],
            dst_ref=line_s.at[lax.rem(lon + 8 - k, 8)],
            send_sem=line_send.at[k],
            recv_sem=line_recv.at[k],
            device_id={"lon": lax.rem(lon + k, 8)},
            device_id_type=MESH,
        ).wait_recv()
        return carry

    lax.fori_loop(1, 8, start_line, 0)
    lax.fori_loop(1, 8, wait_line, 0)
    total = line_s[0].astype(F32)
    for n in range(1, 8):
        total = total + line_s[n].astype(F32)
    out_ref[core, me] = total.astype(BF16)

    def back_copy(k, j):
        return pltpu.make_async_remote_copy(
            src_ref=out_ref.at[core, j],
            dst_ref=out_ref.at[core, j],
            send_sem=back_send.at[k],
            recv_sem=back_recv.at[k],
            device_id=spot(lax.rem(me + k, SPOTS)),
            device_id_type=MESH,
        )

    def last_copy(k, half):
        j = lax.rem(me + SPOTS - k, SPOTS)
        return pltpu.make_async_remote_copy(
            src_ref=out_ref.at[half, j],
            dst_ref=out_ref.at[half, j],
            send_sem=last_send.at[k],
            recv_sem=last_recv.at[k],
            device_id=partner,
            device_id_type=MESH,
        )

    def start_back(k, carry):
        back_copy(k, me).start()
        return carry

    def forward(k, carry):
        back_copy(k, me).wait_send()
        back_copy(k, lax.rem(me + SPOTS - k, SPOTS)).wait_recv()
        last_copy(k, core).start()
        return carry

    def finish(k, carry):
        last_copy(k, core).wait_send()
        last_copy(k, 1 - core).wait_recv()
        return carry

    lax.fori_loop(1, SPOTS, start_back, 0)
    last_copy(0, core).start()
    lax.fori_loop(1, SPOTS, forward, 0)
    lax.fori_loop(0, SPOTS, finish, 0)


def unpack_kernel(in_ref, *outs):
    for block in range(2):
        gain, qkv, out, bias = outs[4 * block : 4 * block + 4]
        at = block * HALF

        def rows(count):
            nonlocal at
            at += count
            return in_ref[at - count : at, :].astype(F32)

        gq, gk, gv, go = (rows(C) for _ in range(4))
        one, two = rows(C), rows(C)
        qkv[...] = jnp.concatenate(
            [gq, one[:, :64], gk, one[:, 64:], gv, two[:, :64]], axis=1
        )
        out[...] = jnp.concatenate([go, two[:, 64:]], axis=1)
        main = [rows(WT) for _ in range(HEADS)]
        tails = rows(WT)
        for h in range(HEADS):
            bias[h] = jnp.concatenate([main[h], tails[:, 16 * h : 16 * h + 16]], axis=1)
        last = rows(16)
        gain[...] = jnp.concatenate([last[0:1, :], last[1:2, :64]], axis=1)


def saves():
    return (
        pltpu.VMEM((TOK, C), F32),
        pltpu.VMEM((TOK, 1), F32),
        pltpu.VMEM((TOK, C), BF16),
        pltpu.VMEM((TOK, C), BF16),
        pltpu.VMEM((TOK, C), BF16),
        pltpu.VMEM((TOK, C), BF16),
        pltpu.VMEM((WINDOWS * HEADS, WT, WT), BF16),
        pltpu.VMEM((TOK, C), BF16),
    )


def totals():
    return (
        pltpu.VMEM((C, C), F32),
        pltpu.VMEM((C, C), F32),
        pltpu.VMEM((C, C), F32),
        pltpu.VMEM((C, C), F32),
        pltpu.VMEM((HEADS, WT, WT), F32),
        pltpu.VMEM((1, C), F32),
    )


def run_layer(lats, lons, *args):
    return pl.pallas_call(
        functools.partial(layer_kernel, lats, lons),
        out_shape=(
            jax.ShapeDtypeStruct((TOK, C), BF16),
            jax.ShapeDtypeStruct((2 * HALF, 128), BF16),
        ),
        in_specs=[pl.BlockSpec(memory_space=pltpu.VMEM)] * 11,
        out_specs=(pl.BlockSpec(memory_space=pltpu.VMEM),) * 2,
        scratch_shapes=[
            saves(),
            saves(),
            totals(),
            totals(),
            pltpu.VMEM((4, TOK, TOK), BF16),
            pltpu.VMEM((2, WT, WT), F32),
            pltpu.VMEM((TOK, C), BF16),
            pltpu.VMEM((3, TOK, C), BF16),
            pltpu.VMEM((3, TOK, C), BF16),
            pltpu.VMEM((TOK, C), BF16),
            pltpu.VMEM((TOK, C), BF16),
            pltpu.SemaphoreType.DMA((9,)),
            pltpu.SemaphoreType.DMA((9,)),
        ],
        compiler_params=pltpu.CompilerParams(
            collective_id=0, has_side_effects=True, vmem_limit_bytes=VMEM_LIMIT
        ),
        name="layer",
    )(*args)


def run_sum(value):
    piece = (PIECE, 128)
    return pl.pallas_call(
        sum_kernel,
        out_shape=jax.ShapeDtypeStruct((2, SPOTS) + piece, BF16),
        in_specs=[pl.BlockSpec(memory_space=pltpu.VMEM)],
        out_specs=pl.BlockSpec(memory_space=pltpu.VMEM),
        scratch_shapes=[
            pltpu.VMEM((SPOTS,) + piece, BF16),
            pltpu.VMEM((SPOTS,) + piece, BF16),
            pltpu.VMEM((SPOTS,) + piece, BF16),
            pltpu.VMEM((8,) + piece, BF16),
        ]
        + [pltpu.SemaphoreType.DMA((SPOTS,))] * 4
        + [pltpu.SemaphoreType.DMA((8,))] * 2
        + [pltpu.SemaphoreType.DMA((SPOTS,))] * 4,
        compiler_params=pltpu.CompilerParams(
            collective_id=1, has_side_effects=True, vmem_limit_bytes=VMEM_LIMIT
        ),
        name="gradient_sum",
    )(value)


def run_unpack(value):
    block = (
        jax.ShapeDtypeStruct((1, C), F32),
        jax.ShapeDtypeStruct((C, 3 * C), F32),
        jax.ShapeDtypeStruct((C, C), F32),
        jax.ShapeDtypeStruct((HEADS, WT, WT), F32),
    )
    return pl.pallas_call(
        unpack_kernel,
        out_shape=block + block,
        in_specs=[pl.BlockSpec(memory_space=pltpu.VMEM)],
        out_specs=(pl.BlockSpec(memory_space=pltpu.VMEM),) * 8,
        compiler_params=pltpu.CompilerParams(vmem_limit_bytes=VMEM_LIMIT),
        name="unpack",
    )(value)


def solution(mesh):
    lats, lons = mesh.shape["lat"], mesh.shape["lon"]
    route = routes()

    def local(tokens, cotangent, gain_a, qkv_a, out_a, bias_a, gain_b, qkv_b, out_b, bias_b):
        d_tokens, packed = run_layer(
            lats,
            lons,
            tokens.reshape(TOK, C),
            cotangent.reshape(TOK, C),
            gain_a.reshape(1, C),
            qkv_a,
            out_a,
            bias_a,
            gain_b.reshape(1, C),
            qkv_b,
            out_b,
            bias_b,
            jnp.asarray(route),
        )
        summed = run_sum(packed.reshape(2, SPOTS, PIECE, 128))
        res = run_unpack(summed.reshape(2 * HALF, 128))
        ga, qa, oa, ba, gb, qb, ob, bb = res
        return (
            d_tokens.reshape(tokens.shape),
            ga.reshape(C),
            qa,
            oa,
            ba,
            gb.reshape(C),
            qb,
            ob,
            bb,
        )

    grid = P("rep", None, "lat", "lon", None)
    return jax.shard_map(
        local,
        mesh=mesh,
        in_specs=(grid, grid) + (P(),) * 8,
        out_specs=(grid,) + (P(),) * 8,
        check_vma=False,
    )
```

```python
import functools

import jax
import jax.numpy as jnp
import numpy as np
from jax import lax
from jax.experimental import pallas as pl
from jax.experimental.pallas import tpu as pltpu
from jax.sharding import PartitionSpec as P

MESH = pl.DeviceIdType.MESH
C = 192
HEADS = 6
HEAD = 32
WT = 144
LEVELS = 8
WINDOWS = 4
TOK = WT * WINDOWS
FACTOR = HEAD ** (-0.5)
F32 = jnp.float32
BF16 = jnp.bfloat16
PIECE = 80
SPOTS = 16
HALF = PIECE * SPOTS
STEP = 144
SLOT = 48
VMEM_LIMIT = 56 * 1024 * 1024


def nt(left, right):
    return lax.dot_general(left, right, (((1,), (1,)), ((), ())), preferred_element_type=F32)


def tn(left, right):
    return lax.dot_general(left, right, (((0,), (0,)), ((), ())), preferred_element_type=F32)


def nn(left, right):
    return lax.dot_general(left, right, (((1,), (0,)), ((), ())), preferred_element_type=F32)


def routes():
    out = np.full((16, TOK), -1, np.int32)
    for z in range(LEVELS):
        for i in range(6):
            for j in range(12):
                stored = (i * 12 + j) * LEVELS + z
                token = z * 72 + i * 12 + j
                out[0, stored] = token
                out[1, token] = stored
                zr, ir, jr = (z - 1) % LEVELS, (i + 3) % 6, (j + 6) % 12
                quarter = 2 * (ir >= 3) + (jr >= 6)
                window, level = zr // 2, zr % 2
                inside = level * 18 + (ir % 3) * 6 + jr % 6
                slot = quarter * SLOT + inside
                place = level * 72 + ir * 12 + jr
                column = i * 12 + j
                out[2, stored] = (quarter * WINDOWS + window) * SLOT + inside
                out[3 + level, column] = slot
                out[5, slot] = place
                out[6, place] = slot
                out[7 + level, slot] = column
    return out


def head_mask(h, dtype):
    lane = lax.broadcasted_iota(jnp.int32, (1, C), 1)
    return jnp.where((lane >= h * HEAD) & (lane < (h + 1) * HEAD), 1.0, 0.0).astype(dtype)


def spread(value):
    return jnp.concatenate([value * head_mask(h, BF16) for h in range(HEADS)], axis=0)


def gather_heads(stacked):
    total = stacked[:WT]
    lane = lax.broadcasted_iota(jnp.int32, (1, C), 1)
    for h in range(1, HEADS):
        total = jnp.where(lane >= h * HEAD, stacked[h * WT : (h + 1) * WT], total)
    return total


def window_forward(w, x, gain, wq, wk, wv, bias, extra, save):
    unit_s, inv_s, normed_s, q_s, k_s, v_s, p_s, att_s, s_s, d_s = save
    rows = pl.ds(w * WT, WT)
    xf = x.astype(F32)
    center = xf - jnp.mean(xf, axis=-1, keepdims=True)
    inv = lax.rsqrt(jnp.mean(center * center, axis=-1, keepdims=True) + 1e-05)
    unit = center * inv
    normed = (unit * gain).astype(BF16)
    unit_s[rows, :] = unit
    inv_s[rows, :] = inv
    normed_s[rows, :] = normed
    q = (nn(normed, wq) * FACTOR).astype(BF16)
    k = nn(normed, wk).astype(BF16)
    v = nn(normed, wv).astype(BF16)
    q_s[rows, :] = q
    k_s[rows, :] = k
    v_s[rows, :] = v
    s_s[w] = nt(spread(q), k)
    for at in range(0, HEADS * WT, STEP):
        h, first = at // WT, at % WT
        s = s_s[w, at : at + STEP, :] + bias[h, first : first + STEP, :]
        if extra is not None:
            s = s + extra[first : first + STEP]
        e = jnp.exp(s - jnp.max(s, axis=-1, keepdims=True))
        p = (e * (1.0 / jnp.sum(e, axis=-1, keepdims=True))).astype(BF16)
        p_s[w, at : at + STEP, :] = p
    att = gather_heads(nn(p_s[w], v)).astype(BF16)
    att_s[rows, :] = att
    return xf, att


def window_backward(w, first_one, g, gain, wq, wk, wv, wo, save, grads):
    unit_s, inv_s, normed_s, q_s, k_s, v_s, p_s, att_s, s_s, d_s = save
    gq_s, gk_s, gv_s, go_s, gb_s, gg_s = grads
    rows = pl.ds(w * WT, WT)

    def add(ref, index, value):
        ref[index] = value if first_one else ref[index] + value

    add(go_s, ..., tn(att_s[rows, :], g))
    da = spread(nt(g, wo).astype(BF16))
    s_s[w] = nt(da, v_s[rows, :])
    dv = tn(p_s[w], da).astype(BF16)
    for at in range(0, HEADS * WT, STEP):
        h, first = at // WT, at % WT
        pf = p_s[w, at : at + STEP, :].astype(F32)
        t = pf * s_s[w, at : at + STEP, :]
        ds = t - pf * jnp.sum(t, axis=-1, keepdims=True)
        add(gb_s, (h, slice(first, first + STEP), slice(None)), ds)
        d_s[w, at : at + STEP, :] = ds.astype(BF16)
    ds = d_s[w]
    dk = tn(ds, spread(q_s[rows, :])).astype(BF16)
    dq = (gather_heads(nn(ds, k_s[rows, :])) * FACTOR).astype(BF16)
    normed = normed_s[rows, :]
    add(gq_s, ..., tn(normed, dq))
    add(gk_s, ..., tn(normed, dk))
    add(gv_s, ..., tn(normed, dv))
    dn = nt(dq, wq) + nt(dk, wk) + nt(dv, wv)
    unit = unit_s[rows, :]
    add(gg_s, ..., jnp.sum(dn * unit, axis=0, keepdims=True))
    dh = dn * gain
    d_in = g.astype(F32) + inv_s[rows, :] * (
        dh
        - jnp.mean(dh, axis=-1, keepdims=True)
        - unit * jnp.mean(dh * unit, axis=-1, keepdims=True)
    )
    return d_in.astype(BF16)


def pack(out, grads):
    gq_s, gk_s, gv_s, go_s, gb_s, gg_s = grads
    at = 0

    def put(value):
        nonlocal at
        value = value.astype(BF16)
        done = 0
        while done < value.shape[0]:
            piece, first = (at + done) // PIECE, (at + done) % PIECE
            count = min(PIECE - first, value.shape[0] - done)
            out[piece // SPOTS, piece % SPOTS, first : first + count, :] = value[done : done + count]
            done += count
        at += value.shape[0]

    for ref in (gq_s, gk_s, gv_s, go_s):
        put(ref[:, :128])
    for one, two in ((gq_s, gk_s), (gv_s, go_s)):
        put(jnp.concatenate([one[:, 128:], two[:, 128:]], axis=1))
    for h in range(HEADS):
        put(gb_s[h, :, :128])
    tails = [gb_s[h, :, 128:] for h in range(HEADS)] + [jnp.zeros((WT, 32), F32)]
    put(jnp.concatenate(tails, axis=1))
    gg = gg_s[...]
    second = jnp.concatenate([gg[:, 128:], jnp.zeros((1, 64), F32)], axis=1)
    put(jnp.concatenate([gg[:, :128], second, jnp.zeros((14, 128), F32)], axis=0))
    put(jnp.zeros((2 * HALF - at, 128), F32))


class Sum:
    def __init__(self, lon_count, refs):
        self.in_ref, self.out_ref, self.core_s, self.part_s, self.plane_s, self.line_s = refs[:6]
        self.sems = refs[6:]
        rep, lat = lax.axis_index("rep"), lax.axis_index("lat")
        self.lon = lax.axis_index("lon")
        self.lons = lon_count
        self.core = rep % 2
        x_hi, x_lo, y = rep // 2, lat // 4, lat % 4
        self.me = (x_hi * 2 + x_lo) * 4 + y
        self.partner = {"rep": x_hi * 2 + (1 - self.core)}

    def spot(self, k):
        index = lax.rem(self.me + k, SPOTS)
        x, y = index // 4, index % 4
        return {"rep": (x // 2) * 2 + self.core, "lat": (x % 2) * 4 + y}

    def neighbour(self, k):
        return {"lon": lax.rem(self.lon + k, self.lons)}

    def greet(self, barrier):
        pl.semaphore_signal(barrier, inc=1, device_id=self.partner, device_id_type=MESH)

        def greet_plane(k, carry):
            pl.semaphore_signal(barrier, inc=1, device_id=self.spot(k), device_id_type=MESH)
            return carry

        def greet_line(k, carry):
            pl.semaphore_signal(barrier, inc=1, device_id=self.neighbour(k), device_id_type=MESH)
            return carry

        lax.fori_loop(1, SPOTS, greet_plane, 0)
        lax.fori_loop(1, self.lons, greet_line, 0)
        return SPOTS + self.lons - 1

    def copy(self, pair, k, source, target, device):
        return pltpu.make_async_remote_copy(
            src_ref=source,
            dst_ref=target,
            send_sem=self.sems[2 * pair].at[k],
            recv_sem=self.sems[2 * pair + 1].at[k],
            device_id=device,
            device_id_type=MESH,
        )

    def core_copy(self, k):
        j = lax.rem(self.me + k, SPOTS)
        return self.copy(0, k, self.in_ref.at[1 - self.core, j], self.core_s.at[k], self.partner)

    def plane_copy(self, k):
        return self.copy(1, k, self.part_s.at[k], self.plane_s.at[k], self.spot(k))

    def line_copy(self, k, slot):
        return self.copy(2, k, self.line_s.at[slot], self.line_s.at[slot], self.neighbour(k))

    def back_copy(self, k, j):
        ref = self.out_ref.at[self.core, j]
        return self.copy(3, k, ref, ref, self.spot(k))

    def last_copy(self, k, half):
        ref = self.out_ref.at[half, lax.rem(self.me + SPOTS - k, SPOTS)]
        return self.copy(4, k, ref, ref, self.partner)

    def merge(self, k):
        self.core_copy(k).wait()
        j = lax.rem(self.me + k, SPOTS)
        return self.in_ref[self.core, j].astype(F32) + self.core_s[k].astype(F32)

    def loop(self, first, last, step):
        def body(k, carry):
            step(k)
            return carry

        lax.fori_loop(first, last, body, 0)

    def start_core(self):
        self.loop(1, SPOTS, lambda k: self.core_copy(k).start())
        self.core_copy(0).start()

    def start_plane(self):
        def step(k):
            self.part_s[k] = self.merge(k).astype(BF16)
            self.plane_copy(k).start()

        self.loop(1, SPOTS, step)

    def start_line(self):
        def add(k, total):
            self.plane_copy(k).wait()
            return total + self.plane_s[k].astype(F32)

        total = lax.fori_loop(1, SPOTS, add, self.merge(0))
        self.line_s[self.lon] = total.astype(BF16)
        self.loop(1, self.lons, lambda k: self.line_copy(k, self.lon).start())

    def start_back(self):
        def wait(k):
            self.line_copy(k, self.lon).wait_send()
            self.line_copy(k, lax.rem(self.lon + self.lons - k, self.lons)).wait_recv()

        self.loop(1, self.lons, wait)
        total = self.line_s[0].astype(F32)
        for n in range(1, self.lons):
            total = total + self.line_s[n].astype(F32)
        self.out_ref[self.core, self.me] = total.astype(BF16)
        self.loop(1, SPOTS, lambda k: self.back_copy(k, self.me).start())
        self.last_copy(0, self.core).start()

    def start_last(self):
        def step(k):
            self.back_copy(k, self.me).wait_send()
            self.back_copy(k, lax.rem(self.me + SPOTS - k, SPOTS)).wait_recv()
            self.last_copy(k, self.core).start()

        self.loop(1, SPOTS, step)

    def finish(self):
        def step(k):
            self.last_copy(k, self.core).wait_send()
            self.last_copy(k, 1 - self.core).wait_recv()

        self.loop(0, SPOTS, step)


def layer_kernel(
    lats,
    lons,
    make_sum,
    tok_ref,
    cot_ref,
    gain_a,
    qkv_a,
    out_a,
    bias_a,
    gain_b,
    qkv_b,
    out_b,
    bias_b,
    route_ref,
    dtok_ref,
    sum_ref,
    save_a,
    save_b,
    grad_a,
    grad_b,
    order_s,
    slots_s,
    ahead_s,
    place_s,
    back_s,
    home_s,
    extra_s,
    x_a,
    mid_s,
    dmid_s,
    send_s,
    recv_s,
    send_sem,
    recv_sem,
    packed_s,
    parts_a,
    parts_b,
):
    lat = lax.axis_index("lat")
    lon = lax.axis_index("lon")

    def shifted(dlat, dlon):
        return {"lat": lax.rem(lat + dlat + lats, lats), "lon": lax.rem(lon + dlon + lons, lons)}

    before = [shifted(0, -1), shifted(-1, 0), shifted(-1, -1)]
    after = [shifted(0, 1), shifted(1, 0), shifted(1, 1)]

    def quarters(leg, window):
        copies = []
        for n, target in enumerate(after if leg == 2 else before):
            at = (leg, n + 1) if window is None else (leg, n + 1, window)
            sem = n if window is None else 3 + (leg - 1) * 12 + window * 3 + n
            copies.append(
                pltpu.make_async_remote_copy(
                    src_ref=send_s.at[at],
                    dst_ref=recv_s.at[at],
                    send_sem=send_sem.at[sem],
                    recv_sem=recv_sem.at[sem],
                    device_id=target,
                    device_id_type=MESH,
                )
            )
        return copies

    def post(leg, window, value):
        value = value.astype(BF16)
        recv_s[leg, 0, window] = value[:SLOT]
        for n in range(1, 4):
            send_s[leg, n, window] = value[n * SLOT : (n + 1) * SLOT]
        copies = quarters(leg, window)
        for copy in copies:
            copy.start()
        return copies

    def arrived(leg, window):
        return recv_s[leg, :, window].reshape(4 * SLOT, C)

    sum_a = make_sum(lons, (packed_s.at[0], sum_ref.at[0]) + parts_a)
    sum_b = make_sum(lons, (packed_s.at[1], sum_ref.at[1]) + parts_b)

    barrier = pltpu.get_barrier_semaphore()
    for other in before + after:
        pl.semaphore_signal(barrier, inc=1, device_id=other, device_id_type=MESH)
    greeted = 6 + sum_a.greet(barrier)

    def one_hot(rows, row, columns):
        target = route_ref[row : row + 1, :columns]
        spot = lax.broadcasted_iota(jnp.int32, (rows, columns), 0)
        return jnp.where(spot == target, 1.0, 0.0).astype(BF16)

    x_a[...] = nn(one_hot(TOK, 0, TOK), tok_ref[...]).astype(BF16)
    order_s[...] = one_hot(TOK, 1, TOK)
    slots_s[...] = one_hot(16 * SLOT, 2, TOK)
    place_s[...] = one_hot(WT, 5, 4 * SLOT)
    back_s[...] = one_hot(4 * SLOT, 6, WT)
    for n in range(2):
        ahead_s[n] = one_hot(4 * SLOT, 3 + n, 72)
        home_s[n] = one_hot(72, 7 + n, 4 * SLOT)

    ga = gain_a[...]
    wo = out_a[...]
    wqa, wka, wva = (qkv_a[:, n * C : (n + 1) * C] for n in range(3))
    mids = [None] * WINDOWS
    backs = [None] * WINDOWS

    def send_mid(w):
        levels = (2 * w + 1, (2 * w + 2) % LEVELS)
        mids[w] = post(1, w, nn(ahead_s[0], mid_s[levels[0]]) + nn(ahead_s[1], mid_s[levels[1]]))

    for w in range(WINDOWS):
        xf, att = window_forward(w, x_a[w * WT : (w + 1) * WT, :], ga, wqa, wka, wva, bias_a, None, save_a)
        middle = xf + nn(att, wo)
        mid_s[2 * w] = middle[:72].astype(BF16)
        mid_s[2 * w + 1] = middle[72:].astype(BF16)
        if w == 0:
            cots = nn(slots_s[...], cot_ref[...]).astype(BF16)
            cots = cots.reshape(4, WINDOWS, SLOT, C)
            recv_s[0, 0] = cots[0]
            for n in range(1, 4):
                send_s[0, n] = cots[n]
            pl.semaphore_wait(barrier, greeted)
            cot_copies = quarters(0, None)
            for copy in cot_copies:
                copy.start()
        else:
            send_mid(w - 1)
    send_mid(WINDOWS - 1)

    def label(shape, axis, level):
        at = lax.broadcasted_iota(jnp.int32, shape, axis)
        upper = jnp.where(at >= 72, 1, 0)
        inside = at - 72 * upper
        late = jnp.where(inside >= 36, 1, 0) * jnp.where(lat == lats - 1, 1, 0)
        return late + 2 * upper if level else late

    for n in range(2):
        same = label((WT, WT), 0, n) == label((WT, WT), 1, n)
        extra_s[n] = jnp.where(same, 0.0, -1e30)

    gb = gain_b[...]
    wob = out_b[...]
    wqb, wkb, wvb = (qkv_b[:, n * C : (n + 1) * C] for n in range(3))

    for copy in cot_copies:
        copy.wait()
    for w in range(WINDOWS):
        for copy in mids[w]:
            copy.wait()
        x = nn(place_s[...], arrived(1, w)).astype(BF16)
        g = nn(place_s[...], arrived(0, w)).astype(BF16)
        window_forward(w, x, gb, wqb, wkb, wvb, bias_b, extra_s.at[w // (WINDOWS - 1)], save_b)
        d_in = window_backward(w, w == 0, g, gb, wqb, wkb, wvb, wob, save_b, grad_b)
        backs[w] = post(2, w, nn(back_s[...], d_in))

    pack(packed_s.at[1], grad_b)
    sum_b.start_core()

    def take_back(w):
        for copy in backs[w]:
            copy.wait()
        value = arrived(2, w)
        dmid_s[2 * w + 1] = nn(home_s[0], value)
        dmid_s[(2 * w + 2) % LEVELS] = nn(home_s[1], value)

    def regular_back(w, first_one):
        g = jnp.concatenate([dmid_s[2 * w], dmid_s[2 * w + 1]], axis=0).astype(BF16)
        x_a[w * WT : (w + 1) * WT, :] = window_backward(
            w, first_one, g, ga, wqa, wka, wva, wo, save_a, grad_a
        )

    take_back(0)
    take_back(1)
    regular_back(1, True)
    sum_b.start_plane()
    take_back(2)
    regular_back(2, False)
    take_back(3)
    regular_back(3, False)
    regular_back(0, False)
    pack(packed_s.at[0], grad_a)
    sum_a.start_core()
    dtok_ref[...] = nn(order_s[...], x_a[...]).astype(BF16)
    sum_a.start_plane()
    sum_b.start_line()
    sum_b.start_back()
    sum_a.start_line()
    sum_b.start_last()
    sum_a.start_back()
    sum_a.start_last()
    sum_b.finish()
    sum_a.finish()


def unpack_kernel(in_ref, dtok_ref, dtok_out, *outs):
    dtok_out[...] = dtok_ref[...]
    for block in range(2):
        gain, qkv, out, bias = outs[4 * block : 4 * block + 4]
        at = block * 2 * HALF

        def rows(count):
            nonlocal at
            at += count
            return in_ref[at - count : at, :].astype(F32)

        gq, gk, gv, go = (rows(C) for _ in range(4))
        one, two = rows(C), rows(C)
        qkv[...] = jnp.concatenate(
            [gq, one[:, :64], gk, one[:, 64:], gv, two[:, :64]], axis=1
        )
        out[...] = jnp.concatenate([go, two[:, 64:]], axis=1)
        main = [rows(WT) for _ in range(HEADS)]
        tails = rows(WT)
        for h in range(HEADS):
            bias[h] = jnp.concatenate([main[h], tails[:, 16 * h : 16 * h + 16]], axis=1)
        last = rows(16)
        gain[...] = jnp.concatenate([last[0:1, :], last[1:2, :64]], axis=1)


def saves():
    return (
        pltpu.VMEM((TOK, C), F32),
        pltpu.VMEM((TOK, 1), F32),
        pltpu.VMEM((TOK, C), BF16),
        pltpu.VMEM((TOK, C), BF16),
        pltpu.VMEM((TOK, C), BF16),
        pltpu.VMEM((TOK, C), BF16),
        pltpu.VMEM((WINDOWS, HEADS * WT, WT), BF16),
        pltpu.VMEM((TOK, C), BF16),
        pltpu.VMEM((WINDOWS, HEADS * WT, WT), F32),
        pltpu.VMEM((WINDOWS, HEADS * WT, WT), BF16),
    )


def totals():
    return (
        pltpu.VMEM((C, C), F32),
        pltpu.VMEM((C, C), F32),
        pltpu.VMEM((C, C), F32),
        pltpu.VMEM((C, C), F32),
        pltpu.VMEM((HEADS, WT, WT), F32),
        pltpu.VMEM((1, C), F32),
    )


def parts(lons):
    piece = (PIECE, 128)
    return (
        (pltpu.VMEM((SPOTS,) + piece, BF16),) * 3
        + (pltpu.VMEM((lons,) + piece, BF16),)
        + (pltpu.SemaphoreType.DMA((SPOTS,)),) * 4
        + (pltpu.SemaphoreType.DMA((lons,)),) * 2
        + (pltpu.SemaphoreType.DMA((SPOTS,)),) * 4
    )


def run_layer(lats, lons, *args):
    return pl.pallas_call(
        functools.partial(layer_kernel, lats, lons, Sum),
        out_shape=(
            jax.ShapeDtypeStruct((TOK, C), BF16),
            jax.ShapeDtypeStruct((2, 2, SPOTS, PIECE, 128), BF16),
        ),
        in_specs=[pl.BlockSpec(memory_space=pltpu.VMEM)] * 11,
        out_specs=(pl.BlockSpec(memory_space=pltpu.VMEM),) * 2,
        scratch_shapes=[
            saves(),
            saves(),
            totals(),
            totals(),
            pltpu.VMEM((TOK, TOK), BF16),
            pltpu.VMEM((16 * SLOT, TOK), BF16),
            pltpu.VMEM((2, 4 * SLOT, 72), BF16),
            pltpu.VMEM((WT, 4 * SLOT), BF16),
            pltpu.VMEM((4 * SLOT, WT), BF16),
            pltpu.VMEM((2, 72, 4 * SLOT), BF16),
            pltpu.VMEM((2, WT, WT), F32),
            pltpu.VMEM((TOK, C), BF16),
            pltpu.VMEM((LEVELS, 72, C), BF16),
            pltpu.VMEM((LEVELS, 72, C), F32),
            pltpu.VMEM((3, 4, WINDOWS, SLOT, C), BF16),
            pltpu.VMEM((3, 4, WINDOWS, SLOT, C), BF16),
            pltpu.SemaphoreType.DMA((27,)),
            pltpu.SemaphoreType.DMA((27,)),
            pltpu.VMEM((2, 2, SPOTS, PIECE, 128), BF16),
            parts(lons),
            parts(lons),
        ],
        compiler_params=pltpu.CompilerParams(
            collective_id=0, has_side_effects=True, vmem_limit_bytes=VMEM_LIMIT
        ),
        name="layer",
    )(*args)


def run_unpack(summed, d_tokens):
    block = (
        jax.ShapeDtypeStruct((1, C), F32),
        jax.ShapeDtypeStruct((C, 3 * C), F32),
        jax.ShapeDtypeStruct((C, C), F32),
        jax.ShapeDtypeStruct((HEADS, WT, WT), F32),
    )
    return pl.pallas_call(
        unpack_kernel,
        out_shape=(jax.ShapeDtypeStruct((TOK, C), BF16),) + block + block,
        in_specs=[pl.BlockSpec(memory_space=pltpu.VMEM)] * 2,
        out_specs=(pl.BlockSpec(memory_space=pltpu.VMEM),) * 9,
        compiler_params=pltpu.CompilerParams(vmem_limit_bytes=VMEM_LIMIT),
        name="unpack",
    )(summed, d_tokens)


def solution(mesh):
    lats, lons = mesh.shape["lat"], mesh.shape["lon"]
    route = routes()

    def stored(grid):
        return grid.transpose(0, 2, 3, 1, 4).reshape(TOK, C)

    def local(tokens, cotangent, gain_a, qkv_a, out_a, bias_a, gain_b, qkv_b, out_b, bias_b):
        d_tokens, summed = run_layer(
            lats,
            lons,
            stored(tokens),
            stored(cotangent),
            gain_a.reshape(1, C),
            qkv_a,
            out_a,
            bias_a,
            gain_b.reshape(1, C),
            qkv_b,
            out_b,
            bias_b,
            jnp.asarray(route),
        )
        d_tokens, ga, qa, oa, ba, gb, qb, ob, bb = run_unpack(
            summed.reshape(4 * HALF, 128), d_tokens
        )
        d_tokens = d_tokens.reshape(1, 6, 12, LEVELS, C).transpose(0, 3, 1, 2, 4)
        return (
            d_tokens,
            ga.reshape(C),
            qa,
            oa,
            ba,
            gb.reshape(C),
            qb,
            ob,
            bb,
        )

    grid = P("rep", None, "lat", "lon", None)
    return jax.shard_map(
        local,
        mesh=mesh,
        in_specs=(grid, grid) + (P(),) * 8,
        out_specs=(grid,) + (P(),) * 8,
        check_vma=False,
    )
```

```python
import functools

import jax
import jax.numpy as jnp
import numpy as np
from jax import lax
from jax.experimental import pallas as pl
from jax.experimental.pallas import tpu as pltpu
from jax.sharding import PartitionSpec as P

MESH = pl.DeviceIdType.MESH
C = 192
HEADS = 6
HEAD = 32
WT = 144
LEVELS = 8
WINDOWS = 4
TOK = WT * WINDOWS
FACTOR = HEAD ** (-0.5)
F32 = jnp.float32
BF16 = jnp.bfloat16
PIECE = 80
SPOTS = 16
HALF = PIECE * SPOTS
STEP = 144
GROUPS = ((0, 4, 0, 128), (4, 6, 128, 192))
LOG2E = 1.4426950408889634
SLOT = 48
VMEM_LIMIT = 40 * 1024 * 1024


def nt(left, right):
    return lax.dot_general(left, right, (((1,), (1,)), ((), ())), preferred_element_type=F32)


def tn(left, right):
    return lax.dot_general(left, right, (((0,), (0,)), ((), ())), preferred_element_type=F32)


def nn(left, right):
    return lax.dot_general(left, right, (((1,), (0,)), ((), ())), preferred_element_type=F32)


def routes():
    out = np.full((16, TOK), -1, np.int32)
    for z in range(LEVELS):
        for i in range(6):
            for j in range(12):
                stored = (i * 12 + j) * LEVELS + z
                token = z * 72 + i * 12 + j
                out[0, stored] = token
                out[1, token] = stored
                zr, ir, jr = (z - 1) % LEVELS, (i + 3) % 6, (j + 6) % 12
                quarter = 2 * (ir >= 3) + (jr >= 6)
                window, level = zr // 2, zr % 2
                inside = level * 18 + (ir % 3) * 6 + jr % 6
                slot = quarter * SLOT + inside
                place = level * 72 + ir * 12 + jr
                column = i * 12 + j
                out[2, stored] = (quarter * WINDOWS + window) * SLOT + inside
                out[3 + level, column] = slot
                out[5, slot] = place
                out[6, place] = slot
                out[7 + level, slot] = column
    return out


def head_mask(h, dtype):
    lane = lax.broadcasted_iota(jnp.int32, (1, C), 1)
    return jnp.where((lane >= h * HEAD) & (lane < (h + 1) * HEAD), 1.0, 0.0).astype(dtype)


def spread(value):
    return [
        jnp.concatenate(
            [value[:, lo:hi] * head_mask(h, BF16)[:, lo:hi] for h in range(first, last)], axis=0
        )
        for first, last, lo, hi in GROUPS
    ]


def gather_heads(stacked):
    parts = []
    for group, (first, last, lo, hi) in zip(stacked, GROUPS):
        lane = lax.broadcasted_iota(jnp.int32, (1, hi - lo), 1)
        total = group[:WT]
        for n in range(1, last - first):
            total = jnp.where(lane >= n * HEAD, group[n * WT : (n + 1) * WT], total)
        parts.append(total)
    return jnp.concatenate(parts, axis=1)


def stacked_rows(first, last):
    return slice(first * WT, last * WT)


def window_forward(w, x, gain, wq, wk, wv, bias, extra, save):
    (unit_s, inv_s, normed_s, q_s, k_s, v_s, p_s, att_s), (s_s, d_s) = save
    rows = pl.ds(w * WT, WT)
    xf = x.astype(F32)
    center = xf - jnp.mean(xf, axis=-1, keepdims=True)
    inv = lax.rsqrt(jnp.mean(center * center, axis=-1, keepdims=True) + 1e-05)
    unit = center * inv
    normed = (unit * gain).astype(BF16)
    unit_s[rows, :] = unit
    inv_s[rows, :] = inv
    normed_s[rows, :] = normed
    q = (nn(normed, wq) * (FACTOR * LOG2E)).astype(BF16)
    k = nn(normed, wk).astype(BF16)
    v = nn(normed, wv).astype(BF16)
    q_s[rows, :] = q
    k_s[rows, :] = k
    v_s[rows, :] = v
    for left, (head, stop, lo, hi) in zip(spread(q), GROUPS):
        s_s[w, stacked_rows(head, stop), :] = nt(left, k[:, lo:hi])
    for at in range(0, HEADS * WT, STEP):
        h, first = at // WT, at % WT
        s = s_s[w, at : at + STEP, :] + bias[h, first : first + STEP, :]
        if extra is not None:
            s = s + extra[first : first + STEP]
        e = jnp.exp2(s - jnp.max(s, axis=-1, keepdims=True))
        p = (e * (1.0 / jnp.sum(e, axis=-1, keepdims=True))).astype(BF16)
        p_s[w, at : at + STEP, :] = p
    att = gather_heads(
        [nn(p_s[w, stacked_rows(head, stop), :], v[:, lo:hi]) for head, stop, lo, hi in GROUPS]
    ).astype(BF16)
    att_s[rows, :] = att
    return xf, att


def window_backward(w, first_one, g, gain, wq, wk, wv, wo, save, grads):
    (unit_s, inv_s, normed_s, q_s, k_s, v_s, p_s, att_s), (s_s, d_s) = save
    gq_s, gk_s, gv_s, go_s, gb_s, gg_s = grads
    rows = pl.ds(w * WT, WT)

    def add(ref, index, value):
        ref[index] = value if first_one else ref[index] + value

    add(go_s, ..., tn(att_s[rows, :], g))
    da = spread(nt(g, wo).astype(BF16))
    v = v_s[rows, :]
    k = k_s[rows, :]
    dvs = []
    for left, (head, stop, lo, hi) in zip(da, GROUPS):
        s_s[w, stacked_rows(head, stop), :] = nt(left, v[:, lo:hi])
        dvs.append(tn(p_s[w, stacked_rows(head, stop), :], left))
    dv = jnp.concatenate(dvs, axis=1).astype(BF16)
    for at in range(0, HEADS * WT, STEP):
        h, first = at // WT, at % WT
        pf = p_s[w, at : at + STEP, :].astype(F32)
        t = pf * s_s[w, at : at + STEP, :]
        ds = t - pf * jnp.sum(t, axis=-1, keepdims=True)
        add(gb_s, (h, slice(first, first + STEP), slice(None)), ds)
        d_s[w, at : at + STEP, :] = ds.astype(BF16)
    dks, dqs = [], []
    for left, (head, stop, lo, hi) in zip(spread(q_s[rows, :]), GROUPS):
        ds = d_s[w, stacked_rows(head, stop), :]
        dks.append(tn(ds, left))
        dqs.append(nn(ds, k[:, lo:hi]))
    dk = (jnp.concatenate(dks, axis=1) * (1.0 / LOG2E)).astype(BF16)
    dq = (gather_heads(dqs) * FACTOR).astype(BF16)
    normed = normed_s[rows, :]
    add(gq_s, ..., tn(normed, dq))
    add(gk_s, ..., tn(normed, dk))
    add(gv_s, ..., tn(normed, dv))
    dn = nt(dq, wq) + nt(dk, wk) + nt(dv, wv)
    unit = unit_s[rows, :]
    add(gg_s, ..., jnp.sum(dn * unit, axis=0, keepdims=True))
    dh = dn * gain
    d_in = g.astype(F32) + inv_s[rows, :] * (
        dh
        - jnp.mean(dh, axis=-1, keepdims=True)
        - unit * jnp.mean(dh * unit, axis=-1, keepdims=True)
    )
    return d_in.astype(BF16)


def pack(out, grads):
    gq_s, gk_s, gv_s, go_s, gb_s, gg_s = grads
    at = 0

    def put(value):
        nonlocal at
        value = value.astype(BF16)
        done = 0
        while done < value.shape[0]:
            piece, first = (at + done) // PIECE, (at + done) % PIECE
            count = min(PIECE - first, value.shape[0] - done)
            out[piece // SPOTS, piece % SPOTS, first : first + count, :] = value[done : done + count]
            done += count
        at += value.shape[0]

    for ref in (gq_s, gk_s, gv_s, go_s):
        put(ref[:, :128])
    for one, two in ((gq_s, gk_s), (gv_s, go_s)):
        put(jnp.concatenate([one[:, 128:], two[:, 128:]], axis=1))
    for h in range(HEADS):
        put(gb_s[h, :, :128])
    tails = [gb_s[h, :, 128:] for h in range(HEADS)] + [jnp.zeros((WT, 32), F32)]
    put(jnp.concatenate(tails, axis=1))
    gg = gg_s[...]
    second = jnp.concatenate([gg[:, 128:], jnp.zeros((1, 64), F32)], axis=1)
    put(jnp.concatenate([gg[:, :128], second, jnp.zeros((14, 128), F32)], axis=0))
    put(jnp.zeros((2 * HALF - at, 128), F32))


class Sum:
    def __init__(self, lon_count, refs):
        self.in_ref, self.out_ref, self.core_s, self.part_s, self.plane_s, self.line_s = refs[:6]
        self.sems = refs[6:]
        rep, lat = lax.axis_index("rep"), lax.axis_index("lat")
        self.lon = lax.axis_index("lon")
        self.lons = lon_count
        self.core = rep % 2
        x_hi, x_lo, y = rep // 2, lat // 4, lat % 4
        self.me = (x_hi * 2 + x_lo) * 4 + y
        self.partner = {"rep": x_hi * 2 + (1 - self.core)}

    def spot(self, k):
        index = lax.rem(self.me + k, SPOTS)
        x, y = index // 4, index % 4
        return {"rep": (x // 2) * 2 + self.core, "lat": (x % 2) * 4 + y}

    def neighbour(self, k):
        return {"lon": lax.rem(self.lon + k, self.lons)}

    def greet(self, barrier):
        pl.semaphore_signal(barrier, inc=1, device_id=self.partner, device_id_type=MESH)

        def greet_plane(k, carry):
            pl.semaphore_signal(barrier, inc=1, device_id=self.spot(k), device_id_type=MESH)
            return carry

        def greet_line(k, carry):
            pl.semaphore_signal(barrier, inc=1, device_id=self.neighbour(k), device_id_type=MESH)
            return carry

        lax.fori_loop(1, SPOTS, greet_plane, 0)
        lax.fori_loop(1, self.lons, greet_line, 0)
        return SPOTS + self.lons - 1

    def copy(self, pair, k, source, target, device):
        return pltpu.make_async_remote_copy(
            src_ref=source,
            dst_ref=target,
            send_sem=self.sems[2 * pair].at[k],
            recv_sem=self.sems[2 * pair + 1].at[k],
            device_id=device,
            device_id_type=MESH,
        )

    def core_copy(self, k):
        j = lax.rem(self.me + k, SPOTS)
        return self.copy(0, k, self.in_ref.at[1 - self.core, j], self.core_s.at[k], self.partner)

    def plane_copy(self, k):
        return self.copy(1, k, self.part_s.at[k], self.plane_s.at[k], self.spot(k))

    def line_copy(self, k, slot):
        return self.copy(2, k, self.line_s.at[slot], self.line_s.at[slot], self.neighbour(k))

    def back_copy(self, k, j):
        ref = self.out_ref.at[self.core, j]
        return self.copy(3, k, ref, ref, self.spot(k))

    def last_copy(self, k, half):
        ref = self.out_ref.at[half, lax.rem(self.me + SPOTS - k, SPOTS)]
        return self.copy(4, k, ref, ref, self.partner)

    def merge(self, k):
        self.core_copy(k).wait()
        j = lax.rem(self.me + k, SPOTS)
        return self.in_ref[self.core, j].astype(F32) + self.core_s[k].astype(F32)

    def loop(self, first, last, step):
        def body(k, carry):
            step(k)
            return carry

        lax.fori_loop(first, last, body, 0)

    def start_core(self):
        self.loop(1, SPOTS, lambda k: self.core_copy(k).start())
        self.core_copy(0).start()

    def start_plane(self):
        def step(k):
            self.part_s[k] = self.merge(k).astype(BF16)
            self.plane_copy(k).start()

        self.loop(1, SPOTS, step)

    def start_line(self):
        def add(k, total):
            self.plane_copy(k).wait()
            return total + self.plane_s[k].astype(F32)

        total = lax.fori_loop(1, SPOTS, add, self.merge(0))
        self.line_s[self.lon] = total.astype(BF16)
        self.loop(1, self.lons, lambda k: self.line_copy(k, self.lon).start())

    def start_back(self):
        def wait(k):
            self.line_copy(k, self.lon).wait_send()
            self.line_copy(k, lax.rem(self.lon + self.lons - k, self.lons)).wait_recv()

        self.loop(1, self.lons, wait)
        total = self.line_s[0].astype(F32)
        for n in range(1, self.lons):
            total = total + self.line_s[n].astype(F32)
        self.out_ref[self.core, self.me] = total.astype(BF16)
        self.loop(1, SPOTS, lambda k: self.back_copy(k, self.me).start())
        self.last_copy(0, self.core).start()

    def start_last(self):
        def step(k):
            self.back_copy(k, self.me).wait_send()
            self.back_copy(k, lax.rem(self.me + SPOTS - k, SPOTS)).wait_recv()
            self.last_copy(k, self.core).start()

        self.loop(1, SPOTS, step)

    def finish(self):
        def step(k):
            self.last_copy(k, self.core).wait_send()
            self.last_copy(k, 1 - self.core).wait_recv()

        self.loop(0, SPOTS, step)


def layer_kernel(
    lats,
    lons,
    make_sum,
    tok_ref,
    cot_ref,
    gain_a,
    qkv_a,
    out_a,
    bias_a,
    gain_b,
    qkv_b,
    out_b,
    bias_b,
    route_ref,
    dtok_ref,
    sum_ref,
    scaled_s,
    room,
    save_a,
    save_b,
    grad_a,
    grad_b,
    order_s,
    slots_s,
    ahead_s,
    place_s,
    back_s,
    home_s,
    extra_s,
    x_a,
    mid_s,
    dmid_s,
    send_s,
    recv_s,
    send_sem,
    recv_sem,
    packed_s,
    parts_a,
    parts_b,
):
    lat = lax.axis_index("lat")
    lon = lax.axis_index("lon")
    save_a, save_b = (save_a, room), (save_b, room)

    def shifted(dlat, dlon):
        return {"lat": lax.rem(lat + dlat + lats, lats), "lon": lax.rem(lon + dlon + lons, lons)}

    before = [shifted(0, -1), shifted(-1, 0), shifted(-1, -1)]
    after = [shifted(0, 1), shifted(1, 0), shifted(1, 1)]

    def quarters(leg, window):
        copies = []
        for n, target in enumerate(after if leg == 2 else before):
            at = (leg, n + 1) if window is None else (leg, n + 1, window)
            sem = n if window is None else 3 + (leg - 1) * 12 + window * 3 + n
            copies.append(
                pltpu.make_async_remote_copy(
                    src_ref=send_s.at[at],
                    dst_ref=recv_s.at[at],
                    send_sem=send_sem.at[sem],
                    recv_sem=recv_sem.at[sem],
                    device_id=target,
                    device_id_type=MESH,
                )
            )
        return copies

    def post(leg, window, value):
        value = value.astype(BF16)
        recv_s[leg, 0, window] = value[:SLOT]
        for n in range(1, 4):
            send_s[leg, n, window] = value[n * SLOT : (n + 1) * SLOT]
        copies = quarters(leg, window)
        for copy in copies:
            copy.start()
        return copies

    def arrived(leg, window):
        return recv_s[leg, :, window].reshape(4 * SLOT, C)

    sum_a = make_sum(lons, (packed_s.at[0], sum_ref.at[0]) + parts_a)
    sum_b = make_sum(lons, (packed_s.at[1], sum_ref.at[1]) + parts_b)

    barrier = pltpu.get_barrier_semaphore()
    for other in before + after:
        pl.semaphore_signal(barrier, inc=1, device_id=other, device_id_type=MESH)
    greeted = 6 + sum_a.greet(barrier)

    def one_hot(rows, row, columns):
        target = route_ref[row : row + 1, :columns]
        spot = lax.broadcasted_iota(jnp.int32, (rows, columns), 0)
        return jnp.where(spot == target, 1.0, 0.0).astype(BF16)

    x_a[...] = nn(one_hot(TOK, 0, TOK), tok_ref[...]).astype(BF16)
    scaled_s[0] = bias_a[...] * LOG2E
    slots_s[...] = one_hot(16 * SLOT, 2, TOK)
    for n in range(2):
        ahead_s[n] = one_hot(4 * SLOT, 3 + n, 72)

    ga = gain_a[...]
    wo = out_a[...]
    wqa, wka, wva = (qkv_a[:, n * C : (n + 1) * C] for n in range(3))
    mids = [None] * WINDOWS
    backs = [None] * WINDOWS

    def send_mid(w):
        levels = (2 * w + 1, (2 * w + 2) % LEVELS)
        mids[w] = post(1, w, nn(ahead_s[0], mid_s[levels[0]]) + nn(ahead_s[1], mid_s[levels[1]]))

    for w in range(WINDOWS):
        xf, att = window_forward(w, x_a[w * WT : (w + 1) * WT, :], ga, wqa, wka, wva, scaled_s.at[0], None, save_a)
        middle = xf + nn(att, wo)
        mid_s[2 * w] = middle[:72].astype(BF16)
        mid_s[2 * w + 1] = middle[72:].astype(BF16)
        if w == 0:
            cots = nn(slots_s[...], cot_ref[...]).astype(BF16)
            cots = cots.reshape(4, WINDOWS, SLOT, C)
            recv_s[0, 0] = cots[0]
            for n in range(1, 4):
                send_s[0, n] = cots[n]
        else:
            if w == 1:
                pl.semaphore_wait(barrier, greeted)
                cot_copies = quarters(0, None)
                for copy in cot_copies:
                    copy.start()
            send_mid(w - 1)
    send_mid(WINDOWS - 1)

    order_s[...] = one_hot(TOK, 1, TOK)
    place_s[...] = one_hot(WT, 5, 4 * SLOT)
    back_s[...] = one_hot(4 * SLOT, 6, WT)
    for n in range(2):
        home_s[n] = one_hot(72, 7 + n, 4 * SLOT)
    scaled_s[1] = bias_b[...] * LOG2E

    def label(shape, axis, level):
        at = lax.broadcasted_iota(jnp.int32, shape, axis)
        upper = jnp.where(at >= 72, 1, 0)
        inside = at - 72 * upper
        late = jnp.where(inside >= 36, 1, 0) * jnp.where(lat == lats - 1, 1, 0)
        return late + 2 * upper if level else late

    for n in range(2):
        same = label((WT, WT), 0, n) == label((WT, WT), 1, n)
        extra_s[n] = jnp.where(same, 0.0, -1e30)

    gb = gain_b[...]
    wob = out_b[...]
    wqb, wkb, wvb = (qkv_b[:, n * C : (n + 1) * C] for n in range(3))

    for copy in cot_copies:
        copy.wait()
    for w in range(WINDOWS):
        for copy in mids[w]:
            copy.wait()
        x = nn(place_s[...], arrived(1, w)).astype(BF16)
        g = nn(place_s[...], arrived(0, w)).astype(BF16)
        window_forward(w, x, gb, wqb, wkb, wvb, scaled_s.at[1], extra_s.at[w // (WINDOWS - 1)], save_b)
        d_in = window_backward(w, w == 0, g, gb, wqb, wkb, wvb, wob, save_b, grad_b)
        backs[w] = post(2, w, nn(back_s[...], d_in))

    pack(packed_s.at[1], grad_b)
    sum_b.start_core()

    def take_back(w):
        for copy in backs[w]:
            copy.wait()
        value = arrived(2, w)
        dmid_s[2 * w + 1] = nn(home_s[0], value)
        dmid_s[(2 * w + 2) % LEVELS] = nn(home_s[1], value)

    def regular_back(w, first_one):
        g = jnp.concatenate([dmid_s[2 * w], dmid_s[2 * w + 1]], axis=0).astype(BF16)
        x_a[w * WT : (w + 1) * WT, :] = window_backward(
            w, first_one, g, ga, wqa, wka, wva, wo, save_a, grad_a
        )

    take_back(0)
    take_back(1)
    regular_back(1, True)
    sum_b.start_plane()
    take_back(2)
    regular_back(2, False)
    take_back(3)
    regular_back(3, False)
    regular_back(0, False)
    pack(packed_s.at[0], grad_a)
    sum_a.start_core()
    dtok_ref[...] = nn(order_s[...], x_a[...]).astype(BF16)
    sum_a.start_plane()
    sum_b.start_line()
    sum_b.start_back()
    sum_a.start_line()
    sum_b.start_last()
    sum_a.start_back()
    sum_a.start_last()
    sum_b.finish()
    sum_a.finish()


def unpack_kernel(in_ref, dtok_ref, dtok_out, *outs):
    dtok_out[...] = dtok_ref[...]
    for block in range(2):
        gain, qkv, out, bias = outs[4 * block : 4 * block + 4]
        at = block * 2 * HALF

        def rows(count):
            nonlocal at
            at += count
            return in_ref[at - count : at, :].astype(F32)

        gq, gk, gv, go = (rows(C) for _ in range(4))
        one, two = rows(C), rows(C)
        qkv[...] = jnp.concatenate(
            [gq, one[:, :64], gk, one[:, 64:], gv, two[:, :64]], axis=1
        )
        out[...] = jnp.concatenate([go, two[:, 64:]], axis=1)
        main = [rows(WT) for _ in range(HEADS)]
        tails = rows(WT)
        for h in range(HEADS):
            bias[h] = jnp.concatenate([main[h], tails[:, 16 * h : 16 * h + 16]], axis=1)
        last = rows(16)
        gain[...] = jnp.concatenate([last[0:1, :], last[1:2, :64]], axis=1)


def saves():
    return (
        pltpu.VMEM((TOK, C), F32),
        pltpu.VMEM((TOK, 1), F32),
        pltpu.VMEM((TOK, C), BF16),
        pltpu.VMEM((TOK, C), BF16),
        pltpu.VMEM((TOK, C), BF16),
        pltpu.VMEM((TOK, C), BF16),
        pltpu.VMEM((WINDOWS, HEADS * WT, WT), BF16),
        pltpu.VMEM((TOK, C), BF16),
    )


def rooms():
    return (
        pltpu.VMEM((WINDOWS, HEADS * WT, WT), F32),
        pltpu.VMEM((WINDOWS, HEADS * WT, WT), BF16),
    )


def totals():
    return (
        pltpu.VMEM((C, C), F32),
        pltpu.VMEM((C, C), F32),
        pltpu.VMEM((C, C), F32),
        pltpu.VMEM((C, C), F32),
        pltpu.VMEM((HEADS, WT, WT), F32),
        pltpu.VMEM((1, C), F32),
    )


def parts(lons):
    piece = (PIECE, 128)
    return (
        (pltpu.VMEM((SPOTS,) + piece, BF16),) * 3
        + (pltpu.VMEM((lons,) + piece, BF16),)
        + (pltpu.SemaphoreType.DMA((SPOTS,)),) * 4
        + (pltpu.SemaphoreType.DMA((lons,)),) * 2
        + (pltpu.SemaphoreType.DMA((SPOTS,)),) * 4
    )


def run_layer(lats, lons, *args):
    return pl.pallas_call(
        functools.partial(layer_kernel, lats, lons, Sum),
        out_shape=(
            jax.ShapeDtypeStruct((TOK, C), BF16),
            jax.ShapeDtypeStruct((2, 2, SPOTS, PIECE, 128), BF16),
        ),
        in_specs=[pl.BlockSpec(memory_space=pltpu.VMEM)] * 11,
        out_specs=(pl.BlockSpec(memory_space=pltpu.VMEM),) * 2,
        scratch_shapes=[
            pltpu.VMEM((2, HEADS, WT, WT), F32),
            rooms(),
            saves(),
            saves(),
            totals(),
            totals(),
            pltpu.VMEM((TOK, TOK), BF16),
            pltpu.VMEM((16 * SLOT, TOK), BF16),
            pltpu.VMEM((2, 4 * SLOT, 72), BF16),
            pltpu.VMEM((WT, 4 * SLOT), BF16),
            pltpu.VMEM((4 * SLOT, WT), BF16),
            pltpu.VMEM((2, 72, 4 * SLOT), BF16),
            pltpu.VMEM((2, WT, WT), F32),
            pltpu.VMEM((TOK, C), BF16),
            pltpu.VMEM((LEVELS, 72, C), BF16),
            pltpu.VMEM((LEVELS, 72, C), F32),
            pltpu.VMEM((3, 4, WINDOWS, SLOT, C), BF16),
            pltpu.VMEM((3, 4, WINDOWS, SLOT, C), BF16),
            pltpu.SemaphoreType.DMA((27,)),
            pltpu.SemaphoreType.DMA((27,)),
            pltpu.VMEM((2, 2, SPOTS, PIECE, 128), BF16),
            parts(lons),
            parts(lons),
        ],
        compiler_params=pltpu.CompilerParams(
            collective_id=0, has_side_effects=True, vmem_limit_bytes=VMEM_LIMIT
        ),
        name="layer",
    )(*args)


def run_unpack(summed, d_tokens):
    block = (
        jax.ShapeDtypeStruct((1, C), F32),
        jax.ShapeDtypeStruct((C, 3 * C), F32),
        jax.ShapeDtypeStruct((C, C), F32),
        jax.ShapeDtypeStruct((HEADS, WT, WT), F32),
    )
    return pl.pallas_call(
        unpack_kernel,
        out_shape=(jax.ShapeDtypeStruct((TOK, C), BF16),) + block + block,
        in_specs=[pl.BlockSpec(memory_space=pltpu.VMEM)] * 2,
        out_specs=(pl.BlockSpec(memory_space=pltpu.VMEM),) * 9,
        compiler_params=pltpu.CompilerParams(vmem_limit_bytes=VMEM_LIMIT),
        name="unpack",
    )(summed, d_tokens)


def solution(mesh):
    lats, lons = mesh.shape["lat"], mesh.shape["lon"]
    route = routes()

    def stored(grid):
        return grid.transpose(0, 2, 3, 1, 4).reshape(TOK, C)

    def local(tokens, cotangent, gain_a, qkv_a, out_a, bias_a, gain_b, qkv_b, out_b, bias_b):
        d_tokens, summed = run_layer(
            lats,
            lons,
            stored(tokens),
            stored(cotangent),
            gain_a.reshape(1, C),
            qkv_a,
            out_a,
            bias_a,
            gain_b.reshape(1, C),
            qkv_b,
            out_b,
            bias_b,
            jnp.asarray(route),
        )
        d_tokens, ga, qa, oa, ba, gb, qb, ob, bb = run_unpack(
            summed.reshape(4 * HALF, 128), d_tokens
        )
        d_tokens = d_tokens.reshape(1, 6, 12, LEVELS, C).transpose(0, 3, 1, 2, 4)
        return (
            d_tokens,
            ga.reshape(C),
            qa,
            oa,
            ba,
            gb.reshape(C),
            qb,
            ob,
            bb,
        )

    grid = P("rep", None, "lat", "lon", None)
    return jax.shard_map(
        local,
        mesh=mesh,
        in_specs=(grid, grid) + (P(),) * 8,
        out_specs=(grid,) + (P(),) * 8,
        check_vma=False,
    )
```

```python
import functools

import jax
import jax.numpy as jnp
import numpy as np
from jax import lax
from jax.experimental import pallas as pl
from jax.experimental.pallas import tpu as pltpu
from jax.sharding import PartitionSpec as P

MESH = pl.DeviceIdType.MESH
C = 192
HEADS = 6
HEAD = 32
WT = 144
LEVELS = 8
WINDOWS = 4
TOK = WT * WINDOWS
FACTOR = HEAD ** (-0.5)
F32 = jnp.float32
BF16 = jnp.bfloat16
PIECE = 80
SPOTS = 16
HALF = PIECE * SPOTS
STEP = 144
GROUPS = ((0, 4, 0, 128), (4, 6, 128, 192))
LOG2E = 1.4426950408889634
SLOT = 48
VMEM_LIMIT = 56 * 1024 * 1024


def nt(left, right):
    return lax.dot_general(left, right, (((1,), (1,)), ((), ())), preferred_element_type=F32)


def tn(left, right):
    return lax.dot_general(left, right, (((0,), (0,)), ((), ())), preferred_element_type=F32)


def nn(left, right):
    return lax.dot_general(left, right, (((1,), (0,)), ((), ())), preferred_element_type=F32)


def routes():
    out = np.full((16, TOK), -1, np.int32)
    for z in range(LEVELS):
        for i in range(6):
            for j in range(12):
                stored = (i * 12 + j) * LEVELS + z
                token = z * 72 + i * 12 + j
                out[0, stored] = token
                out[1, token] = stored
                zr, ir, jr = (z - 1) % LEVELS, (i + 3) % 6, (j + 6) % 12
                quarter = 2 * (ir >= 3) + (jr >= 6)
                window, level = zr // 2, zr % 2
                inside = level * 18 + (ir % 3) * 6 + jr % 6
                slot = quarter * SLOT + inside
                place = level * 72 + ir * 12 + jr
                column = i * 12 + j
                out[2, stored] = (quarter * WINDOWS + window) * SLOT + inside
                out[3 + level, column] = slot
                out[5, slot] = place
                out[6, place] = slot
                out[7 + level, slot] = column
    return out


def head_mask(h, dtype):
    lane = lax.broadcasted_iota(jnp.int32, (1, C), 1)
    return jnp.where((lane >= h * HEAD) & (lane < (h + 1) * HEAD), 1.0, 0.0).astype(dtype)


def spread(value):
    return [
        jnp.concatenate(
            [value[:, lo:hi] * head_mask(h, BF16)[:, lo:hi] for h in range(first, last)], axis=0
        )
        for first, last, lo, hi in GROUPS
    ]


def gather_heads(stacked):
    parts = []
    for group, (first, last, lo, hi) in zip(stacked, GROUPS):
        lane = lax.broadcasted_iota(jnp.int32, (1, hi - lo), 1)
        total = group[:WT]
        for n in range(1, last - first):
            total = jnp.where(lane >= n * HEAD, group[n * WT : (n + 1) * WT], total)
        parts.append(total)
    return jnp.concatenate(parts, axis=1)


def stacked_rows(first, last):
    return slice(first * WT, last * WT)


def window_forward(w, x, gain, wq, wk, wv, bias, extra, save):
    (unit_s, inv_s, normed_s, q_s, k_s, v_s, p_s, att_s), (s_s, d_s) = save
    rows = pl.ds(w * WT, WT)
    xf = x.astype(F32)
    center = xf - jnp.mean(xf, axis=-1, keepdims=True)
    inv = lax.rsqrt(jnp.mean(center * center, axis=-1, keepdims=True) + 1e-05)
    unit = center * inv
    normed = (unit * gain).astype(BF16)
    unit_s[rows, :] = unit
    inv_s[rows, :] = inv
    normed_s[rows, :] = normed
    q = (nn(normed, wq) * (FACTOR * LOG2E)).astype(BF16)
    k = nn(normed, wk).astype(BF16)
    v = nn(normed, wv).astype(BF16)
    q_s[rows, :] = q
    k_s[rows, :] = k
    v_s[rows, :] = v
    for left, (head, stop, lo, hi) in zip(spread(q), GROUPS):
        s_s[w, stacked_rows(head, stop), :] = nt(left, k[:, lo:hi])
    for at in range(0, HEADS * WT, STEP):
        h, first = at // WT, at % WT
        s = s_s[w, at : at + STEP, :] + bias[h, first : first + STEP, :]
        if extra is not None:
            s = s + extra[first : first + STEP]
        e = jnp.exp2(s - jnp.max(s, axis=-1, keepdims=True))
        p = (e * (1.0 / jnp.sum(e, axis=-1, keepdims=True))).astype(BF16)
        p_s[w, at : at + STEP, :] = p
    att = gather_heads(
        [nn(p_s[w, stacked_rows(head, stop), :], v[:, lo:hi]) for head, stop, lo, hi in GROUPS]
    ).astype(BF16)
    att_s[rows, :] = att
    return xf, att


def window_backward(w, first_one, g, gain, wq, wk, wv, wo, save, grads):
    (unit_s, inv_s, normed_s, q_s, k_s, v_s, p_s, att_s), (s_s, d_s) = save
    gq_s, gk_s, gv_s, go_s, gb_s, gg_s = grads
    rows = pl.ds(w * WT, WT)

    def add(ref, index, value):
        ref[index] = value if first_one else ref[index] + value

    add(go_s, ..., tn(att_s[rows, :], g))
    da = spread(nt(g, wo).astype(BF16))
    v = v_s[rows, :]
    k = k_s[rows, :]
    dvs = []
    for left, (head, stop, lo, hi) in zip(da, GROUPS):
        s_s[w, stacked_rows(head, stop), :] = nt(left, v[:, lo:hi])
        dvs.append(tn(p_s[w, stacked_rows(head, stop), :], left))
    dv = jnp.concatenate(dvs, axis=1).astype(BF16)
    for at in range(0, HEADS * WT, STEP):
        h, first = at // WT, at % WT
        pf = p_s[w, at : at + STEP, :].astype(F32)
        t = pf * s_s[w, at : at + STEP, :]
        ds = t - pf * jnp.sum(t, axis=-1, keepdims=True)
        add(gb_s, (h, slice(first, first + STEP), slice(None)), ds)
        d_s[w, at : at + STEP, :] = ds.astype(BF16)
    dks, dqs = [], []
    for left, (head, stop, lo, hi) in zip(spread(q_s[rows, :]), GROUPS):
        ds = d_s[w, stacked_rows(head, stop), :]
        dks.append(tn(ds, left))
        dqs.append(nn(ds, k[:, lo:hi]))
    dk = (jnp.concatenate(dks, axis=1) * (1.0 / LOG2E)).astype(BF16)
    dq = (gather_heads(dqs) * FACTOR).astype(BF16)
    normed = normed_s[rows, :]
    add(gq_s, ..., tn(normed, dq))
    add(gk_s, ..., tn(normed, dk))
    add(gv_s, ..., tn(normed, dv))
    dn = nt(dq, wq) + nt(dk, wk) + nt(dv, wv)
    unit = unit_s[rows, :]
    add(gg_s, ..., jnp.sum(dn * unit, axis=0, keepdims=True))
    dh = dn * gain
    d_in = g.astype(F32) + inv_s[rows, :] * (
        dh
        - jnp.mean(dh, axis=-1, keepdims=True)
        - unit * jnp.mean(dh * unit, axis=-1, keepdims=True)
    )
    return d_in.astype(BF16)


def pack(out, grads):
    gq_s, gk_s, gv_s, go_s, gb_s, gg_s = grads
    at = 0

    def put(value):
        nonlocal at
        value = value.astype(BF16)
        done = 0
        while done < value.shape[0]:
            piece, first = (at + done) // PIECE, (at + done) % PIECE
            count = min(PIECE - first, value.shape[0] - done)
            out[piece // SPOTS, piece % SPOTS, first : first + count, :] = value[done : done + count]
            done += count
        at += value.shape[0]

    for ref in (gq_s, gk_s, gv_s, go_s):
        put(ref[:, :128])
    for one, two in ((gq_s, gk_s), (gv_s, go_s)):
        put(jnp.concatenate([one[:, 128:], two[:, 128:]], axis=1))
    for h in range(HEADS):
        put(gb_s[h, :, :128])
    tails = [gb_s[h, :, 128:] for h in range(HEADS)] + [jnp.zeros((WT, 32), F32)]
    put(jnp.concatenate(tails, axis=1))
    gg = gg_s[...]
    second = jnp.concatenate([gg[:, 128:], jnp.zeros((1, 64), F32)], axis=1)
    put(jnp.concatenate([gg[:, :128], second, jnp.zeros((14, 128), F32)], axis=0))
    put(jnp.zeros((2 * HALF - at, 128), F32))


def ring_distance(step, count):
    return min(step, count - step)


FAR_FIRST = sorted(
    range(1, SPOTS), key=lambda k: -ring_distance(k // 4, 4) - ring_distance(k % 4, 4)
)


class Sum:
    def __init__(self, lon_count, refs):
        self.in_ref, self.out_ref, self.core_s, self.part_s, self.plane_s, self.line_s = refs[:6]
        self.sems = refs[6:]
        rep, lat = lax.axis_index("rep"), lax.axis_index("lat")
        self.lon = lax.axis_index("lon")
        self.lons = lon_count
        self.core = rep % 2
        x_hi, x_lo, y = rep // 2, lat // 4, lat % 4
        self.x, self.y = x_hi * 2 + x_lo, y
        self.me = self.x * 4 + y
        self.far_line = sorted(range(1, lon_count), key=lambda k: -ring_distance(k, lon_count))
        self.partner = {"rep": x_hi * 2 + (1 - self.core)}

    def there(self, k):
        return lax.rem(self.x + k // 4, 4) * 4 + lax.rem(self.y + k % 4, 4)

    def origin(self, k):
        return lax.rem(self.x + 4 - k // 4, 4) * 4 + lax.rem(self.y + 4 - k % 4, 4)

    def spot(self, k):
        x, y = lax.rem(self.x + k // 4, 4), lax.rem(self.y + k % 4, 4)
        return {"rep": (x // 2) * 2 + self.core, "lat": (x % 2) * 4 + y}

    def neighbour(self, k):
        return {"lon": lax.rem(self.lon + k, self.lons)}

    def greet(self, barrier):
        pl.semaphore_signal(barrier, inc=1, device_id=self.partner, device_id_type=MESH)

        def greet_plane(k, carry):
            pl.semaphore_signal(barrier, inc=1, device_id=self.spot(k), device_id_type=MESH)
            return carry

        def greet_line(k, carry):
            pl.semaphore_signal(barrier, inc=1, device_id=self.neighbour(k), device_id_type=MESH)
            return carry

        lax.fori_loop(1, SPOTS, greet_plane, 0)
        lax.fori_loop(1, self.lons, greet_line, 0)
        return SPOTS + self.lons - 1

    def copy(self, pair, k, source, target, device):
        return pltpu.make_async_remote_copy(
            src_ref=source,
            dst_ref=target,
            send_sem=self.sems[2 * pair].at[k],
            recv_sem=self.sems[2 * pair + 1].at[k],
            device_id=device,
            device_id_type=MESH,
        )

    def core_copy(self, k):
        j = self.there(k)
        return self.copy(0, k, self.in_ref.at[1 - self.core, j], self.core_s.at[k], self.partner)

    def plane_copy(self, k):
        return self.copy(1, k, self.part_s.at[k], self.plane_s.at[k], self.spot(k))

    def line_copy(self, k, slot):
        return self.copy(2, k, self.line_s.at[slot], self.line_s.at[slot], self.neighbour(k))

    def back_copy(self, k, j):
        ref = self.out_ref.at[self.core, j]
        return self.copy(3, k, ref, ref, self.spot(k))

    def last_copy(self, k, half):
        ref = self.out_ref.at[half, self.origin(k)]
        return self.copy(4, k, ref, ref, self.partner)

    def merge(self, k):
        self.core_copy(k).wait()
        j = self.there(k)
        return self.in_ref[self.core, j].astype(F32) + self.core_s[k].astype(F32)

    def loop(self, first, last, step):
        def body(k, carry):
            step(k)
            return carry

        lax.fori_loop(first, last, body, 0)

    def start_core(self):
        for k in FAR_FIRST + [0]:
            self.core_copy(k).start()

    def start_plane(self):
        for k in FAR_FIRST:
            self.part_s[k] = self.merge(k).astype(BF16)
            self.plane_copy(k).start()

    def start_line(self):
        def add(k, total):
            self.plane_copy(k).wait()
            return total + self.plane_s[k].astype(F32)

        total = lax.fori_loop(1, SPOTS, add, self.merge(0))
        self.line_s[self.lon] = total.astype(BF16)
        for k in self.far_line:
            self.line_copy(k, self.lon).start()

    def start_back(self):
        def wait(k):
            self.line_copy(k, self.lon).wait_send()
            self.line_copy(k, lax.rem(self.lon + self.lons - k, self.lons)).wait_recv()

        self.loop(1, self.lons, wait)
        total = self.line_s[0].astype(F32)
        for n in range(1, self.lons):
            total = total + self.line_s[n].astype(F32)
        self.out_ref[self.core, self.me] = total.astype(BF16)
        for k in FAR_FIRST:
            self.back_copy(k, self.me).start()
        self.last_copy(0, self.core).start()

    def start_last(self):
        for k in FAR_FIRST[::-1]:
            self.back_copy(k, self.origin(k)).wait_recv()
            self.last_copy(k, self.core).start()

    def finish(self):
        self.loop(1, SPOTS, lambda k: self.back_copy(k, self.me).wait_send())
        self.loop(0, SPOTS, lambda k: self.last_copy(k, self.core).wait_send())
        self.loop(0, SPOTS, lambda k: self.last_copy(k, 1 - self.core).wait_recv())


def layer_kernel(
    lats,
    lons,
    make_sum,
    tok_ref,
    cot_ref,
    gain_a,
    qkv_a,
    out_a,
    bias_a,
    gain_b,
    qkv_b,
    out_b,
    bias_b,
    route_ref,
    dtok_ref,
    sum_ref,
    inputs_s,
    input_sem,
    scaled_s,
    room,
    save_a,
    save_b,
    grad_a,
    grad_b,
    order_s,
    slots_s,
    ahead_s,
    place_s,
    back_s,
    home_s,
    extra_s,
    x_a,
    mid_s,
    dmid_s,
    send_s,
    recv_s,
    send_sem,
    recv_sem,
    packed_s,
    parts_a,
    parts_b,
):
    lat = lax.axis_index("lat")
    lon = lax.axis_index("lon")
    save_a, save_b = (save_a, room), (save_b, room)

    def shifted(dlat, dlon):
        return {"lat": lax.rem(lat + dlat + lats, lats), "lon": lax.rem(lon + dlon + lons, lons)}

    before = [shifted(0, -1), shifted(-1, 0), shifted(-1, -1)]
    after = [shifted(0, 1), shifted(1, 0), shifted(1, 1)]

    def quarters(leg, window):
        copies = []
        for n, target in enumerate(after if leg == 2 else before):
            at = (leg, n + 1) if window is None else (leg, n + 1, window)
            sem = n if window is None else 3 + (leg - 1) * 12 + window * 3 + n
            copies.append(
                pltpu.make_async_remote_copy(
                    src_ref=send_s.at[at],
                    dst_ref=recv_s.at[at],
                    send_sem=send_sem.at[sem],
                    recv_sem=recv_sem.at[sem],
                    device_id=target,
                    device_id_type=MESH,
                )
            )
        return copies

    def post(leg, window, value):
        value = value.astype(BF16)
        recv_s[leg, 0, window] = value[:SLOT]
        for n in range(1, 4):
            send_s[leg, n, window] = value[n * SLOT : (n + 1) * SLOT]
        copies = quarters(leg, window)
        for copy in copies:
            copy.start()
        return copies

    def arrived(leg, window):
        return recv_s[leg, :, window].reshape(4 * SLOT, C)

    sources = (
        tok_ref, cot_ref, gain_a, qkv_a, out_a, bias_a, gain_b, qkv_b, out_b, bias_b, route_ref
    )
    loads = [
        pltpu.make_async_copy(source, target, input_sem.at[n])
        for n, (source, target) in enumerate(zip(sources, inputs_s))
    ]
    for n in (10, 0, 2, 3, 4, 5, 1, 6, 7, 8, 9):
        loads[n].start()
    tok_ref, cot_ref, gain_a, qkv_a, out_a, bias_a, gain_b, qkv_b, out_b, bias_b, route_ref = inputs_s

    sum_a = make_sum(lons, (packed_s.at[0], sum_ref.at[0]) + parts_a)
    sum_b = make_sum(lons, (packed_s.at[1], sum_ref.at[1]) + parts_b)

    barrier = pltpu.get_barrier_semaphore()
    for other in before + after:
        pl.semaphore_signal(barrier, inc=1, device_id=other, device_id_type=MESH)
    greeted = 6 + sum_a.greet(barrier)

    def one_hot(rows, row, columns):
        target = route_ref[row : row + 1, :columns]
        spot = lax.broadcasted_iota(jnp.int32, (rows, columns), 0)
        return jnp.where(spot == target, 1.0, 0.0).astype(BF16)

    loads[10].wait()
    loads[0].wait()
    x_a[...] = nn(one_hot(TOK, 0, TOK), tok_ref[...]).astype(BF16)
    for n in (2, 3, 4, 5):
        loads[n].wait()
    scaled_s[0] = bias_a[...] * LOG2E
    slots_s[...] = one_hot(16 * SLOT, 2, TOK)
    for n in range(2):
        ahead_s[n] = one_hot(4 * SLOT, 3 + n, 72)

    ga = gain_a[...]
    wo = out_a[...]
    wqa, wka, wva = (qkv_a[:, n * C : (n + 1) * C] for n in range(3))
    mids = [None] * WINDOWS
    backs = [None] * WINDOWS

    def send_mid(w):
        levels = (2 * w + 1, (2 * w + 2) % LEVELS)
        mids[w] = post(1, w, nn(ahead_s[0], mid_s[levels[0]]) + nn(ahead_s[1], mid_s[levels[1]]))

    for w in range(WINDOWS):
        xf, att = window_forward(w, x_a[w * WT : (w + 1) * WT, :], ga, wqa, wka, wva, scaled_s.at[0], None, save_a)
        middle = xf + nn(att, wo)
        mid_s[2 * w] = middle[:72].astype(BF16)
        mid_s[2 * w + 1] = middle[72:].astype(BF16)
        if w == 0:
            loads[1].wait()
            cots = nn(slots_s[...], cot_ref[...]).astype(BF16)
            cots = cots.reshape(4, WINDOWS, SLOT, C)
            recv_s[0, 0] = cots[0]
            for n in range(1, 4):
                send_s[0, n] = cots[n]
        else:
            if w == 1:
                pl.semaphore_wait(barrier, greeted)
                cot_copies = quarters(0, None)
                for copy in cot_copies:
                    copy.start()
            send_mid(w - 1)
    send_mid(WINDOWS - 1)

    order_s[...] = one_hot(TOK, 1, TOK)
    place_s[...] = one_hot(WT, 5, 4 * SLOT)
    back_s[...] = one_hot(4 * SLOT, 6, WT)
    for n in range(2):
        home_s[n] = one_hot(72, 7 + n, 4 * SLOT)
    for n in (6, 7, 8, 9):
        loads[n].wait()
    scaled_s[1] = bias_b[...] * LOG2E

    def label(shape, axis, level):
        at = lax.broadcasted_iota(jnp.int32, shape, axis)
        upper = jnp.where(at >= 72, 1, 0)
        inside = at - 72 * upper
        late = jnp.where(inside >= 36, 1, 0) * jnp.where(lat == lats - 1, 1, 0)
        return late + 2 * upper if level else late

    for n in range(2):
        same = label((WT, WT), 0, n) == label((WT, WT), 1, n)
        extra_s[n] = jnp.where(same, 0.0, -1e30)

    gb = gain_b[...]
    wob = out_b[...]
    wqb, wkb, wvb = (qkv_b[:, n * C : (n + 1) * C] for n in range(3))

    for copy in cot_copies:
        copy.wait()
    gs = [None] * WINDOWS

    def shifted_forward(w):
        for copy in mids[w]:
            copy.wait()
        x = nn(place_s[...], arrived(1, w)).astype(BF16)
        gs[w] = nn(place_s[...], arrived(0, w)).astype(BF16)
        extra = extra_s.at[w // (WINDOWS - 1)]
        window_forward(w, x, gb, wqb, wkb, wvb, scaled_s.at[1], extra, save_b)

    shifted_forward(0)
    for w in range(WINDOWS):
        if w + 1 < WINDOWS:
            shifted_forward(w + 1)
        d_in = window_backward(w, w == 0, gs[w], gb, wqb, wkb, wvb, wob, save_b, grad_b)
        backs[w] = post(2, w, nn(back_s[...], d_in))

    pack(packed_s.at[1], grad_b)
    sum_b.start_core()

    def take_back(w):
        for copy in backs[w]:
            copy.wait()
        value = arrived(2, w)
        dmid_s[2 * w + 1] = nn(home_s[0], value)
        dmid_s[(2 * w + 2) % LEVELS] = nn(home_s[1], value)

    def regular_back(w, first_one):
        g = jnp.concatenate([dmid_s[2 * w], dmid_s[2 * w + 1]], axis=0).astype(BF16)
        x_a[w * WT : (w + 1) * WT, :] = window_backward(
            w, first_one, g, ga, wqa, wka, wva, wo, save_a, grad_a
        )

    take_back(0)
    take_back(1)
    regular_back(1, True)
    sum_b.start_plane()
    take_back(2)
    regular_back(2, False)
    take_back(3)
    regular_back(3, False)
    regular_back(0, False)
    pack(packed_s.at[0], grad_a)
    sum_a.start_core()
    dtok_ref[...] = nn(order_s[...], x_a[...]).astype(BF16)
    sum_a.start_plane()
    sum_b.start_line()
    sum_b.start_back()
    sum_a.start_line()
    sum_b.start_last()
    sum_a.start_back()
    sum_a.start_last()
    sum_b.finish()
    sum_a.finish()


def unpack_kernel(in_ref, dtok_ref, dtok_out, *outs):
    dtok_out[...] = dtok_ref[...]
    for block in range(2):
        gain, qkv, out, bias = outs[4 * block : 4 * block + 4]
        at = block * 2 * HALF

        def rows(count):
            nonlocal at
            at += count
            return in_ref[at - count : at, :].astype(F32)

        gq, gk, gv, go = (rows(C) for _ in range(4))
        one, two = rows(C), rows(C)
        qkv[...] = jnp.concatenate(
            [gq, one[:, :64], gk, one[:, 64:], gv, two[:, :64]], axis=1
        )
        out[...] = jnp.concatenate([go, two[:, 64:]], axis=1)
        main = [rows(WT) for _ in range(HEADS)]
        tails = rows(WT)
        for h in range(HEADS):
            bias[h] = jnp.concatenate([main[h], tails[:, 16 * h : 16 * h + 16]], axis=1)
        last = rows(16)
        gain[...] = jnp.concatenate([last[0:1, :], last[1:2, :64]], axis=1)


def saves():
    return (
        pltpu.VMEM((TOK, C), F32),
        pltpu.VMEM((TOK, 1), F32),
        pltpu.VMEM((TOK, C), BF16),
        pltpu.VMEM((TOK, C), BF16),
        pltpu.VMEM((TOK, C), BF16),
        pltpu.VMEM((TOK, C), BF16),
        pltpu.VMEM((WINDOWS, HEADS * WT, WT), BF16),
        pltpu.VMEM((TOK, C), BF16),
    )


def rooms():
    return (
        pltpu.VMEM((WINDOWS, HEADS * WT, WT), F32),
        pltpu.VMEM((WINDOWS, HEADS * WT, WT), BF16),
    )


def totals():
    return (
        pltpu.VMEM((C, C), F32),
        pltpu.VMEM((C, C), F32),
        pltpu.VMEM((C, C), F32),
        pltpu.VMEM((C, C), F32),
        pltpu.VMEM((HEADS, WT, WT), F32),
        pltpu.VMEM((1, C), F32),
    )


def parts(lons):
    piece = (PIECE, 128)
    return (
        (pltpu.VMEM((SPOTS,) + piece, BF16),) * 3
        + (pltpu.VMEM((lons,) + piece, BF16),)
        + (pltpu.SemaphoreType.DMA((SPOTS,)),) * 4
        + (pltpu.SemaphoreType.DMA((lons,)),) * 2
        + (pltpu.SemaphoreType.DMA((SPOTS,)),) * 4
    )


def run_layer(lats, lons, *args):
    return pl.pallas_call(
        functools.partial(layer_kernel, lats, lons, Sum),
        out_shape=(
            jax.ShapeDtypeStruct((TOK, C), BF16),
            jax.ShapeDtypeStruct((2, 2, SPOTS, PIECE, 128), BF16),
        ),
        in_specs=[pl.BlockSpec(memory_space=pl.ANY)] * 11,
        out_specs=(pl.BlockSpec(memory_space=pltpu.VMEM),) * 2,
        scratch_shapes=[
            tuple(pltpu.VMEM(arg.shape, arg.dtype) for arg in args),
            pltpu.SemaphoreType.DMA((11,)),
            pltpu.VMEM((2, HEADS, WT, WT), F32),
            rooms(),
            saves(),
            saves(),
            totals(),
            totals(),
            pltpu.VMEM((TOK, TOK), BF16),
            pltpu.VMEM((16 * SLOT, TOK), BF16),
            pltpu.VMEM((2, 4 * SLOT, 72), BF16),
            pltpu.VMEM((WT, 4 * SLOT), BF16),
            pltpu.VMEM((4 * SLOT, WT), BF16),
            pltpu.VMEM((2, 72, 4 * SLOT), BF16),
            pltpu.VMEM((2, WT, WT), F32),
            pltpu.VMEM((TOK, C), BF16),
            pltpu.VMEM((LEVELS, 72, C), BF16),
            pltpu.VMEM((LEVELS, 72, C), F32),
            pltpu.VMEM((3, 4, WINDOWS, SLOT, C), BF16),
            pltpu.VMEM((3, 4, WINDOWS, SLOT, C), BF16),
            pltpu.SemaphoreType.DMA((27,)),
            pltpu.SemaphoreType.DMA((27,)),
            pltpu.VMEM((2, 2, SPOTS, PIECE, 128), BF16),
            parts(lons),
            parts(lons),
        ],
        compiler_params=pltpu.CompilerParams(
            collective_id=0, has_side_effects=True, vmem_limit_bytes=VMEM_LIMIT
        ),
        name="layer",
    )(*args)


def run_unpack(summed, d_tokens):
    block = (
        jax.ShapeDtypeStruct((1, C), F32),
        jax.ShapeDtypeStruct((C, 3 * C), F32),
        jax.ShapeDtypeStruct((C, C), F32),
        jax.ShapeDtypeStruct((HEADS, WT, WT), F32),
    )
    return pl.pallas_call(
        unpack_kernel,
        out_shape=(jax.ShapeDtypeStruct((TOK, C), BF16),) + block + block,
        in_specs=[pl.BlockSpec(memory_space=pltpu.VMEM)] * 2,
        out_specs=(pl.BlockSpec(memory_space=pltpu.VMEM),) * 9,
        compiler_params=pltpu.CompilerParams(vmem_limit_bytes=VMEM_LIMIT),
        name="unpack",
    )(summed, d_tokens)


def solution(mesh):
    lats, lons = mesh.shape["lat"], mesh.shape["lon"]
    route = routes()

    def stored(grid):
        return grid.transpose(0, 2, 3, 1, 4).reshape(TOK, C)

    def local(tokens, cotangent, gain_a, qkv_a, out_a, bias_a, gain_b, qkv_b, out_b, bias_b):
        d_tokens, summed = run_layer(
            lats,
            lons,
            stored(tokens),
            stored(cotangent),
            gain_a.reshape(1, C),
            qkv_a,
            out_a,
            bias_a,
            gain_b.reshape(1, C),
            qkv_b,
            out_b,
            bias_b,
            jnp.asarray(route),
        )
        d_tokens, ga, qa, oa, ba, gb, qb, ob, bb = run_unpack(
            summed.reshape(4 * HALF, 128), d_tokens
        )
        d_tokens = d_tokens.reshape(1, 6, 12, LEVELS, C).transpose(0, 3, 1, 2, 4)
        return (
            d_tokens,
            ga.reshape(C),
            qa,
            oa,
            ba,
            gb.reshape(C),
            qb,
            ob,
            bb,
        )

    grid = P("rep", None, "lat", "lon", None)
    return jax.shard_map(
        local,
        mesh=mesh,
        in_specs=(grid, grid) + (P(),) * 8,
        out_specs=(grid,) + (P(),) * 8,
        check_vma=False,
    )
```

```python
import functools

import jax
import jax.numpy as jnp
import numpy as np
from jax import lax
from jax.experimental import pallas as pl
from jax.experimental.pallas import tpu as pltpu
from jax.sharding import PartitionSpec as P

MESH = pl.DeviceIdType.MESH
C = 192
HEADS = 6
HEAD = 32
WT = 144
LEVELS = 8
WINDOWS = 4
TOK = WT * WINDOWS
FACTOR = HEAD ** (-0.5)
F32 = jnp.float32
BF16 = jnp.bfloat16
PIECE = 80
SPOTS = 16
HALF = PIECE * SPOTS
STEP = 144
GROUPS = ((0, 4, 0, 128), (4, 6, 128, 192))
LOG2E = 1.4426950408889634
SLOT = 48
VMEM_LIMIT = 56 * 1024 * 1024


def nt(left, right):
    return lax.dot_general(left, right, (((1,), (1,)), ((), ())), preferred_element_type=F32)


def tn(left, right):
    return lax.dot_general(left, right, (((0,), (0,)), ((), ())), preferred_element_type=F32)


def nn(left, right):
    return lax.dot_general(left, right, (((1,), (0,)), ((), ())), preferred_element_type=F32)


def routes():
    out = np.full((16, TOK), -1, np.int32)
    for z in range(LEVELS):
        for i in range(6):
            for j in range(12):
                stored = (i * 12 + j) * LEVELS + z
                token = z * 72 + i * 12 + j
                out[0, stored] = token
                out[1, token] = stored
                zr, ir, jr = (z - 1) % LEVELS, (i + 3) % 6, (j + 6) % 12
                quarter = 2 * (ir >= 3) + (jr >= 6)
                window, level = zr // 2, zr % 2
                inside = level * 18 + (ir % 3) * 6 + jr % 6
                slot = quarter * SLOT + inside
                place = level * 72 + ir * 12 + jr
                column = i * 12 + j
                out[2, stored] = (quarter * WINDOWS + window) * SLOT + inside
                out[3 + level, column] = slot
                out[5, slot] = place
                out[6, place] = slot
                out[7 + level, slot] = column
    return out


def head_mask(h, dtype):
    lane = lax.broadcasted_iota(jnp.int32, (1, C), 1)
    return jnp.where((lane >= h * HEAD) & (lane < (h + 1) * HEAD), 1.0, 0.0).astype(dtype)


def spread(value):
    return [
        jnp.concatenate(
            [value[:, lo:hi] * head_mask(h, BF16)[:, lo:hi] for h in range(first, last)], axis=0
        )
        for first, last, lo, hi in GROUPS
    ]


def gather_heads(stacked):
    parts = []
    for group, (first, last, lo, hi) in zip(stacked, GROUPS):
        lane = lax.broadcasted_iota(jnp.int32, (1, hi - lo), 1)
        total = group[:WT]
        for n in range(1, last - first):
            total = jnp.where(lane >= n * HEAD, group[n * WT : (n + 1) * WT], total)
        parts.append(total)
    return jnp.concatenate(parts, axis=1)


def stacked_rows(first, last):
    return slice(first * WT, last * WT)


def window_forward(w, x, gain, wq, wk, wv, bias, extra, save):
    (unit_s, inv_s, normed_s, q_s, k_s, v_s, p_s, att_s), (s_s, d_s) = save
    rows = pl.ds(w * WT, WT)
    xf = x.astype(F32)
    center = xf - jnp.mean(xf, axis=-1, keepdims=True)
    inv = lax.rsqrt(jnp.mean(center * center, axis=-1, keepdims=True) + 1e-05)
    unit = center * inv
    normed = (unit * gain).astype(BF16)
    unit_s[rows, :] = unit
    inv_s[rows, :] = inv
    normed_s[rows, :] = normed
    q = (nn(normed, wq) * (FACTOR * LOG2E)).astype(BF16)
    k = nn(normed, wk).astype(BF16)
    v = nn(normed, wv).astype(BF16)
    q_s[rows, :] = q
    k_s[rows, :] = k
    v_s[rows, :] = v
    for left, (head, stop, lo, hi) in zip(spread(q), GROUPS):
        s_s[w, stacked_rows(head, stop), :] = nt(left, k[:, lo:hi])
    for at in range(0, HEADS * WT, STEP):
        h, first = at // WT, at % WT
        s = s_s[w, at : at + STEP, :] + bias[h, first : first + STEP, :]
        if extra is not None:
            s = s + extra[first : first + STEP]
        e = jnp.exp2(s - jnp.max(s, axis=-1, keepdims=True))
        p = (e * (1.0 / jnp.sum(e, axis=-1, keepdims=True))).astype(BF16)
        p_s[w, at : at + STEP, :] = p
    att = gather_heads(
        [nn(p_s[w, stacked_rows(head, stop), :], v[:, lo:hi]) for head, stop, lo, hi in GROUPS]
    ).astype(BF16)
    att_s[rows, :] = att
    return xf, att


def window_backward(w, first_one, g, gain, wq, wk, wv, wo, save, grads):
    (unit_s, inv_s, normed_s, q_s, k_s, v_s, p_s, att_s), (s_s, d_s) = save
    gq_s, gk_s, gv_s, go_s, gb_s, gg_s = grads
    rows = pl.ds(w * WT, WT)

    def add(ref, index, value):
        ref[index] = value if first_one else ref[index] + value

    add(go_s, ..., tn(att_s[rows, :], g))
    da = spread(nt(g, wo).astype(BF16))
    v = v_s[rows, :]
    k = k_s[rows, :]
    dvs = []
    for left, (head, stop, lo, hi) in zip(da, GROUPS):
        s_s[w, stacked_rows(head, stop), :] = nt(left, v[:, lo:hi])
        dvs.append(tn(p_s[w, stacked_rows(head, stop), :], left))
    dv = jnp.concatenate(dvs, axis=1).astype(BF16)
    for at in range(0, HEADS * WT, STEP):
        h, first = at // WT, at % WT
        pf = p_s[w, at : at + STEP, :].astype(F32)
        t = pf * s_s[w, at : at + STEP, :]
        ds = t - pf * jnp.sum(t, axis=-1, keepdims=True)
        add(gb_s, (h, slice(first, first + STEP), slice(None)), ds)
        d_s[w, at : at + STEP, :] = ds.astype(BF16)
    dks, dqs = [], []
    for left, (head, stop, lo, hi) in zip(spread(q_s[rows, :]), GROUPS):
        ds = d_s[w, stacked_rows(head, stop), :]
        dks.append(tn(ds, left))
        dqs.append(nn(ds, k[:, lo:hi]))
    dk = (jnp.concatenate(dks, axis=1) * (1.0 / LOG2E)).astype(BF16)
    dq = (gather_heads(dqs) * FACTOR).astype(BF16)
    normed = normed_s[rows, :]
    add(gq_s, ..., tn(normed, dq))
    add(gk_s, ..., tn(normed, dk))
    add(gv_s, ..., tn(normed, dv))
    dn = nt(dq, wq) + nt(dk, wk) + nt(dv, wv)
    unit = unit_s[rows, :]
    add(gg_s, ..., jnp.sum(dn * unit, axis=0, keepdims=True))
    dh = dn * gain
    d_in = g.astype(F32) + inv_s[rows, :] * (
        dh
        - jnp.mean(dh, axis=-1, keepdims=True)
        - unit * jnp.mean(dh * unit, axis=-1, keepdims=True)
    )
    return d_in.astype(BF16)


def pack(out, grads):
    gq_s, gk_s, gv_s, go_s, gb_s, gg_s = grads
    at = 0

    def put(value):
        nonlocal at
        value = value.astype(BF16)
        done = 0
        while done < value.shape[0]:
            piece, first = (at + done) // PIECE, (at + done) % PIECE
            count = min(PIECE - first, value.shape[0] - done)
            out[piece // SPOTS, piece % SPOTS, first : first + count, :] = value[done : done + count]
            done += count
        at += value.shape[0]

    for ref in (gq_s, gk_s, gv_s, go_s):
        put(ref[:, :128])
    for one, two in ((gq_s, gk_s), (gv_s, go_s)):
        put(jnp.concatenate([one[:, 128:], two[:, 128:]], axis=1))
    for h in range(HEADS):
        put(gb_s[h, :, :128])
    tails = [gb_s[h, :, 128:] for h in range(HEADS)] + [jnp.zeros((WT, 32), F32)]
    put(jnp.concatenate(tails, axis=1))
    gg = gg_s[...]
    second = jnp.concatenate([gg[:, 128:], jnp.zeros((1, 64), F32)], axis=1)
    put(jnp.concatenate([gg[:, :128], second, jnp.zeros((14, 128), F32)], axis=0))
    put(jnp.zeros((2 * HALF - at, 128), F32))


def ring_distance(step, count):
    return min(step, count - step)


FAR_FIRST = sorted(
    range(1, SPOTS), key=lambda k: -ring_distance(k // 4, 4) - ring_distance(k % 4, 4)
)


class Sum:
    def __init__(self, lon_count, refs):
        self.in_ref, self.out_ref, self.core_s, self.part_s, self.plane_s, self.line_s = refs[:6]
        self.sems = refs[6:]
        rep, lat = lax.axis_index("rep"), lax.axis_index("lat")
        self.lon = lax.axis_index("lon")
        self.lons = lon_count
        self.core = rep % 2
        x_hi, x_lo, y = rep // 2, lat // 4, lat % 4
        self.x, self.y = x_hi * 2 + x_lo, y
        self.me = self.x * 4 + y
        self.far_line = sorted(range(1, lon_count), key=lambda k: -ring_distance(k, lon_count))
        self.partner = {"rep": x_hi * 2 + (1 - self.core)}

    def there(self, k):
        return lax.rem(self.x + k // 4, 4) * 4 + lax.rem(self.y + k % 4, 4)

    def origin(self, k):
        return lax.rem(self.x + 4 - k // 4, 4) * 4 + lax.rem(self.y + 4 - k % 4, 4)

    def spot(self, k):
        x, y = lax.rem(self.x + k // 4, 4), lax.rem(self.y + k % 4, 4)
        return {"rep": (x // 2) * 2 + self.core, "lat": (x % 2) * 4 + y}

    def neighbour(self, k):
        return {"lon": lax.rem(self.lon + k, self.lons)}

    def greet(self, barrier):
        pl.semaphore_signal(barrier, inc=1, device_id=self.partner, device_id_type=MESH)

        def greet_plane(k, carry):
            pl.semaphore_signal(barrier, inc=1, device_id=self.spot(k), device_id_type=MESH)
            return carry

        def greet_line(k, carry):
            pl.semaphore_signal(barrier, inc=1, device_id=self.neighbour(k), device_id_type=MESH)
            return carry

        lax.fori_loop(1, SPOTS, greet_plane, 0)
        lax.fori_loop(1, self.lons, greet_line, 0)
        return SPOTS + self.lons - 1

    def copy(self, pair, k, source, target, device):
        return pltpu.make_async_remote_copy(
            src_ref=source,
            dst_ref=target,
            send_sem=self.sems[2 * pair].at[k],
            recv_sem=self.sems[2 * pair + 1].at[k],
            device_id=device,
            device_id_type=MESH,
        )

    def core_copy(self, k):
        j = self.there(k)
        return self.copy(0, k, self.in_ref.at[1 - self.core, j], self.core_s.at[k], self.partner)

    def plane_copy(self, k):
        return self.copy(1, k, self.part_s.at[k], self.plane_s.at[k], self.spot(k))

    def line_copy(self, k, slot):
        return self.copy(2, k, self.line_s.at[slot], self.line_s.at[slot], self.neighbour(k))

    def back_copy(self, k, j):
        ref = self.out_ref.at[self.core, j]
        return self.copy(3, k, ref, ref, self.spot(k))

    def last_copy(self, k, half):
        ref = self.out_ref.at[half, self.origin(k)]
        return self.copy(4, k, ref, ref, self.partner)

    def merge(self, k):
        self.core_copy(k).wait()
        j = self.there(k)
        return self.in_ref[self.core, j].astype(F32) + self.core_s[k].astype(F32)

    def loop(self, first, last, step):
        def body(k, carry):
            step(k)
            return carry

        lax.fori_loop(first, last, body, 0)

    def start_core(self):
        for k in FAR_FIRST + [0]:
            self.core_copy(k).start()

    def start_plane(self):
        for k in FAR_FIRST:
            self.part_s[k] = self.merge(k).astype(BF16)
            self.plane_copy(k).start()

    def start_line(self):
        def add(k, total):
            self.plane_copy(k).wait()
            return total + self.plane_s[k].astype(F32)

        total = lax.fori_loop(1, SPOTS, add, self.merge(0))
        self.line_s[self.lon] = total.astype(BF16)
        for k in self.far_line:
            self.line_copy(k, self.lon).start()

    def start_back(self):
        def wait(k):
            self.line_copy(k, self.lon).wait_send()
            self.line_copy(k, lax.rem(self.lon + self.lons - k, self.lons)).wait_recv()

        self.loop(1, self.lons, wait)
        total = self.line_s[0].astype(F32)
        for n in range(1, self.lons):
            total = total + self.line_s[n].astype(F32)
        self.out_ref[self.core, self.me] = total.astype(BF16)
        self.send_back()

    def send_back(self):
        for k in FAR_FIRST:
            self.back_copy(k, self.me).start()
        self.last_copy(0, self.core).start()

    def start_last(self):
        for k in FAR_FIRST[::-1]:
            self.back_copy(k, self.origin(k)).wait_recv()
            self.last_copy(k, self.core).start()

    def finish(self):
        self.loop(1, SPOTS, lambda k: self.back_copy(k, self.me).wait_send())
        self.loop(0, SPOTS, lambda k: self.last_copy(k, self.core).wait_send())
        self.loop(0, SPOTS, lambda k: self.last_copy(k, 1 - self.core).wait_recv())


class RingSum(Sum):
    ORDER = (2, 1, 3)

    def row(self, step):
        return lax.rem(self.x + 4 + step, 4)

    def group(self, step):
        return pl.ds(self.row(step) * 4, 4)

    def x_device(self, step):
        x = self.row(step)
        return {"rep": (x // 2) * 2 + self.core, "lat": (x % 2) * 4 + self.y}

    def column(self, step):
        return lax.rem(self.y + 4 + step, 4)

    def y_device(self, step):
        return {"lat": (self.x % 2) * 4 + self.column(step)}

    def core_copy(self, dx):
        part = self.group(dx)
        source = self.in_ref.at[1 - self.core, part]
        return self.copy(0, dx, source, self.core_s.at[part], self.partner)

    def x_copy(self, dx):
        target = self.plane_s.at[pl.ds(4 * dx, 4)]
        return self.copy(1, dx, self.part_s.at[self.group(dx)], target, self.x_device(dx))

    def y_copy(self, dy):
        source = self.part_s.at[self.x * 4 + self.column(dy)]
        return self.copy(1, 4 + dy, source, self.plane_s.at[dy], self.y_device(dy))

    def y_back(self, dy, owner):
        ref = self.out_ref.at[self.core, self.x * 4 + owner]
        return self.copy(3, 4 + dy, ref, ref, self.y_device(dy))

    def x_back(self, dx, part):
        ref = self.out_ref.at[self.core, part]
        return self.copy(3, dx, ref, ref, self.x_device(dx))

    def last_group(self, dx, half):
        ref = self.out_ref.at[half, self.group(-dx)]
        return self.copy(4, dx, ref, ref, self.partner)

    def merge(self, dx):
        self.core_copy(dx).wait()
        part = self.group(dx)
        return self.in_ref[self.core, part].astype(F32) + self.core_s[part].astype(F32)

    def start_core(self):
        for dx in self.ORDER + (0,):
            self.core_copy(dx).start()

    def start_plane(self):
        for dx in self.ORDER:
            self.part_s[self.group(dx)] = self.merge(dx).astype(BF16)
            self.x_copy(dx).start()

    def start_second(self):
        total = self.merge(0)
        for dx in self.ORDER:
            self.x_copy(dx).wait()
            total = total + self.plane_s[4 * dx : 4 * dx + 4].astype(F32)
        self.part_s[self.group(0)] = total.astype(BF16)
        for dy in self.ORDER:
            self.y_copy(dy).start()

    def start_line(self):
        total = self.part_s[self.me].astype(F32)
        for dy in self.ORDER:
            self.y_copy(dy).wait()
            total = total + self.plane_s[dy].astype(F32)
        self.line_s[self.lon] = total.astype(BF16)
        for k in self.far_line:
            self.line_copy(k, self.lon).start()

    def send_back(self):
        for dy in self.ORDER:
            self.y_back(dy, self.y).start()

    def start_back_x(self):
        for dy in self.ORDER:
            self.y_back(dy, self.y).wait_send()
            self.y_back(dy, self.column(-dy)).wait_recv()
        for dx in self.ORDER:
            self.x_back(dx, self.group(0)).start()
        self.last_group(0, self.core).start()

    def start_last(self):
        for dx in self.ORDER:
            self.x_back(dx, self.group(-dx)).wait_recv()
            self.last_group(dx, self.core).start()

    def finish(self):
        for dx in self.ORDER:
            self.x_back(dx, self.group(0)).wait_send()
        for dx in (0,) + self.ORDER:
            self.last_group(dx, self.core).wait_send()
            self.last_group(dx, 1 - self.core).wait_recv()


def layer_kernel(
    lats,
    lons,
    make_sum,
    make_ring,
    tok_ref,
    cot_ref,
    gain_a,
    qkv_a,
    out_a,
    bias_a,
    gain_b,
    qkv_b,
    out_b,
    bias_b,
    route_ref,
    dtok_out,
    sum_out,
    dtok_s,
    sum_ref,
    out_sem,
    inputs_s,
    input_sem,
    scaled_s,
    room,
    save_a,
    save_b,
    grad_a,
    grad_b,
    order_s,
    slots_s,
    ahead_s,
    place_s,
    back_s,
    home_s,
    extra_s,
    x_a,
    mid_s,
    dmid_s,
    send_s,
    recv_s,
    send_sem,
    recv_sem,
    packed_s,
    parts_a,
    parts_b,
):
    lat = lax.axis_index("lat")
    lon = lax.axis_index("lon")
    save_a, save_b = (save_a, room), (save_b, room)

    def shifted(dlat, dlon):
        return {"lat": lax.rem(lat + dlat + lats, lats), "lon": lax.rem(lon + dlon + lons, lons)}

    before = [shifted(0, -1), shifted(-1, 0), shifted(-1, -1)]
    after = [shifted(0, 1), shifted(1, 0), shifted(1, 1)]

    def quarters(leg, window):
        copies = []
        for n, target in enumerate(after if leg == 2 else before):
            at = (leg, n + 1) if window is None else (leg, n + 1, window)
            sem = n if window is None else 3 + (leg - 1) * 12 + window * 3 + n
            copies.append(
                pltpu.make_async_remote_copy(
                    src_ref=send_s.at[at],
                    dst_ref=recv_s.at[at],
                    send_sem=send_sem.at[sem],
                    recv_sem=recv_sem.at[sem],
                    device_id=target,
                    device_id_type=MESH,
                )
            )
        return copies

    def post(leg, window, value):
        value = value.astype(BF16)
        recv_s[leg, 0, window] = value[:SLOT]
        for n in range(1, 4):
            send_s[leg, n, window] = value[n * SLOT : (n + 1) * SLOT]
        copies = quarters(leg, window)
        for copy in copies:
            copy.start()
        return copies

    def arrived(leg, window):
        return recv_s[leg, :, window].reshape(4 * SLOT, C)

    sources = (
        tok_ref, cot_ref, gain_a, qkv_a, out_a, bias_a, gain_b, qkv_b, out_b, bias_b, route_ref
    )
    loads = [
        pltpu.make_async_copy(source, target, input_sem.at[n])
        for n, (source, target) in enumerate(zip(sources, inputs_s))
    ]
    for n in (10, 0, 2, 3, 4, 5, 1, 6, 7, 8, 9):
        loads[n].start()
    tok_ref, cot_ref, gain_a, qkv_a, out_a, bias_a, gain_b, qkv_b, out_b, bias_b, route_ref = inputs_s

    sum_a = make_sum(lons, (packed_s.at[0], sum_ref.at[0]) + parts_a)
    sum_b = make_ring(lons, (packed_s.at[1], sum_ref.at[1]) + parts_b)

    barrier = pltpu.get_barrier_semaphore()
    for other in before + after:
        pl.semaphore_signal(barrier, inc=1, device_id=other, device_id_type=MESH)
    greeted = 6 + sum_a.greet(barrier)

    def one_hot(rows, row, columns):
        target = route_ref[row : row + 1, :columns]
        spot = lax.broadcasted_iota(jnp.int32, (rows, columns), 0)
        return jnp.where(spot == target, 1.0, 0.0).astype(BF16)

    loads[10].wait()
    loads[0].wait()
    x_a[...] = nn(one_hot(TOK, 0, TOK), tok_ref[...]).astype(BF16)
    for n in (2, 3, 4, 5):
        loads[n].wait()
    scaled_s[0] = bias_a[...] * LOG2E
    slots_s[...] = one_hot(16 * SLOT, 2, TOK)
    for n in range(2):
        ahead_s[n] = one_hot(4 * SLOT, 3 + n, 72)

    ga = gain_a[...]
    wo = out_a[...]
    wqa, wka, wva = (qkv_a[:, n * C : (n + 1) * C] for n in range(3))
    mids = [None] * WINDOWS
    backs = [None] * WINDOWS

    def send_mid(w):
        levels = (2 * w + 1, (2 * w + 2) % LEVELS)
        mids[w] = post(1, w, nn(ahead_s[0], mid_s[levels[0]]) + nn(ahead_s[1], mid_s[levels[1]]))

    for w in range(WINDOWS):
        xf, att = window_forward(w, x_a[w * WT : (w + 1) * WT, :], ga, wqa, wka, wva, scaled_s.at[0], None, save_a)
        middle = xf + nn(att, wo)
        mid_s[2 * w] = middle[:72].astype(BF16)
        mid_s[2 * w + 1] = middle[72:].astype(BF16)
        if w == 0:
            loads[1].wait()
            cots = nn(slots_s[...], cot_ref[...]).astype(BF16)
            cots = cots.reshape(4, WINDOWS, SLOT, C)
            recv_s[0, 0] = cots[0]
            for n in range(1, 4):
                send_s[0, n] = cots[n]
        if w == 1:
            pl.semaphore_wait(barrier, greeted)
            cot_copies = quarters(0, None)
            for copy in cot_copies:
                copy.start()
            send_mid(0)
    for w in range(1, WINDOWS):
        send_mid(w)

    order_s[...] = one_hot(TOK, 1, TOK)
    place_s[...] = one_hot(WT, 5, 4 * SLOT)
    back_s[...] = one_hot(4 * SLOT, 6, WT)
    for n in range(2):
        home_s[n] = one_hot(72, 7 + n, 4 * SLOT)
    for n in (6, 7, 8, 9):
        loads[n].wait()
    scaled_s[1] = bias_b[...] * LOG2E

    def label(shape, axis, level):
        at = lax.broadcasted_iota(jnp.int32, shape, axis)
        upper = jnp.where(at >= 72, 1, 0)
        inside = at - 72 * upper
        late = jnp.where(inside >= 36, 1, 0) * jnp.where(lat == lats - 1, 1, 0)
        return late + 2 * upper if level else late

    for n in range(2):
        same = label((WT, WT), 0, n) == label((WT, WT), 1, n)
        extra_s[n] = jnp.where(same, 0.0, -1e30)

    gb = gain_b[...]
    wob = out_b[...]
    wqb, wkb, wvb = (qkv_b[:, n * C : (n + 1) * C] for n in range(3))

    for copy in cot_copies:
        copy.wait()
    gs = [None] * WINDOWS

    def shifted_forward(w):
        for copy in mids[w]:
            copy.wait()
        x = nn(place_s[...], arrived(1, w)).astype(BF16)
        gs[w] = nn(place_s[...], arrived(0, w)).astype(BF16)
        extra = extra_s.at[w // (WINDOWS - 1)]
        window_forward(w, x, gb, wqb, wkb, wvb, scaled_s.at[1], extra, save_b)

    shifted_forward(0)
    for w in range(WINDOWS):
        if w + 1 < WINDOWS:
            shifted_forward(w + 1)
        d_in = window_backward(w, w == 0, gs[w], gb, wqb, wkb, wvb, wob, save_b, grad_b)
        backs[w] = post(2, w, nn(back_s[...], d_in))

    def take_back(w):
        for copy in backs[w]:
            copy.wait()
        value = arrived(2, w)
        dmid_s[2 * w + 1] = nn(home_s[0], value)
        dmid_s[(2 * w + 2) % LEVELS] = nn(home_s[1], value)

    def regular_back(w, first_one):
        g = jnp.concatenate([dmid_s[2 * w], dmid_s[2 * w + 1]], axis=0).astype(BF16)
        x_a[w * WT : (w + 1) * WT, :] = window_backward(
            w, first_one, g, ga, wqa, wka, wva, wo, save_a, grad_a
        )

    take_back(0)
    take_back(1)
    regular_back(1, True)
    pack(packed_s.at[1], grad_b)
    sum_b.start_core()
    take_back(2)
    regular_back(2, False)
    sum_b.start_plane()
    take_back(3)
    regular_back(3, False)
    regular_back(0, False)
    pack(packed_s.at[0], grad_a)
    sum_a.start_core()
    sum_a.start_plane()
    sum_b.start_second()
    dtok_s[...] = nn(order_s[...], x_a[...]).astype(BF16)
    leave = [
        pltpu.make_async_copy(dtok_s, dtok_out, out_sem.at[0]),
        pltpu.make_async_copy(sum_ref.at[1], sum_out.at[1], out_sem.at[1]),
        pltpu.make_async_copy(sum_ref.at[0], sum_out.at[0], out_sem.at[2]),
    ]
    leave[0].start()
    sum_b.start_line()
    sum_a.start_line()
    sum_b.start_back()
    sum_a.start_back()
    sum_b.start_back_x()
    sum_a.start_last()
    sum_b.start_last()
    sum_b.finish()
    leave[1].start()
    sum_a.finish()
    leave[2].start()
    for copy in leave:
        copy.wait()


def unpack_kernel(in_hbm, dtok_ref, dtok_out, *refs):
    outs, (in_ref, in_sem, held, out_sem) = refs[:8], refs[8:]
    across = pltpu.make_async_copy(dtok_ref, dtok_out, in_sem.at[2])
    loads = []
    for block in range(2):
        part = pl.ds(block * 2 * HALF, 2 * HALF)
        loads.append(pltpu.make_async_copy(in_hbm.at[part], in_ref.at[part], in_sem.at[block]))
        loads[block].start()
    across.start()
    stores = [
        pltpu.make_async_copy(source, target, out_sem.at[n])
        for n, (source, target) in enumerate(zip(held, outs))
    ]
    for block in range(2):
        gain, qkv, out, bias = held[4 * block : 4 * block + 4]
        at = block * 2 * HALF
        loads[block].wait()

        def rows(count):
            nonlocal at
            at += count
            return in_ref[at - count : at, :].astype(F32)

        gq, gk, gv, go = (rows(C) for _ in range(4))
        one, two = rows(C), rows(C)
        qkv[...] = jnp.concatenate(
            [gq, one[:, :64], gk, one[:, 64:], gv, two[:, :64]], axis=1
        )
        stores[4 * block + 1].start()
        out[...] = jnp.concatenate([go, two[:, 64:]], axis=1)
        stores[4 * block + 2].start()
        main = [rows(WT) for _ in range(HEADS)]
        tails = rows(WT)
        for h in range(HEADS):
            bias[h] = jnp.concatenate([main[h], tails[:, 16 * h : 16 * h + 16]], axis=1)
        stores[4 * block + 3].start()
        last = rows(16)
        gain[...] = jnp.concatenate([last[0:1, :], last[1:2, :64]], axis=1)
        stores[4 * block].start()
    across.wait()
    for copy in stores:
        copy.wait()


def saves():
    return (
        pltpu.VMEM((TOK, C), F32),
        pltpu.VMEM((TOK, 1), F32),
        pltpu.VMEM((TOK, C), BF16),
        pltpu.VMEM((TOK, C), BF16),
        pltpu.VMEM((TOK, C), BF16),
        pltpu.VMEM((TOK, C), BF16),
        pltpu.VMEM((WINDOWS, HEADS * WT, WT), BF16),
        pltpu.VMEM((TOK, C), BF16),
    )


def rooms():
    return (
        pltpu.VMEM((WINDOWS, HEADS * WT, WT), F32),
        pltpu.VMEM((WINDOWS, HEADS * WT, WT), BF16),
    )


def totals():
    return (
        pltpu.VMEM((C, C), F32),
        pltpu.VMEM((C, C), F32),
        pltpu.VMEM((C, C), F32),
        pltpu.VMEM((C, C), F32),
        pltpu.VMEM((HEADS, WT, WT), F32),
        pltpu.VMEM((1, C), F32),
    )


def parts(lons):
    piece = (PIECE, 128)
    return (
        (pltpu.VMEM((SPOTS,) + piece, BF16),) * 3
        + (pltpu.VMEM((lons,) + piece, BF16),)
        + (pltpu.SemaphoreType.DMA((SPOTS,)),) * 4
        + (pltpu.SemaphoreType.DMA((lons,)),) * 2
        + (pltpu.SemaphoreType.DMA((SPOTS,)),) * 4
    )


def run_layer(lats, lons, *args):
    return pl.pallas_call(
        functools.partial(layer_kernel, lats, lons, Sum, RingSum),
        out_shape=(
            jax.ShapeDtypeStruct((TOK, C), BF16),
            jax.ShapeDtypeStruct((2, 2, SPOTS, PIECE, 128), BF16),
        ),
        in_specs=[pl.BlockSpec(memory_space=pl.ANY)] * 11,
        out_specs=(pl.BlockSpec(memory_space=pl.ANY),) * 2,
        scratch_shapes=[
            pltpu.VMEM((TOK, C), BF16),
            pltpu.VMEM((2, 2, SPOTS, PIECE, 128), BF16),
            pltpu.SemaphoreType.DMA((3,)),
            tuple(pltpu.VMEM(arg.shape, arg.dtype) for arg in args),
            pltpu.SemaphoreType.DMA((11,)),
            pltpu.VMEM((2, HEADS, WT, WT), F32),
            rooms(),
            saves(),
            saves(),
            totals(),
            totals(),
            pltpu.VMEM((TOK, TOK), BF16),
            pltpu.VMEM((16 * SLOT, TOK), BF16),
            pltpu.VMEM((2, 4 * SLOT, 72), BF16),
            pltpu.VMEM((WT, 4 * SLOT), BF16),
            pltpu.VMEM((4 * SLOT, WT), BF16),
            pltpu.VMEM((2, 72, 4 * SLOT), BF16),
            pltpu.VMEM((2, WT, WT), F32),
            pltpu.VMEM((TOK, C), BF16),
            pltpu.VMEM((LEVELS, 72, C), BF16),
            pltpu.VMEM((LEVELS, 72, C), F32),
            pltpu.VMEM((3, 4, WINDOWS, SLOT, C), BF16),
            pltpu.VMEM((3, 4, WINDOWS, SLOT, C), BF16),
            pltpu.SemaphoreType.DMA((27,)),
            pltpu.SemaphoreType.DMA((27,)),
            pltpu.VMEM((2, 2, SPOTS, PIECE, 128), BF16),
            parts(lons),
            parts(lons),
        ],
        compiler_params=pltpu.CompilerParams(
            collective_id=0, has_side_effects=True, vmem_limit_bytes=VMEM_LIMIT
        ),
        name="layer",
    )(*args)


def run_unpack(summed, d_tokens):
    block = (
        jax.ShapeDtypeStruct((1, C), F32),
        jax.ShapeDtypeStruct((C, 3 * C), F32),
        jax.ShapeDtypeStruct((C, C), F32),
        jax.ShapeDtypeStruct((HEADS, WT, WT), F32),
    )
    return pl.pallas_call(
        unpack_kernel,
        out_shape=(jax.ShapeDtypeStruct((TOK, C), BF16),) + block + block,
        in_specs=[pl.BlockSpec(memory_space=pl.ANY)] * 2,
        out_specs=(pl.BlockSpec(memory_space=pl.ANY),) * 9,
        scratch_shapes=[
            pltpu.VMEM((4 * HALF, 128), BF16),
            pltpu.SemaphoreType.DMA((3,)),
            tuple(pltpu.VMEM(out.shape, out.dtype) for out in block + block),
            pltpu.SemaphoreType.DMA((8,)),
        ],
        compiler_params=pltpu.CompilerParams(vmem_limit_bytes=VMEM_LIMIT),
        name="unpack",
    )(summed, d_tokens)


def solution(mesh):
    lats, lons = mesh.shape["lat"], mesh.shape["lon"]
    route = routes()

    def stored(grid):
        return grid.transpose(0, 2, 3, 1, 4).reshape(TOK, C)

    def local(tokens, cotangent, gain_a, qkv_a, out_a, bias_a, gain_b, qkv_b, out_b, bias_b):
        d_tokens, summed = run_layer(
            lats,
            lons,
            stored(tokens),
            stored(cotangent),
            gain_a.reshape(1, C),
            qkv_a,
            out_a,
            bias_a,
            gain_b.reshape(1, C),
            qkv_b,
            out_b,
            bias_b,
            jnp.asarray(route),
        )
        d_tokens, ga, qa, oa, ba, gb, qb, ob, bb = run_unpack(
            summed.reshape(4 * HALF, 128), d_tokens
        )
        d_tokens = d_tokens.reshape(1, 6, 12, LEVELS, C).transpose(0, 3, 1, 2, 4)
        return (
            d_tokens,
            ga.reshape(C),
            qa,
            oa,
            ba,
            gb.reshape(C),
            qb,
            ob,
            bb,
        )

    grid = P("rep", None, "lat", "lon", None)
    return jax.shard_map(
        local,
        mesh=mesh,
        in_specs=(grid, grid) + (P(),) * 8,
        out_specs=(grid,) + (P(),) * 8,
        check_vma=False,
    )
```

```python
import functools

import jax
import jax.numpy as jnp
import numpy as np
from jax import lax
from jax.experimental import pallas as pl
from jax.experimental.pallas import tpu as pltpu
from jax.sharding import PartitionSpec as P

MESH = pl.DeviceIdType.MESH
C = 192
HEADS = 6
HEAD = 32
WT = 144
LEVELS = 8
WINDOWS = 4
TOK = WT * WINDOWS
FACTOR = HEAD ** (-0.5)
F32 = jnp.float32
BF16 = jnp.bfloat16
PIECE = 80
SPOTS = 16
HALF = PIECE * SPOTS
STEP = 144
GROUPS = ((0, 4, 0, 128), (4, 6, 128, 192))
LOG2E = 1.4426950408889634
SLOT = 48
VMEM_LIMIT = 56 * 1024 * 1024
UNPACK_LIMIT = 16 * 1024 * 1024


def nt(left, right):
    return lax.dot_general(left, right, (((1,), (1,)), ((), ())), preferred_element_type=F32)


def tn(left, right):
    return lax.dot_general(left, right, (((0,), (0,)), ((), ())), preferred_element_type=F32)


def nn(left, right):
    return lax.dot_general(left, right, (((1,), (0,)), ((), ())), preferred_element_type=F32)


def routes():
    out = np.full((16, TOK), -1, np.int32)
    for z in range(LEVELS):
        for i in range(6):
            for j in range(12):
                stored = (i * 12 + j) * LEVELS + z
                token = z * 72 + i * 12 + j
                out[0, stored] = token
                out[1, token] = stored
                zr, ir, jr = (z - 1) % LEVELS, (i + 3) % 6, (j + 6) % 12
                quarter = 2 * (ir >= 3) + (jr >= 6)
                window, level = zr // 2, zr % 2
                inside = level * 18 + (ir % 3) * 6 + jr % 6
                slot = quarter * SLOT + inside
                place = level * 72 + ir * 12 + jr
                column = i * 12 + j
                out[2, stored] = (quarter * WINDOWS + window) * SLOT + inside
                out[3 + level, column] = slot
                out[5, slot] = place
                out[6, place] = slot
                out[7 + level, slot] = column
    return out


def head_mask(h, dtype):
    lane = lax.broadcasted_iota(jnp.int32, (1, C), 1)
    return jnp.where((lane >= h * HEAD) & (lane < (h + 1) * HEAD), 1.0, 0.0).astype(dtype)


def spread(value):
    return [
        jnp.concatenate(
            [value[:, lo:hi] * head_mask(h, BF16)[:, lo:hi] for h in range(first, last)], axis=0
        )
        for first, last, lo, hi in GROUPS
    ]


def gather_heads(stacked):
    parts = []
    for group, (first, last, lo, hi) in zip(stacked, GROUPS):
        lane = lax.broadcasted_iota(jnp.int32, (1, hi - lo), 1)
        total = group[:WT]
        for n in range(1, last - first):
            total = jnp.where(lane >= n * HEAD, group[n * WT : (n + 1) * WT], total)
        parts.append(total)
    return jnp.concatenate(parts, axis=1)


def stacked_rows(first, last):
    return slice(first * WT, last * WT)


def window_forward(w, x, gain, wq, wk, wv, bias, extra, save):
    (unit_s, inv_s, normed_s, q_s, k_s, v_s, p_s, att_s), (s_s, d_s) = save
    rows = pl.ds(w * WT, WT)
    xf = x.astype(F32)
    center = xf - jnp.mean(xf, axis=-1, keepdims=True)
    inv = lax.rsqrt(jnp.mean(center * center, axis=-1, keepdims=True) + 1e-05)
    unit = center * inv
    normed = (unit * gain).astype(BF16)
    unit_s[rows, :] = unit
    inv_s[rows, :] = inv
    normed_s[rows, :] = normed
    q = (nn(normed, wq) * (FACTOR * LOG2E)).astype(BF16)
    k = nn(normed, wk).astype(BF16)
    v = nn(normed, wv).astype(BF16)
    q_s[rows, :] = q
    k_s[rows, :] = k
    v_s[rows, :] = v
    for left, (head, stop, lo, hi) in zip(spread(q), GROUPS):
        s_s[w, stacked_rows(head, stop), :] = nt(left, k[:, lo:hi])
    for at in range(0, HEADS * WT, STEP):
        h, first = at // WT, at % WT
        s = s_s[w, at : at + STEP, :] + bias[h, first : first + STEP, :]
        if extra is not None:
            s = s + extra[first : first + STEP]
        e = jnp.exp2(s - jnp.max(s, axis=-1, keepdims=True))
        p = (e * (1.0 / jnp.sum(e, axis=-1, keepdims=True))).astype(BF16)
        p_s[w, at : at + STEP, :] = p
    att = gather_heads(
        [nn(p_s[w, stacked_rows(head, stop), :], v[:, lo:hi]) for head, stop, lo, hi in GROUPS]
    ).astype(BF16)
    att_s[rows, :] = att
    return xf, att


def window_backward(w, first_one, g, gain, wq, wk, wv, wo, save, grads):
    (unit_s, inv_s, normed_s, q_s, k_s, v_s, p_s, att_s), (s_s, d_s) = save
    gq_s, gk_s, gv_s, go_s, gb_s, gg_s = grads
    rows = pl.ds(w * WT, WT)

    def add(ref, index, value):
        ref[index] = value if first_one else ref[index] + value

    add(go_s, ..., tn(att_s[rows, :], g))
    da = spread(nt(g, wo).astype(BF16))
    v = v_s[rows, :]
    k = k_s[rows, :]
    dvs = []
    for left, (head, stop, lo, hi) in zip(da, GROUPS):
        s_s[w, stacked_rows(head, stop), :] = nt(left, v[:, lo:hi])
        dvs.append(tn(p_s[w, stacked_rows(head, stop), :], left))
    dv = jnp.concatenate(dvs, axis=1).astype(BF16)
    for at in range(0, HEADS * WT, STEP):
        h, first = at // WT, at % WT
        pf = p_s[w, at : at + STEP, :].astype(F32)
        t = pf * s_s[w, at : at + STEP, :]
        ds = t - pf * jnp.sum(t, axis=-1, keepdims=True)
        add(gb_s, (h, slice(first, first + STEP), slice(None)), ds)
        d_s[w, at : at + STEP, :] = ds.astype(BF16)
    dks, dqs = [], []
    for left, (head, stop, lo, hi) in zip(spread(q_s[rows, :]), GROUPS):
        ds = d_s[w, stacked_rows(head, stop), :]
        dks.append(tn(ds, left))
        dqs.append(nn(ds, k[:, lo:hi]))
    dk = (jnp.concatenate(dks, axis=1) * (1.0 / LOG2E)).astype(BF16)
    dq = (gather_heads(dqs) * FACTOR).astype(BF16)
    normed = normed_s[rows, :]
    add(gq_s, ..., tn(normed, dq))
    add(gk_s, ..., tn(normed, dk))
    add(gv_s, ..., tn(normed, dv))
    dn = nt(dq, wq) + nt(dk, wk) + nt(dv, wv)
    unit = unit_s[rows, :]
    add(gg_s, ..., jnp.sum(dn * unit, axis=0, keepdims=True))
    dh = dn * gain
    d_in = g.astype(F32) + inv_s[rows, :] * (
        dh
        - jnp.mean(dh, axis=-1, keepdims=True)
        - unit * jnp.mean(dh * unit, axis=-1, keepdims=True)
    )
    return d_in.astype(BF16)


def pack(out, grads):
    gq_s, gk_s, gv_s, go_s, gb_s, gg_s = grads
    at = 0

    def put(value):
        nonlocal at
        value = value.astype(BF16)
        done = 0
        while done < value.shape[0]:
            piece, first = (at + done) // PIECE, (at + done) % PIECE
            count = min(PIECE - first, value.shape[0] - done)
            out[piece // SPOTS, piece % SPOTS, first : first + count, :] = value[done : done + count]
            done += count
        at += value.shape[0]

    for ref in (gq_s, gk_s, gv_s, go_s):
        put(ref[:, :128])
    for one, two in ((gq_s, gk_s), (gv_s, go_s)):
        put(jnp.concatenate([one[:, 128:], two[:, 128:]], axis=1))
    for h in range(HEADS):
        put(gb_s[h, :, :128])
    tails = [gb_s[h, :, 128:] for h in range(HEADS)] + [jnp.zeros((WT, 32), F32)]
    put(jnp.concatenate(tails, axis=1))
    gg = gg_s[...]
    second = jnp.concatenate([gg[:, 128:], jnp.zeros((1, 64), F32)], axis=1)
    put(jnp.concatenate([gg[:, :128], second, jnp.zeros((14, 128), F32)], axis=0))
    put(jnp.zeros((2 * HALF - at, 128), F32))


def ring_distance(step, count):
    return min(step, count - step)


FAR_FIRST = sorted(
    range(1, SPOTS), key=lambda k: -ring_distance(k // 4, 4) - ring_distance(k % 4, 4)
)


class Sum:
    def __init__(self, lon_count, refs):
        self.in_ref, self.out_ref, self.core_s, self.part_s, self.plane_s, self.line_s = refs[:6]
        self.sems = refs[6:]
        rep, lat = lax.axis_index("rep"), lax.axis_index("lat")
        self.lon = lax.axis_index("lon")
        self.lons = lon_count
        self.core = rep % 2
        x_hi, x_lo, y = rep // 2, lat // 4, lat % 4
        self.x, self.y = x_hi * 2 + x_lo, y
        self.me = self.x * 4 + y
        self.far_line = sorted(range(1, lon_count), key=lambda k: -ring_distance(k, lon_count))
        self.partner = {"rep": x_hi * 2 + (1 - self.core)}

    def there(self, k):
        return lax.rem(self.x + k // 4, 4) * 4 + lax.rem(self.y + k % 4, 4)

    def origin(self, k):
        return lax.rem(self.x + 4 - k // 4, 4) * 4 + lax.rem(self.y + 4 - k % 4, 4)

    def spot(self, k):
        x, y = lax.rem(self.x + k // 4, 4), lax.rem(self.y + k % 4, 4)
        return {"rep": (x // 2) * 2 + self.core, "lat": (x % 2) * 4 + y}

    def neighbour(self, k):
        return {"lon": lax.rem(self.lon + k, self.lons)}

    def greet(self, barrier):
        pl.semaphore_signal(barrier, inc=1, device_id=self.partner, device_id_type=MESH)

        def greet_plane(k, carry):
            pl.semaphore_signal(barrier, inc=1, device_id=self.spot(k), device_id_type=MESH)
            return carry

        def greet_line(k, carry):
            pl.semaphore_signal(barrier, inc=1, device_id=self.neighbour(k), device_id_type=MESH)
            return carry

        lax.fori_loop(1, SPOTS, greet_plane, 0)
        lax.fori_loop(1, self.lons, greet_line, 0)
        return SPOTS + self.lons - 1

    def copy(self, pair, k, source, target, device):
        return pltpu.make_async_remote_copy(
            src_ref=source,
            dst_ref=target,
            send_sem=self.sems[2 * pair].at[k],
            recv_sem=self.sems[2 * pair + 1].at[k],
            device_id=device,
            device_id_type=MESH,
        )

    def core_copy(self, k):
        j = self.there(k)
        return self.copy(0, k, self.in_ref.at[1 - self.core, j], self.core_s.at[k], self.partner)

    def plane_copy(self, k):
        return self.copy(1, k, self.part_s.at[k], self.plane_s.at[k], self.spot(k))

    def line_copy(self, k, slot):
        return self.copy(2, k, self.line_s.at[slot], self.line_s.at[slot], self.neighbour(k))

    def back_copy(self, k, j):
        ref = self.out_ref.at[self.core, j]
        return self.copy(3, k, ref, ref, self.spot(k))

    def last_copy(self, k, half):
        ref = self.out_ref.at[half, self.origin(k)]
        return self.copy(4, k, ref, ref, self.partner)

    def merge(self, k):
        self.core_copy(k).wait()
        j = self.there(k)
        return self.in_ref[self.core, j].astype(F32) + self.core_s[k].astype(F32)

    def loop(self, first, last, step):
        def body(k, carry):
            step(k)
            return carry

        lax.fori_loop(first, last, body, 0)

    def start_core(self):
        for k in FAR_FIRST + [0]:
            self.core_copy(k).start()

    def start_plane(self):
        for k in FAR_FIRST:
            self.part_s[k] = self.merge(k).astype(BF16)
            self.plane_copy(k).start()

    def start_line(self):
        def add(k, total):
            self.plane_copy(k).wait()
            return total + self.plane_s[k].astype(F32)

        total = lax.fori_loop(1, SPOTS, add, self.merge(0))
        self.line_s[self.lon] = total.astype(BF16)
        for k in self.far_line:
            self.line_copy(k, self.lon).start()

    def start_back(self):
        def wait(k):
            self.line_copy(k, self.lon).wait_send()
            self.line_copy(k, lax.rem(self.lon + self.lons - k, self.lons)).wait_recv()

        self.loop(1, self.lons, wait)
        total = self.line_s[0].astype(F32)
        for n in range(1, self.lons):
            total = total + self.line_s[n].astype(F32)
        self.out_ref[self.core, self.me] = total.astype(BF16)
        for k in FAR_FIRST:
            self.back_copy(k, self.me).start()
        self.last_copy(0, self.core).start()

    def start_last(self):
        for k in FAR_FIRST[::-1]:
            self.back_copy(k, self.origin(k)).wait_recv()
            self.last_copy(k, self.core).start()

    def finish(self):
        self.loop(1, SPOTS, lambda k: self.back_copy(k, self.me).wait_send())
        self.loop(0, SPOTS, lambda k: self.last_copy(k, self.core).wait_send())
        self.loop(0, SPOTS, lambda k: self.last_copy(k, 1 - self.core).wait_recv())


def layer_kernel(
    lats,
    lons,
    make_sum,
    tok_ref,
    cot_ref,
    gain_a,
    qkv_a,
    out_a,
    bias_a,
    gain_b,
    qkv_b,
    out_b,
    bias_b,
    route_ref,
    dtok_ref,
    sum_ref,
    inputs_s,
    input_sem,
    scaled_s,
    room,
    save_a,
    save_b,
    grad_a,
    grad_b,
    order_s,
    slots_s,
    ahead_s,
    place_s,
    back_s,
    home_s,
    extra_s,
    x_a,
    mid_s,
    dmid_s,
    send_s,
    recv_s,
    send_sem,
    recv_sem,
    packed_s,
    parts_a,
    parts_b,
):
    lat = lax.axis_index("lat")
    lon = lax.axis_index("lon")
    save_a, save_b = (save_a, room), (save_b, room)

    def shifted(dlat, dlon):
        return {"lat": lax.rem(lat + dlat + lats, lats), "lon": lax.rem(lon + dlon + lons, lons)}

    before = [shifted(0, -1), shifted(-1, 0), shifted(-1, -1)]
    after = [shifted(0, 1), shifted(1, 0), shifted(1, 1)]

    def quarters(leg, window):
        copies = []
        for n, target in enumerate(after if leg == 2 else before):
            at = (leg, n + 1) if window is None else (leg, n + 1, window)
            sem = n if window is None else 3 + (leg - 1) * 12 + window * 3 + n
            copies.append(
                pltpu.make_async_remote_copy(
                    src_ref=send_s.at[at],
                    dst_ref=recv_s.at[at],
                    send_sem=send_sem.at[sem],
                    recv_sem=recv_sem.at[sem],
                    device_id=target,
                    device_id_type=MESH,
                )
            )
        return copies

    def post(leg, window, value):
        value = value.astype(BF16)
        recv_s[leg, 0, window] = value[:SLOT]
        for n in range(1, 4):
            send_s[leg, n, window] = value[n * SLOT : (n + 1) * SLOT]
        copies = quarters(leg, window)
        for copy in copies:
            copy.start()
        return copies

    def arrived(leg, window):
        return recv_s[leg, :, window].reshape(4 * SLOT, C)

    sources = (
        tok_ref, cot_ref, gain_a, qkv_a, out_a, bias_a, gain_b, qkv_b, out_b, bias_b, route_ref
    )
    loads = [
        pltpu.make_async_copy(source, target, input_sem.at[n])
        for n, (source, target) in enumerate(zip(sources, inputs_s))
    ]
    for n in (10, 0, 2, 3, 4, 5, 1, 6, 7, 8, 9):
        loads[n].start()
    tok_ref, cot_ref, gain_a, qkv_a, out_a, bias_a, gain_b, qkv_b, out_b, bias_b, route_ref = inputs_s

    sum_a = make_sum(lons, (packed_s.at[0], sum_ref.at[0]) + parts_a)
    sum_b = make_sum(lons, (packed_s.at[1], sum_ref.at[1]) + parts_b)

    barrier = pltpu.get_barrier_semaphore()
    for other in before + after:
        pl.semaphore_signal(barrier, inc=1, device_id=other, device_id_type=MESH)
    greeted = 6 + sum_a.greet(barrier)

    def one_hot(rows, row, columns):
        target = route_ref[row : row + 1, :columns]
        spot = lax.broadcasted_iota(jnp.int32, (rows, columns), 0)
        return jnp.where(spot == target, 1.0, 0.0).astype(BF16)

    loads[10].wait()
    loads[0].wait()
    x_a[...] = nn(one_hot(TOK, 0, TOK), tok_ref[...]).astype(BF16)
    for n in (2, 3, 4, 5):
        loads[n].wait()
    scaled_s[0] = bias_a[...] * LOG2E
    slots_s[...] = one_hot(16 * SLOT, 2, TOK)
    for n in range(2):
        ahead_s[n] = one_hot(4 * SLOT, 3 + n, 72)

    ga = gain_a[...]
    wo = out_a[...]
    wqa, wka, wva = (qkv_a[:, n * C : (n + 1) * C] for n in range(3))
    mids = [None] * WINDOWS
    backs = [None] * WINDOWS

    def send_mid(w):
        levels = (2 * w + 1, (2 * w + 2) % LEVELS)
        mids[w] = post(1, w, nn(ahead_s[0], mid_s[levels[0]]) + nn(ahead_s[1], mid_s[levels[1]]))

    for w in range(WINDOWS):
        xf, att = window_forward(w, x_a[w * WT : (w + 1) * WT, :], ga, wqa, wka, wva, scaled_s.at[0], None, save_a)
        middle = xf + nn(att, wo)
        mid_s[2 * w] = middle[:72].astype(BF16)
        mid_s[2 * w + 1] = middle[72:].astype(BF16)
        if w == 0:
            loads[1].wait()
            cots = nn(slots_s[...], cot_ref[...]).astype(BF16)
            cots = cots.reshape(4, WINDOWS, SLOT, C)
            recv_s[0, 0] = cots[0]
            for n in range(1, 4):
                send_s[0, n] = cots[n]
        else:
            if w == 1:
                pl.semaphore_wait(barrier, greeted)
                cot_copies = quarters(0, None)
                for copy in cot_copies:
                    copy.start()
            send_mid(w - 1)
    send_mid(WINDOWS - 1)

    order_s[...] = one_hot(TOK, 1, TOK)
    place_s[...] = one_hot(WT, 5, 4 * SLOT)
    back_s[...] = one_hot(4 * SLOT, 6, WT)
    for n in range(2):
        home_s[n] = one_hot(72, 7 + n, 4 * SLOT)
    for n in (6, 7, 8, 9):
        loads[n].wait()
    scaled_s[1] = bias_b[...] * LOG2E

    def label(shape, axis, level):
        at = lax.broadcasted_iota(jnp.int32, shape, axis)
        upper = jnp.where(at >= 72, 1, 0)
        inside = at - 72 * upper
        late = jnp.where(inside >= 36, 1, 0) * jnp.where(lat == lats - 1, 1, 0)
        return late + 2 * upper if level else late

    for n in range(2):
        same = label((WT, WT), 0, n) == label((WT, WT), 1, n)
        extra_s[n] = jnp.where(same, 0.0, -1e30)

    gb = gain_b[...]
    wob = out_b[...]
    wqb, wkb, wvb = (qkv_b[:, n * C : (n + 1) * C] for n in range(3))

    for copy in cot_copies:
        copy.wait()
    gs = [None] * WINDOWS

    def shifted_forward(w):
        for copy in mids[w]:
            copy.wait()
        x = nn(place_s[...], arrived(1, w)).astype(BF16)
        gs[w] = nn(place_s[...], arrived(0, w)).astype(BF16)
        extra = extra_s.at[w // (WINDOWS - 1)]
        window_forward(w, x, gb, wqb, wkb, wvb, scaled_s.at[1], extra, save_b)

    shifted_forward(0)
    for w in range(WINDOWS):
        if w + 1 < WINDOWS:
            shifted_forward(w + 1)
        d_in = window_backward(w, w == 0, gs[w], gb, wqb, wkb, wvb, wob, save_b, grad_b)
        backs[w] = post(2, w, nn(back_s[...], d_in))

    pack(packed_s.at[1], grad_b)
    sum_b.start_core()

    def take_back(w):
        for copy in backs[w]:
            copy.wait()
        value = arrived(2, w)
        dmid_s[2 * w + 1] = nn(home_s[0], value)
        dmid_s[(2 * w + 2) % LEVELS] = nn(home_s[1], value)

    def regular_back(w, first_one):
        g = jnp.concatenate([dmid_s[2 * w], dmid_s[2 * w + 1]], axis=0).astype(BF16)
        x_a[w * WT : (w + 1) * WT, :] = window_backward(
            w, first_one, g, ga, wqa, wka, wva, wo, save_a, grad_a
        )

    take_back(0)
    take_back(1)
    regular_back(1, True)
    sum_b.start_plane()
    take_back(2)
    regular_back(2, False)
    take_back(3)
    regular_back(3, False)
    regular_back(0, False)
    pack(packed_s.at[0], grad_a)
    sum_a.start_core()
    sum_a.start_plane()
    dtok_ref[...] = nn(order_s[...], x_a[...]).astype(BF16)
    sum_b.start_line()
    sum_b.start_back()
    sum_a.start_line()
    sum_b.start_last()
    sum_a.start_back()
    sum_a.start_last()
    sum_b.finish()
    sum_a.finish()


def unpack_kernel(in_ref, dtok_ref, dtok_out, *outs):
    dtok_out[...] = dtok_ref[...]
    for block in range(2):
        gain, qkv, out, bias = outs[4 * block : 4 * block + 4]
        at = block * 2 * HALF

        def rows(count):
            nonlocal at
            at += count
            return in_ref[at - count : at, :].astype(F32)

        gq, gk, gv, go = (rows(C) for _ in range(4))
        one, two = rows(C), rows(C)
        qkv[...] = jnp.concatenate(
            [gq, one[:, :64], gk, one[:, 64:], gv, two[:, :64]], axis=1
        )
        out[...] = jnp.concatenate([go, two[:, 64:]], axis=1)
        main = [rows(WT) for _ in range(HEADS)]
        tails = rows(WT)
        for h in range(HEADS):
            bias[h] = jnp.concatenate([main[h], tails[:, 16 * h : 16 * h + 16]], axis=1)
        last = rows(16)
        gain[...] = jnp.concatenate([last[0:1, :], last[1:2, :64]], axis=1)


def saves():
    return (
        pltpu.VMEM((TOK, C), F32),
        pltpu.VMEM((TOK, 1), F32),
        pltpu.VMEM((TOK, C), BF16),
        pltpu.VMEM((TOK, C), BF16),
        pltpu.VMEM((TOK, C), BF16),
        pltpu.VMEM((TOK, C), BF16),
        pltpu.VMEM((WINDOWS, HEADS * WT, WT), BF16),
        pltpu.VMEM((TOK, C), BF16),
    )


def rooms():
    return (
        pltpu.VMEM((WINDOWS, HEADS * WT, WT), F32),
        pltpu.VMEM((WINDOWS, HEADS * WT, WT), BF16),
    )


def totals():
    return (
        pltpu.VMEM((C, C), F32),
        pltpu.VMEM((C, C), F32),
        pltpu.VMEM((C, C), F32),
        pltpu.VMEM((C, C), F32),
        pltpu.VMEM((HEADS, WT, WT), F32),
        pltpu.VMEM((1, C), F32),
    )


def parts(lons):
    piece = (PIECE, 128)
    return (
        (pltpu.VMEM((SPOTS,) + piece, BF16),) * 3
        + (pltpu.VMEM((lons,) + piece, BF16),)
        + (pltpu.SemaphoreType.DMA((SPOTS,)),) * 4
        + (pltpu.SemaphoreType.DMA((lons,)),) * 2
        + (pltpu.SemaphoreType.DMA((SPOTS,)),) * 4
    )


def run_layer(lats, lons, *args):
    return pl.pallas_call(
        functools.partial(layer_kernel, lats, lons, Sum),
        out_shape=(
            pltpu.VMEM((TOK, C), BF16),
            pltpu.VMEM((2, 2, SPOTS, PIECE, 128), BF16),
        ),
        in_specs=[pl.BlockSpec(memory_space=pl.ANY)] * 11,
        out_specs=(pl.BlockSpec(memory_space=pltpu.VMEM),) * 2,
        scratch_shapes=[
            tuple(pltpu.VMEM(arg.shape, arg.dtype) for arg in args),
            pltpu.SemaphoreType.DMA((11,)),
            pltpu.VMEM((2, HEADS, WT, WT), F32),
            rooms(),
            saves(),
            saves(),
            totals(),
            totals(),
            pltpu.VMEM((TOK, TOK), BF16),
            pltpu.VMEM((16 * SLOT, TOK), BF16),
            pltpu.VMEM((2, 4 * SLOT, 72), BF16),
            pltpu.VMEM((WT, 4 * SLOT), BF16),
            pltpu.VMEM((4 * SLOT, WT), BF16),
            pltpu.VMEM((2, 72, 4 * SLOT), BF16),
            pltpu.VMEM((2, WT, WT), F32),
            pltpu.VMEM((TOK, C), BF16),
            pltpu.VMEM((LEVELS, 72, C), BF16),
            pltpu.VMEM((LEVELS, 72, C), F32),
            pltpu.VMEM((3, 4, WINDOWS, SLOT, C), BF16),
            pltpu.VMEM((3, 4, WINDOWS, SLOT, C), BF16),
            pltpu.SemaphoreType.DMA((27,)),
            pltpu.SemaphoreType.DMA((27,)),
            pltpu.VMEM((2, 2, SPOTS, PIECE, 128), BF16),
            parts(lons),
            parts(lons),
        ],
        compiler_params=pltpu.CompilerParams(
            collective_id=0, has_side_effects=True, vmem_limit_bytes=VMEM_LIMIT
        ),
        name="layer",
    )(*args)


def run_unpack(summed, d_tokens):
    block = (
        jax.ShapeDtypeStruct((1, C), F32),
        jax.ShapeDtypeStruct((C, 3 * C), F32),
        jax.ShapeDtypeStruct((C, C), F32),
        jax.ShapeDtypeStruct((HEADS, WT, WT), F32),
    )
    return pl.pallas_call(
        unpack_kernel,
        out_shape=(jax.ShapeDtypeStruct((TOK, C), BF16),) + block + block,
        in_specs=[pl.BlockSpec(memory_space=pltpu.VMEM)] * 2,
        out_specs=(pl.BlockSpec(memory_space=pltpu.VMEM),) * 9,
        compiler_params=pltpu.CompilerParams(vmem_limit_bytes=UNPACK_LIMIT),
        name="unpack",
    )(summed, d_tokens)


def solution(mesh):
    lats, lons = mesh.shape["lat"], mesh.shape["lon"]
    route = routes()

    def stored(grid):
        return grid.transpose(0, 2, 3, 1, 4).reshape(TOK, C)

    def local(tokens, cotangent, gain_a, qkv_a, out_a, bias_a, gain_b, qkv_b, out_b, bias_b):
        d_tokens, summed = run_layer(
            lats,
            lons,
            stored(tokens),
            stored(cotangent),
            gain_a.reshape(1, C),
            qkv_a,
            out_a,
            bias_a,
            gain_b.reshape(1, C),
            qkv_b,
            out_b,
            bias_b,
            jnp.asarray(route),
        )
        d_tokens, ga, qa, oa, ba, gb, qb, ob, bb = run_unpack(
            summed.reshape(4 * HALF, 128), d_tokens
        )
        d_tokens = d_tokens.reshape(1, 6, 12, LEVELS, C).transpose(0, 3, 1, 2, 4)
        return (
            d_tokens,
            ga.reshape(C),
            qa,
            oa,
            ba,
            gb.reshape(C),
            qb,
            ob,
            bb,
        )

    grid = P("rep", None, "lat", "lon", None)
    return jax.shard_map(
        local,
        mesh=mesh,
        in_specs=(grid, grid) + (P(),) * 8,
        out_specs=(grid,) + (P(),) * 8,
        check_vma=False,
    )
```

```python
import functools

import jax
import jax.numpy as jnp
import numpy as np
from jax import lax
from jax.experimental import pallas as pl
from jax.experimental.pallas import tpu as pltpu
from jax.sharding import PartitionSpec as P

MESH = pl.DeviceIdType.MESH
C = 192
HEADS = 6
HEAD = 32
WT = 144
LEVELS = 8
WINDOWS = 4
TOK = WT * WINDOWS
FACTOR = HEAD ** (-0.5)
F32 = jnp.float32
BF16 = jnp.bfloat16
PIECE = 80
SPOTS = 16
HALF = PIECE * SPOTS
STEP = 144
GROUPS = ((0, 4, 0, 128), (4, 6, 128, 192))
LOG2E = 1.4426950408889634
SLOT = 48
VMEM_LIMIT = 56 * 1024 * 1024
UNPACK_LIMIT = 16 * 1024 * 1024


def nt(left, right):
    return lax.dot_general(left, right, (((1,), (1,)), ((), ())), preferred_element_type=F32)


def tn(left, right):
    return lax.dot_general(left, right, (((0,), (0,)), ((), ())), preferred_element_type=F32)


def nn(left, right):
    return lax.dot_general(left, right, (((1,), (0,)), ((), ())), preferred_element_type=F32)


def routes():
    out = np.full((16, TOK), -1, np.int32)
    for z in range(LEVELS):
        for i in range(6):
            for j in range(12):
                stored = (i * 12 + j) * LEVELS + z
                token = z * 72 + i * 12 + j
                out[0, stored] = token
                out[1, token] = stored
                zr, ir, jr = (z - 1) % LEVELS, (i + 3) % 6, (j + 6) % 12
                quarter = 2 * (ir >= 3) + (jr >= 6)
                window, level = zr // 2, zr % 2
                inside = level * 18 + (ir % 3) * 6 + jr % 6
                slot = quarter * SLOT + inside
                place = level * 72 + ir * 12 + jr
                column = i * 12 + j
                out[2, stored] = (quarter * WINDOWS + window) * SLOT + inside
                out[3 + level, column] = slot
                out[5, slot] = place
                out[6, place] = slot
                out[7 + level, slot] = column
    return out


def head_mask(h, dtype):
    lane = lax.broadcasted_iota(jnp.int32, (1, C), 1)
    return jnp.where((lane >= h * HEAD) & (lane < (h + 1) * HEAD), 1.0, 0.0).astype(dtype)


def spread(value):
    return [
        jnp.concatenate(
            [value[:, lo:hi] * head_mask(h, BF16)[:, lo:hi] for h in range(first, last)], axis=0
        )
        for first, last, lo, hi in GROUPS
    ]


def gather_heads(stacked):
    parts = []
    for group, (first, last, lo, hi) in zip(stacked, GROUPS):
        lane = lax.broadcasted_iota(jnp.int32, (1, hi - lo), 1)
        total = group[:WT]
        for n in range(1, last - first):
            total = jnp.where(lane >= n * HEAD, group[n * WT : (n + 1) * WT], total)
        parts.append(total)
    return jnp.concatenate(parts, axis=1)


def stacked_rows(first, last):
    return slice(first * WT, last * WT)


def window_forward(w, x, gain, wq, wk, wv, bias, extra, save):
    (unit_s, inv_s, normed_s, q_s, k_s, v_s, p_s, att_s), (s_s, d_s) = save
    rows = pl.ds(w * WT, WT)
    xf = x.astype(F32)
    center = xf - jnp.mean(xf, axis=-1, keepdims=True)
    inv = lax.rsqrt(jnp.mean(center * center, axis=-1, keepdims=True) + 1e-05)
    unit = center * inv
    normed = (unit * gain).astype(BF16)
    unit_s[rows, :] = unit
    inv_s[rows, :] = inv
    normed_s[rows, :] = normed
    q = (nn(normed, wq) * (FACTOR * LOG2E)).astype(BF16)
    k = nn(normed, wk).astype(BF16)
    v = nn(normed, wv).astype(BF16)
    q_s[rows, :] = q
    k_s[rows, :] = k
    v_s[rows, :] = v
    for left, (head, stop, lo, hi) in zip(spread(q), GROUPS):
        s_s[w, stacked_rows(head, stop), :] = nt(left, k[:, lo:hi])
    for at in range(0, HEADS * WT, STEP):
        h, first = at // WT, at % WT
        s = s_s[w, at : at + STEP, :] + bias[h, first : first + STEP, :]
        if extra is not None:
            s = s + extra[first : first + STEP]
        e = jnp.exp2(s - jnp.max(s, axis=-1, keepdims=True))
        p = (e * (1.0 / jnp.sum(e, axis=-1, keepdims=True))).astype(BF16)
        p_s[w, at : at + STEP, :] = p
    att = gather_heads(
        [nn(p_s[w, stacked_rows(head, stop), :], v[:, lo:hi]) for head, stop, lo, hi in GROUPS]
    ).astype(BF16)
    att_s[rows, :] = att
    return xf, att


def window_backward(w, first_one, g, gain, wq, wk, wv, wo, save, grads):
    (unit_s, inv_s, normed_s, q_s, k_s, v_s, p_s, att_s), (s_s, d_s) = save
    gq_s, gk_s, gv_s, go_s, gb_s, gg_s = grads
    rows = pl.ds(w * WT, WT)

    def add(ref, index, value):
        ref[index] = value if first_one else ref[index] + value

    add(go_s, ..., tn(att_s[rows, :], g))
    da = spread(nt(g, wo).astype(BF16))
    v = v_s[rows, :]
    k = k_s[rows, :]
    dvs = []
    for left, (head, stop, lo, hi) in zip(da, GROUPS):
        s_s[w, stacked_rows(head, stop), :] = nt(left, v[:, lo:hi])
        dvs.append(tn(p_s[w, stacked_rows(head, stop), :], left))
    dv = jnp.concatenate(dvs, axis=1).astype(BF16)
    for at in range(0, HEADS * WT, STEP):
        h, first = at // WT, at % WT
        pf = p_s[w, at : at + STEP, :].astype(F32)
        t = pf * s_s[w, at : at + STEP, :]
        ds = t - pf * jnp.sum(t, axis=-1, keepdims=True)
        add(gb_s, (h, slice(first, first + STEP), slice(None)), ds)
        d_s[w, at : at + STEP, :] = ds.astype(BF16)
    dks, dqs = [], []
    for left, (head, stop, lo, hi) in zip(spread(q_s[rows, :]), GROUPS):
        ds = d_s[w, stacked_rows(head, stop), :]
        dks.append(tn(ds, left))
        dqs.append(nn(ds, k[:, lo:hi]))
    dk = (jnp.concatenate(dks, axis=1) * (1.0 / LOG2E)).astype(BF16)
    dq = (gather_heads(dqs) * FACTOR).astype(BF16)
    normed = normed_s[rows, :]
    add(gq_s, ..., tn(normed, dq))
    add(gk_s, ..., tn(normed, dk))
    add(gv_s, ..., tn(normed, dv))
    dn = nt(dq, wq) + nt(dk, wk) + nt(dv, wv)
    unit = unit_s[rows, :]
    add(gg_s, ..., jnp.sum(dn * unit, axis=0, keepdims=True))
    dh = dn * gain
    d_in = g.astype(F32) + inv_s[rows, :] * (
        dh
        - jnp.mean(dh, axis=-1, keepdims=True)
        - unit * jnp.mean(dh * unit, axis=-1, keepdims=True)
    )
    return d_in.astype(BF16)


def pack(out, grads):
    gq_s, gk_s, gv_s, go_s, gb_s, gg_s = grads
    at = 0

    def put(value):
        nonlocal at
        value = value.astype(BF16)
        done = 0
        while done < value.shape[0]:
            piece, first = (at + done) // PIECE, (at + done) % PIECE
            count = min(PIECE - first, value.shape[0] - done)
            out[piece // SPOTS, piece % SPOTS, first : first + count, :] = value[done : done + count]
            done += count
        at += value.shape[0]

    for ref in (gq_s, gk_s, gv_s, go_s):
        put(ref[:, :128])
    for one, two in ((gq_s, gk_s), (gv_s, go_s)):
        put(jnp.concatenate([one[:, 128:], two[:, 128:]], axis=1))
    for h in range(HEADS):
        put(gb_s[h, :, :128])
    tails = [gb_s[h, :, 128:] for h in range(HEADS)] + [jnp.zeros((WT, 32), F32)]
    put(jnp.concatenate(tails, axis=1))
    gg = gg_s[...]
    second = jnp.concatenate([gg[:, 128:], jnp.zeros((1, 64), F32)], axis=1)
    put(jnp.concatenate([gg[:, :128], second, jnp.zeros((14, 128), F32)], axis=0))
    put(jnp.zeros((2 * HALF - at, 128), F32))


def ring_distance(step, count):
    return min(step, count - step)


FAR_FIRST = sorted(
    range(1, SPOTS), key=lambda k: -ring_distance(k // 4, 4) - ring_distance(k % 4, 4)
)


class Sum:
    def __init__(self, lon_count, refs):
        self.in_ref, self.out_ref, self.core_s, self.part_s, self.plane_s, self.line_s = refs[:6]
        self.sems = refs[6:]
        rep, lat = lax.axis_index("rep"), lax.axis_index("lat")
        self.lon = lax.axis_index("lon")
        self.lons = lon_count
        self.core = rep % 2
        x_hi, x_lo, y = rep // 2, lat // 4, lat % 4
        self.x, self.y = x_hi * 2 + x_lo, y
        self.me = self.x * 4 + y
        self.far_line = sorted(range(1, lon_count), key=lambda k: -ring_distance(k, lon_count))
        self.partner = {"rep": x_hi * 2 + (1 - self.core)}

    def there(self, k):
        return lax.rem(self.x + k // 4, 4) * 4 + lax.rem(self.y + k % 4, 4)

    def origin(self, k):
        return lax.rem(self.x + 4 - k // 4, 4) * 4 + lax.rem(self.y + 4 - k % 4, 4)

    def spot(self, k):
        x, y = lax.rem(self.x + k // 4, 4), lax.rem(self.y + k % 4, 4)
        return {"rep": (x // 2) * 2 + self.core, "lat": (x % 2) * 4 + y}

    def neighbour(self, k):
        return {"lon": lax.rem(self.lon + k, self.lons)}

    def greet(self, barrier):
        pl.semaphore_signal(barrier, inc=1, device_id=self.partner, device_id_type=MESH)

        def greet_plane(k, carry):
            pl.semaphore_signal(barrier, inc=1, device_id=self.spot(k), device_id_type=MESH)
            return carry

        def greet_line(k, carry):
            pl.semaphore_signal(barrier, inc=1, device_id=self.neighbour(k), device_id_type=MESH)
            return carry

        lax.fori_loop(1, SPOTS, greet_plane, 0)
        lax.fori_loop(1, self.lons, greet_line, 0)
        return SPOTS + self.lons - 1

    def copy(self, pair, k, source, target, device):
        return pltpu.make_async_remote_copy(
            src_ref=source,
            dst_ref=target,
            send_sem=self.sems[2 * pair].at[k],
            recv_sem=self.sems[2 * pair + 1].at[k],
            device_id=device,
            device_id_type=MESH,
        )

    def group(self, dx):
        return pl.ds(lax.rem(self.x + 4 + dx, 4) * 4, 4)

    def core_copy(self, dx):
        part = self.group(dx)
        source = self.in_ref.at[1 - self.core, part]
        return self.copy(0, dx, source, self.core_s.at[part], self.partner)

    def plane_copy(self, k):
        return self.copy(1, k, self.part_s.at[k], self.plane_s.at[k], self.spot(k))

    def line_copy(self, k, slot):
        return self.copy(2, k, self.line_s.at[slot], self.line_s.at[slot], self.neighbour(k))

    def back_copy(self, k, j):
        ref = self.out_ref.at[self.core, j]
        return self.copy(3, k, ref, ref, self.spot(k))

    def last_copy(self, dx, half):
        ref = self.out_ref.at[half, self.group(-dx)]
        return self.copy(4, dx, ref, ref, self.partner)

    def merge(self, k):
        j = self.there(k)
        return self.in_ref[self.core, j].astype(F32) + self.core_s[j].astype(F32)

    def loop(self, first, last, step):
        def body(k, carry):
            step(k)
            return carry

        lax.fori_loop(first, last, body, 0)

    def start_core(self):
        for dx in (2, 1, 3, 0):
            self.core_copy(dx).start()

    def start_plane(self):
        for dx in (2, 1, 3, 0):
            self.core_copy(dx).wait()
            for dy in (2, 1, 3, 0):
                k = dx * 4 + dy
                if k:
                    self.part_s[k] = self.merge(k).astype(BF16)
                    self.plane_copy(k).start()

    def start_line(self):
        def add(k, total):
            self.plane_copy(k).wait()
            return total + self.plane_s[k].astype(F32)

        total = lax.fori_loop(1, SPOTS, add, self.merge(0))
        self.line_s[self.lon] = total.astype(BF16)
        for k in self.far_line:
            self.line_copy(k, self.lon).start()

    def start_back(self):
        def wait(k):
            self.line_copy(k, self.lon).wait_send()
            self.line_copy(k, lax.rem(self.lon + self.lons - k, self.lons)).wait_recv()

        self.loop(1, self.lons, wait)
        total = self.line_s[0].astype(F32)
        for n in range(1, self.lons):
            total = total + self.line_s[n].astype(F32)
        self.out_ref[self.core, self.me] = total.astype(BF16)
        for k in FAR_FIRST:
            self.back_copy(k, self.me).start()

    def start_last(self):
        for dx in (0, 1, 3, 2):
            for dy in (0, 1, 3, 2):
                k = dx * 4 + dy
                if k:
                    self.back_copy(k, self.origin(k)).wait_recv()
            self.last_copy(dx, self.core).start()

    def finish(self):
        self.loop(1, SPOTS, lambda k: self.back_copy(k, self.me).wait_send())
        for dx in range(4):
            self.last_copy(dx, self.core).wait_send()
            self.last_copy(dx, 1 - self.core).wait_recv()


def layer_kernel(
    lats,
    lons,
    make_sum,
    tok_ref,
    cot_ref,
    gain_a,
    qkv_a,
    out_a,
    bias_a,
    gain_b,
    qkv_b,
    out_b,
    bias_b,
    route_ref,
    dtok_ref,
    sum_ref,
    inputs_s,
    input_sem,
    scaled_s,
    room,
    save_a,
    save_b,
    grad_a,
    grad_b,
    order_s,
    slots_s,
    ahead_s,
    place_s,
    back_s,
    home_s,
    extra_s,
    x_a,
    mid_s,
    dmid_s,
    send_s,
    recv_s,
    send_sem,
    recv_sem,
    packed_s,
    parts_a,
    parts_b,
):
    lat = lax.axis_index("lat")
    lon = lax.axis_index("lon")
    save_a, save_b = (save_a, room), (save_b, room)

    def shifted(dlat, dlon):
        return {"lat": lax.rem(lat + dlat + lats, lats), "lon": lax.rem(lon + dlon + lons, lons)}

    before = [shifted(0, -1), shifted(-1, 0), shifted(-1, -1)]
    after = [shifted(0, 1), shifted(1, 0), shifted(1, 1)]

    def quarters(leg, window):
        copies = []
        for n, target in enumerate(after if leg == 2 else before):
            at = (leg, n + 1) if window is None else (leg, n + 1, window)
            sem = n if window is None else 3 + (leg - 1) * 12 + window * 3 + n
            copies.append(
                pltpu.make_async_remote_copy(
                    src_ref=send_s.at[at],
                    dst_ref=recv_s.at[at],
                    send_sem=send_sem.at[sem],
                    recv_sem=recv_sem.at[sem],
                    device_id=target,
                    device_id_type=MESH,
                )
            )
        return copies

    def post(leg, window, value):
        value = value.astype(BF16)
        recv_s[leg, 0, window] = value[:SLOT]
        for n in range(1, 4):
            send_s[leg, n, window] = value[n * SLOT : (n + 1) * SLOT]
        copies = quarters(leg, window)
        for copy in copies:
            copy.start()
        return copies

    def arrived(leg, window):
        return recv_s[leg, :, window].reshape(4 * SLOT, C)

    sources = (
        tok_ref, cot_ref, gain_a, qkv_a, out_a, bias_a, gain_b, qkv_b, out_b, bias_b, route_ref
    )
    loads = [
        pltpu.make_async_copy(source, target, input_sem.at[n])
        for n, (source, target) in enumerate(zip(sources, inputs_s))
    ]
    for n in (10, 0, 2, 3, 4, 5, 1, 6, 7, 8, 9):
        loads[n].start()
    tok_ref, cot_ref, gain_a, qkv_a, out_a, bias_a, gain_b, qkv_b, out_b, bias_b, route_ref = inputs_s

    sum_a = make_sum(lons, (packed_s.at[0], sum_ref.at[0]) + parts_a)
    sum_b = make_sum(lons, (packed_s.at[1], sum_ref.at[1]) + parts_b)

    barrier = pltpu.get_barrier_semaphore()
    for other in before + after:
        pl.semaphore_signal(barrier, inc=1, device_id=other, device_id_type=MESH)
    greeted = 6 + sum_a.greet(barrier)

    def one_hot(rows, row, columns):
        target = route_ref[row : row + 1, :columns]
        spot = lax.broadcasted_iota(jnp.int32, (rows, columns), 0)
        return jnp.where(spot == target, 1.0, 0.0).astype(BF16)

    loads[10].wait()
    loads[0].wait()
    x_a[...] = nn(one_hot(TOK, 0, TOK), tok_ref[...]).astype(BF16)
    for n in (2, 3, 4, 5):
        loads[n].wait()
    scaled_s[0] = bias_a[...] * LOG2E
    slots_s[...] = one_hot(16 * SLOT, 2, TOK)
    for n in range(2):
        ahead_s[n] = one_hot(4 * SLOT, 3 + n, 72)

    ga = gain_a[...]
    wo = out_a[...]
    wqa, wka, wva = (qkv_a[:, n * C : (n + 1) * C] for n in range(3))
    mids = [None] * WINDOWS
    backs = [None] * WINDOWS

    def send_mid(w):
        levels = (2 * w + 1, (2 * w + 2) % LEVELS)
        mids[w] = post(1, w, nn(ahead_s[0], mid_s[levels[0]]) + nn(ahead_s[1], mid_s[levels[1]]))

    for w in range(WINDOWS):
        xf, att = window_forward(w, x_a[w * WT : (w + 1) * WT, :], ga, wqa, wka, wva, scaled_s.at[0], None, save_a)
        middle = xf + nn(att, wo)
        mid_s[2 * w] = middle[:72].astype(BF16)
        mid_s[2 * w + 1] = middle[72:].astype(BF16)
        if w == 0:
            loads[1].wait()
            cots = nn(slots_s[...], cot_ref[...]).astype(BF16)
            cots = cots.reshape(4, WINDOWS, SLOT, C)
            recv_s[0, 0] = cots[0]
            for n in range(1, 4):
                send_s[0, n] = cots[n]
        else:
            if w == 1:
                pl.semaphore_wait(barrier, greeted)
                cot_copies = quarters(0, None)
                for copy in cot_copies:
                    copy.start()
            send_mid(w - 1)
    send_mid(WINDOWS - 1)

    order_s[...] = one_hot(TOK, 1, TOK)
    place_s[...] = one_hot(WT, 5, 4 * SLOT)
    back_s[...] = one_hot(4 * SLOT, 6, WT)
    for n in range(2):
        home_s[n] = one_hot(72, 7 + n, 4 * SLOT)
    for n in (6, 7, 8, 9):
        loads[n].wait()
    scaled_s[1] = bias_b[...] * LOG2E

    def label(shape, axis, level):
        at = lax.broadcasted_iota(jnp.int32, shape, axis)
        upper = jnp.where(at >= 72, 1, 0)
        inside = at - 72 * upper
        late = jnp.where(inside >= 36, 1, 0) * jnp.where(lat == lats - 1, 1, 0)
        return late + 2 * upper if level else late

    for n in range(2):
        same = label((WT, WT), 0, n) == label((WT, WT), 1, n)
        extra_s[n] = jnp.where(same, 0.0, -1e30)

    gb = gain_b[...]
    wob = out_b[...]
    wqb, wkb, wvb = (qkv_b[:, n * C : (n + 1) * C] for n in range(3))

    for copy in cot_copies:
        copy.wait()
    gs = [None] * WINDOWS

    def shifted_forward(w):
        for copy in mids[w]:
            copy.wait()
        x = nn(place_s[...], arrived(1, w)).astype(BF16)
        gs[w] = nn(place_s[...], arrived(0, w)).astype(BF16)
        extra = extra_s.at[w // (WINDOWS - 1)]
        window_forward(w, x, gb, wqb, wkb, wvb, scaled_s.at[1], extra, save_b)

    shifted_forward(0)
    for w in range(WINDOWS):
        if w + 1 < WINDOWS:
            shifted_forward(w + 1)
        d_in = window_backward(w, w == 0, gs[w], gb, wqb, wkb, wvb, wob, save_b, grad_b)
        backs[w] = post(2, w, nn(back_s[...], d_in))

    pack(packed_s.at[1], grad_b)
    sum_b.start_core()

    def take_back(w):
        for copy in backs[w]:
            copy.wait()
        value = arrived(2, w)
        dmid_s[2 * w + 1] = nn(home_s[0], value)
        dmid_s[(2 * w + 2) % LEVELS] = nn(home_s[1], value)

    def regular_back(w, first_one):
        g = jnp.concatenate([dmid_s[2 * w], dmid_s[2 * w + 1]], axis=0).astype(BF16)
        x_a[w * WT : (w + 1) * WT, :] = window_backward(
            w, first_one, g, ga, wqa, wka, wva, wo, save_a, grad_a
        )

    take_back(0)
    take_back(1)
    regular_back(1, True)
    sum_b.start_plane()
    take_back(2)
    regular_back(2, False)
    take_back(3)
    regular_back(3, False)
    regular_back(0, False)
    pack(packed_s.at[0], grad_a)
    sum_a.start_core()
    sum_a.start_plane()
    dtok_ref[...] = nn(order_s[...], x_a[...]).astype(BF16)
    sum_b.start_line()
    sum_b.start_back()
    sum_a.start_line()
    sum_b.start_last()
    sum_a.start_back()
    sum_a.start_last()
    sum_b.finish()
    sum_a.finish()


def unpack_kernel(in_ref, dtok_ref, dtok_out, *outs):
    dtok_out[...] = dtok_ref[...]
    for block in range(2):
        gain, qkv, out, bias = outs[4 * block : 4 * block + 4]
        at = block * 2 * HALF

        def rows(count):
            nonlocal at
            at += count
            return in_ref[at - count : at, :].astype(F32)

        gq, gk, gv, go = (rows(C) for _ in range(4))
        one, two = rows(C), rows(C)
        qkv[...] = jnp.concatenate(
            [gq, one[:, :64], gk, one[:, 64:], gv, two[:, :64]], axis=1
        )
        out[...] = jnp.concatenate([go, two[:, 64:]], axis=1)
        main = [rows(WT) for _ in range(HEADS)]
        tails = rows(WT)
        for h in range(HEADS):
            bias[h] = jnp.concatenate([main[h], tails[:, 16 * h : 16 * h + 16]], axis=1)
        last = rows(16)
        gain[...] = jnp.concatenate([last[0:1, :], last[1:2, :64]], axis=1)


def saves():
    return (
        pltpu.VMEM((TOK, C), F32),
        pltpu.VMEM((TOK, 1), F32),
        pltpu.VMEM((TOK, C), BF16),
        pltpu.VMEM((TOK, C), BF16),
        pltpu.VMEM((TOK, C), BF16),
        pltpu.VMEM((TOK, C), BF16),
        pltpu.VMEM((WINDOWS, HEADS * WT, WT), BF16),
        pltpu.VMEM((TOK, C), BF16),
    )


def rooms():
    return (
        pltpu.VMEM((WINDOWS, HEADS * WT, WT), F32),
        pltpu.VMEM((WINDOWS, HEADS * WT, WT), BF16),
    )


def totals():
    return (
        pltpu.VMEM((C, C), F32),
        pltpu.VMEM((C, C), F32),
        pltpu.VMEM((C, C), F32),
        pltpu.VMEM((C, C), F32),
        pltpu.VMEM((HEADS, WT, WT), F32),
        pltpu.VMEM((1, C), F32),
    )


def parts(lons):
    piece = (PIECE, 128)
    return (
        (pltpu.VMEM((SPOTS,) + piece, BF16),) * 3
        + (pltpu.VMEM((lons,) + piece, BF16),)
        + (pltpu.SemaphoreType.DMA((SPOTS,)),) * 4
        + (pltpu.SemaphoreType.DMA((lons,)),) * 2
        + (pltpu.SemaphoreType.DMA((SPOTS,)),) * 4
    )


def run_layer(lats, lons, *args):
    return pl.pallas_call(
        functools.partial(layer_kernel, lats, lons, Sum),
        out_shape=(
            pltpu.VMEM((TOK, C), BF16),
            pltpu.VMEM((2, 2, SPOTS, PIECE, 128), BF16),
        ),
        in_specs=[pl.BlockSpec(memory_space=pl.ANY)] * 11,
        out_specs=(pl.BlockSpec(memory_space=pltpu.VMEM),) * 2,
        scratch_shapes=[
            tuple(pltpu.VMEM(arg.shape, arg.dtype) for arg in args),
            pltpu.SemaphoreType.DMA((11,)),
            pltpu.VMEM((2, HEADS, WT, WT), F32),
            rooms(),
            saves(),
            saves(),
            totals(),
            totals(),
            pltpu.VMEM((TOK, TOK), BF16),
            pltpu.VMEM((16 * SLOT, TOK), BF16),
            pltpu.VMEM((2, 4 * SLOT, 72), BF16),
            pltpu.VMEM((WT, 4 * SLOT), BF16),
            pltpu.VMEM((4 * SLOT, WT), BF16),
            pltpu.VMEM((2, 72, 4 * SLOT), BF16),
            pltpu.VMEM((2, WT, WT), F32),
            pltpu.VMEM((TOK, C), BF16),
            pltpu.VMEM((LEVELS, 72, C), BF16),
            pltpu.VMEM((LEVELS, 72, C), F32),
            pltpu.VMEM((3, 4, WINDOWS, SLOT, C), BF16),
            pltpu.VMEM((3, 4, WINDOWS, SLOT, C), BF16),
            pltpu.SemaphoreType.DMA((27,)),
            pltpu.SemaphoreType.DMA((27,)),
            pltpu.VMEM((2, 2, SPOTS, PIECE, 128), BF16),
            parts(lons),
            parts(lons),
        ],
        compiler_params=pltpu.CompilerParams(
            collective_id=0, has_side_effects=True, vmem_limit_bytes=VMEM_LIMIT
        ),
        name="layer",
    )(*args)


def run_unpack(summed, d_tokens):
    block = (
        jax.ShapeDtypeStruct((1, C), F32),
        jax.ShapeDtypeStruct((C, 3 * C), F32),
        jax.ShapeDtypeStruct((C, C), F32),
        jax.ShapeDtypeStruct((HEADS, WT, WT), F32),
    )
    return pl.pallas_call(
        unpack_kernel,
        out_shape=(jax.ShapeDtypeStruct((TOK, C), BF16),) + block + block,
        in_specs=[pl.BlockSpec(memory_space=pltpu.VMEM)] * 2,
        out_specs=(pl.BlockSpec(memory_space=pltpu.VMEM),) * 9,
        compiler_params=pltpu.CompilerParams(vmem_limit_bytes=UNPACK_LIMIT),
        name="unpack",
    )(summed, d_tokens)


def solution(mesh):
    lats, lons = mesh.shape["lat"], mesh.shape["lon"]
    route = routes()

    def stored(grid):
        return grid.transpose(0, 2, 3, 1, 4).reshape(TOK, C)

    def local(tokens, cotangent, gain_a, qkv_a, out_a, bias_a, gain_b, qkv_b, out_b, bias_b):
        d_tokens, summed = run_layer(
            lats,
            lons,
            stored(tokens),
            stored(cotangent),
            gain_a.reshape(1, C),
            qkv_a,
            out_a,
            bias_a,
            gain_b.reshape(1, C),
            qkv_b,
            out_b,
            bias_b,
            jnp.asarray(route),
        )
        d_tokens, ga, qa, oa, ba, gb, qb, ob, bb = run_unpack(
            summed.reshape(4 * HALF, 128), d_tokens
        )
        d_tokens = d_tokens.reshape(1, 6, 12, LEVELS, C).transpose(0, 3, 1, 2, 4)
        return (
            d_tokens,
            ga.reshape(C),
            qa,
            oa,
            ba,
            gb.reshape(C),
            qb,
            ob,
            bb,
        )

    grid = P("rep", None, "lat", "lon", None)
    return jax.shard_map(
        local,
        mesh=mesh,
        in_specs=(grid, grid) + (P(),) * 8,
        out_specs=(grid,) + (P(),) * 8,
        check_vma=False,
    )
```

```python
import functools

import jax
import jax.numpy as jnp
import numpy as np
from jax import lax
from jax.experimental import pallas as pl
from jax.experimental.pallas import tpu as pltpu
from jax.sharding import PartitionSpec as P

MESH = pl.DeviceIdType.MESH
C = 192
HEADS = 6
HEAD = 32
WT = 144
LEVELS = 8
WINDOWS = 4
TOK = WT * WINDOWS
FACTOR = HEAD ** (-0.5)
F32 = jnp.float32
BF16 = jnp.bfloat16
PIECE = 80
SPOTS = 16
HALF = PIECE * SPOTS
STEP = 144
GROUPS = ((0, 4, 0, 128), (4, 6, 128, 192))
LOG2E = 1.4426950408889634
SLOT = 48
VMEM_LIMIT = 56 * 1024 * 1024
UNPACK_LIMIT = 16 * 1024 * 1024


def nt(left, right):
    return lax.dot_general(left, right, (((1,), (1,)), ((), ())), preferred_element_type=F32)


def tn(left, right):
    return lax.dot_general(left, right, (((0,), (0,)), ((), ())), preferred_element_type=F32)


def nn(left, right):
    return lax.dot_general(left, right, (((1,), (0,)), ((), ())), preferred_element_type=F32)


def routes():
    out = np.full((16, TOK), -1, np.int32)
    for z in range(LEVELS):
        for i in range(6):
            for j in range(12):
                stored = (i * 12 + j) * LEVELS + z
                token = z * 72 + i * 12 + j
                out[0, stored] = token
                out[1, token] = stored
                zr, ir, jr = (z - 1) % LEVELS, (i + 3) % 6, (j + 6) % 12
                quarter = 2 * (ir >= 3) + (jr >= 6)
                window, level = zr // 2, zr % 2
                inside = level * 18 + (ir % 3) * 6 + jr % 6
                slot = quarter * SLOT + inside
                place = level * 72 + ir * 12 + jr
                column = i * 12 + j
                out[2, stored] = (quarter * WINDOWS + window) * SLOT + inside
                out[3 + level, column] = slot
                out[5, slot] = place
                out[6, place] = slot
                out[7 + level, slot] = column
    return out


def head_mask(h, dtype):
    lane = lax.broadcasted_iota(jnp.int32, (1, C), 1)
    return jnp.where((lane >= h * HEAD) & (lane < (h + 1) * HEAD), 1.0, 0.0).astype(dtype)


def spread(value):
    return [
        jnp.concatenate(
            [value[:, lo:hi] * head_mask(h, BF16)[:, lo:hi] for h in range(first, last)], axis=0
        )
        for first, last, lo, hi in GROUPS
    ]


def gather_heads(stacked):
    parts = []
    for group, (first, last, lo, hi) in zip(stacked, GROUPS):
        lane = lax.broadcasted_iota(jnp.int32, (1, hi - lo), 1)
        total = group[:WT]
        for n in range(1, last - first):
            total = jnp.where(lane >= n * HEAD, group[n * WT : (n + 1) * WT], total)
        parts.append(total)
    return jnp.concatenate(parts, axis=1)


def stacked_rows(first, last):
    return slice(first * WT, last * WT)


def window_forward(w, x, gain, wq, wk, wv, bias, extra, save):
    (unit_s, inv_s, normed_s, q_s, k_s, v_s, p_s, att_s), (s_s, d_s) = save
    rows = pl.ds(w * WT, WT)
    xf = x.astype(F32)
    center = xf - jnp.mean(xf, axis=-1, keepdims=True)
    inv = lax.rsqrt(jnp.mean(center * center, axis=-1, keepdims=True) + 1e-05)
    unit = center * inv
    normed = (unit * gain).astype(BF16)
    unit_s[rows, :] = unit
    inv_s[rows, :] = inv
    normed_s[rows, :] = normed
    q = (nn(normed, wq) * (FACTOR * LOG2E)).astype(BF16)
    k = nn(normed, wk).astype(BF16)
    v = nn(normed, wv).astype(BF16)
    q_s[rows, :] = q
    k_s[rows, :] = k
    v_s[rows, :] = v
    for left, (head, stop, lo, hi) in zip(spread(q), GROUPS):
        s_s[w, stacked_rows(head, stop), :] = nt(left, k[:, lo:hi])
    for at in range(0, HEADS * WT, STEP):
        h, first = at // WT, at % WT
        s = s_s[w, at : at + STEP, :] + bias[h, first : first + STEP, :]
        if extra is not None:
            s = s + extra[first : first + STEP]
        e = jnp.exp2(s - jnp.max(s, axis=-1, keepdims=True))
        p = (e * (1.0 / jnp.sum(e, axis=-1, keepdims=True))).astype(BF16)
        p_s[w, at : at + STEP, :] = p
    att = gather_heads(
        [nn(p_s[w, stacked_rows(head, stop), :], v[:, lo:hi]) for head, stop, lo, hi in GROUPS]
    ).astype(BF16)
    att_s[rows, :] = att
    return xf, att


def window_backward(w, first_one, g, gain, wq, wk, wv, wo, save, grads):
    (unit_s, inv_s, normed_s, q_s, k_s, v_s, p_s, att_s), (s_s, d_s) = save
    gq_s, gk_s, gv_s, go_s, gb_s, gg_s = grads
    rows = pl.ds(w * WT, WT)

    def add(ref, index, value):
        ref[index] = value if first_one else ref[index] + value

    add(go_s, ..., tn(att_s[rows, :], g))
    da = spread(nt(g, wo).astype(BF16))
    v = v_s[rows, :]
    k = k_s[rows, :]
    dvs = []
    for left, (head, stop, lo, hi) in zip(da, GROUPS):
        s_s[w, stacked_rows(head, stop), :] = nt(left, v[:, lo:hi])
        dvs.append(tn(p_s[w, stacked_rows(head, stop), :], left))
    dv = jnp.concatenate(dvs, axis=1).astype(BF16)
    for at in range(0, HEADS * WT, STEP):
        h, first = at // WT, at % WT
        pf = p_s[w, at : at + STEP, :].astype(F32)
        t = pf * s_s[w, at : at + STEP, :]
        ds = t - pf * jnp.sum(t, axis=-1, keepdims=True)
        add(gb_s, (h, slice(first, first + STEP), slice(None)), ds)
        d_s[w, at : at + STEP, :] = ds.astype(BF16)
    dks, dqs = [], []
    for left, (head, stop, lo, hi) in zip(spread(q_s[rows, :]), GROUPS):
        ds = d_s[w, stacked_rows(head, stop), :]
        dks.append(tn(ds, left))
        dqs.append(nn(ds, k[:, lo:hi]))
    dk = (jnp.concatenate(dks, axis=1) * (1.0 / LOG2E)).astype(BF16)
    dq = (gather_heads(dqs) * FACTOR).astype(BF16)
    normed = normed_s[rows, :]
    add(gq_s, ..., tn(normed, dq))
    add(gk_s, ..., tn(normed, dk))
    add(gv_s, ..., tn(normed, dv))
    dn = nt(dq, wq) + nt(dk, wk) + nt(dv, wv)
    unit = unit_s[rows, :]
    add(gg_s, ..., jnp.sum(dn * unit, axis=0, keepdims=True))
    dh = dn * gain
    d_in = g.astype(F32) + inv_s[rows, :] * (
        dh
        - jnp.mean(dh, axis=-1, keepdims=True)
        - unit * jnp.mean(dh * unit, axis=-1, keepdims=True)
    )
    return d_in.astype(BF16)


def pack(out, grads):
    gq_s, gk_s, gv_s, go_s, gb_s, gg_s = grads
    at = 0

    def put(value):
        nonlocal at
        value = value.astype(BF16)
        done = 0
        while done < value.shape[0]:
            piece, first = (at + done) // PIECE, (at + done) % PIECE
            count = min(PIECE - first, value.shape[0] - done)
            out[piece // SPOTS, piece % SPOTS, first : first + count, :] = value[done : done + count]
            done += count
        at += value.shape[0]

    for ref in (gq_s, gk_s, gv_s, go_s):
        put(ref[:, :128])
    for one, two in ((gq_s, gk_s), (gv_s, go_s)):
        put(jnp.concatenate([one[:, 128:], two[:, 128:]], axis=1))
    for h in range(HEADS):
        put(gb_s[h, :, :128])
    tails = [gb_s[h, :, 128:] for h in range(HEADS)] + [jnp.zeros((WT, 32), F32)]
    put(jnp.concatenate(tails, axis=1))
    gg = gg_s[...]
    second = jnp.concatenate([gg[:, 128:], jnp.zeros((1, 64), F32)], axis=1)
    put(jnp.concatenate([gg[:, :128], second, jnp.zeros((14, 128), F32)], axis=0))
    put(jnp.zeros((2 * HALF - at, 128), F32))


def ring_distance(step, count):
    return min(step, count - step)


FAR_FIRST = sorted(
    range(1, SPOTS), key=lambda k: -ring_distance(k // 4, 4) - ring_distance(k % 4, 4)
)


class Sum:
    def __init__(self, lon_count, refs):
        self.in_ref, self.out_ref, self.core_s, self.part_s, self.plane_s, self.line_s = refs[:6]
        self.sems = refs[6:]
        rep, lat = lax.axis_index("rep"), lax.axis_index("lat")
        self.lon = lax.axis_index("lon")
        self.lons = lon_count
        self.core = rep % 2
        x_hi, x_lo, y = rep // 2, lat // 4, lat % 4
        self.x, self.y = x_hi * 2 + x_lo, y
        self.me = self.x * 4 + y
        self.far_line = sorted(range(1, lon_count), key=lambda k: -ring_distance(k, lon_count))
        self.partner = {"rep": x_hi * 2 + (1 - self.core)}

    def there(self, k):
        return lax.rem(self.x + k // 4, 4) * 4 + lax.rem(self.y + k % 4, 4)

    def origin(self, k):
        return lax.rem(self.x + 4 - k // 4, 4) * 4 + lax.rem(self.y + 4 - k % 4, 4)

    def spot(self, k):
        x, y = lax.rem(self.x + k // 4, 4), lax.rem(self.y + k % 4, 4)
        return {"rep": (x // 2) * 2 + self.core, "lat": (x % 2) * 4 + y}

    def neighbour(self, k):
        return {"lon": lax.rem(self.lon + k, self.lons)}

    def greet(self, barrier):
        pl.semaphore_signal(barrier, inc=1, device_id=self.partner, device_id_type=MESH)

        def greet_plane(k, carry):
            pl.semaphore_signal(barrier, inc=1, device_id=self.spot(k), device_id_type=MESH)
            return carry

        def greet_line(k, carry):
            pl.semaphore_signal(barrier, inc=1, device_id=self.neighbour(k), device_id_type=MESH)
            return carry

        lax.fori_loop(1, SPOTS, greet_plane, 0)
        lax.fori_loop(1, self.lons, greet_line, 0)
        return SPOTS + self.lons - 1

    def copy(self, pair, k, source, target, device):
        return pltpu.make_async_remote_copy(
            src_ref=source,
            dst_ref=target,
            send_sem=self.sems[2 * pair].at[k],
            recv_sem=self.sems[2 * pair + 1].at[k],
            device_id=device,
            device_id_type=MESH,
        )

    def group(self, dx):
        return pl.ds(lax.rem(self.x + 4 + dx, 4) * 4, 4)

    def core_copy(self, dx):
        part = self.group(dx)
        source = self.in_ref.at[1 - self.core, part]
        return self.copy(0, dx, source, self.core_s.at[part], self.partner)

    def plane_copy(self, k):
        return self.copy(1, k, self.part_s.at[k], self.plane_s.at[k], self.spot(k))

    def line_copy(self, k, slot):
        return self.copy(2, k, self.line_s.at[slot], self.line_s.at[slot], self.neighbour(k))

    def back_copy(self, k, j):
        ref = self.out_ref.at[self.core, j]
        return self.copy(3, k, ref, ref, self.spot(k))

    def last_copy(self, dx, half):
        ref = self.out_ref.at[half, self.group(-dx)]
        return self.copy(4, dx, ref, ref, self.partner)

    def merge(self, k):
        j = self.there(k)
        return self.in_ref[self.core, j].astype(F32) + self.core_s[j].astype(F32)

    def loop(self, first, last, step):
        def body(k, carry):
            step(k)
            return carry

        lax.fori_loop(first, last, body, 0)

    def start_core(self):
        for dx in (2, 1, 3, 0):
            self.core_copy(dx).start()

    def start_plane(self):
        for dx in (2, 1, 3, 0):
            self.core_copy(dx).wait()
            for dy in (2, 1, 3, 0):
                k = dx * 4 + dy
                if k:
                    self.part_s[k] = self.merge(k).astype(BF16)
                    self.plane_copy(k).start()

    def start_line(self):
        def add(k, total):
            self.plane_copy(k).wait()
            return total + self.plane_s[k].astype(F32)

        total = lax.fori_loop(1, SPOTS, add, self.merge(0))
        self.line_s[self.lon] = total.astype(BF16)
        for k in self.far_line:
            self.line_copy(k, self.lon).start()

    def start_back(self):
        def wait(k):
            self.line_copy(k, self.lon).wait_send()
            self.line_copy(k, lax.rem(self.lon + self.lons - k, self.lons)).wait_recv()

        self.loop(1, self.lons, wait)
        total = self.line_s[0].astype(F32)
        for n in range(1, self.lons):
            total = total + self.line_s[n].astype(F32)
        self.out_ref[self.core, self.me] = total.astype(BF16)
        for k in FAR_FIRST:
            self.back_copy(k, self.me).start()

    def start_last(self):
        for dx in (0, 1, 3, 2):
            for dy in (0, 1, 3, 2):
                k = dx * 4 + dy
                if k:
                    self.back_copy(k, self.origin(k)).wait_recv()
            self.last_copy(dx, self.core).start()

    def finish(self):
        self.loop(1, SPOTS, lambda k: self.back_copy(k, self.me).wait_send())
        for dx in range(4):
            self.last_copy(dx, self.core).wait_send()
            self.last_copy(dx, 1 - self.core).wait_recv()


def layer_kernel(
    lats,
    lons,
    make_sum,
    tok_ref,
    cot_ref,
    gain_a,
    qkv_a,
    out_a,
    bias_a,
    gain_b,
    qkv_b,
    out_b,
    bias_b,
    route_ref,
    dtok_ref,
    sum_ref,
    inputs_s,
    input_sem,
    scaled_s,
    room,
    save_a,
    save_b,
    grad_a,
    grad_b,
    order_s,
    slots_s,
    ahead_s,
    place_s,
    back_s,
    home_s,
    extra_s,
    x_a,
    mid_s,
    dmid_s,
    send_s,
    recv_s,
    send_sem,
    recv_sem,
    packed_s,
    parts_a,
    parts_b,
):
    lat = lax.axis_index("lat")
    lon = lax.axis_index("lon")
    save_a, save_b = (save_a, room), (save_b, room)

    def shifted(dlat, dlon):
        return {"lat": lax.rem(lat + dlat + lats, lats), "lon": lax.rem(lon + dlon + lons, lons)}

    before = [shifted(0, -1), shifted(-1, 0), shifted(-1, -1)]
    after = [shifted(0, 1), shifted(1, 0), shifted(1, 1)]

    def quarters(leg, window):
        copies = []
        for n, target in enumerate(after if leg == 2 else before):
            at = (leg, n + 1) if window is None else (leg, n + 1, window)
            sem = n if window is None else 3 + (leg - 1) * 12 + window * 3 + n
            copies.append(
                pltpu.make_async_remote_copy(
                    src_ref=send_s.at[at],
                    dst_ref=recv_s.at[at],
                    send_sem=send_sem.at[sem],
                    recv_sem=recv_sem.at[sem],
                    device_id=target,
                    device_id_type=MESH,
                )
            )
        return copies

    def post(leg, window, value):
        value = value.astype(BF16)
        recv_s[leg, 0, window] = value[:SLOT]
        for n in range(1, 4):
            send_s[leg, n, window] = value[n * SLOT : (n + 1) * SLOT]
        copies = quarters(leg, window)
        for copy in copies:
            copy.start()
        return copies

    def arrived(leg, window):
        return recv_s[leg, :, window].reshape(4 * SLOT, C)

    sources = (
        tok_ref, cot_ref, gain_a, qkv_a, out_a, bias_a, gain_b, qkv_b, out_b, bias_b, route_ref
    )
    loads = [
        pltpu.make_async_copy(source, target, input_sem.at[n])
        for n, (source, target) in enumerate(zip(sources, inputs_s))
    ]
    for n in (10, 0, 2, 3, 4, 5, 1, 6, 7, 8, 9):
        loads[n].start()
    tok_ref, cot_ref, gain_a, qkv_a, out_a, bias_a, gain_b, qkv_b, out_b, bias_b, route_ref = inputs_s

    sum_a = make_sum(lons, (packed_s.at[0], sum_ref.at[0]) + parts_a)
    sum_b = make_sum(lons, (packed_s.at[1], sum_ref.at[1]) + parts_b)

    barrier = pltpu.get_barrier_semaphore()
    for other in before + after:
        pl.semaphore_signal(barrier, inc=1, device_id=other, device_id_type=MESH)
    greeted = 6 + sum_a.greet(barrier)

    def one_hot(rows, row, columns):
        target = route_ref[row : row + 1, :columns]
        spot = lax.broadcasted_iota(jnp.int32, (rows, columns), 0)
        return jnp.where(spot == target, 1.0, 0.0).astype(BF16)

    loads[10].wait()
    loads[0].wait()
    x_a[...] = nn(one_hot(TOK, 0, TOK), tok_ref[...]).astype(BF16)
    for n in (2, 3, 4, 5):
        loads[n].wait()
    scaled_s[0] = bias_a[...] * LOG2E
    slots_s[...] = one_hot(16 * SLOT, 2, TOK)
    for n in range(2):
        ahead_s[n] = one_hot(4 * SLOT, 3 + n, 72)

    ga = gain_a[...]
    wo = out_a[...]
    wqa, wka, wva = (qkv_a[:, n * C : (n + 1) * C] for n in range(3))
    mids = [None] * WINDOWS
    backs = [None] * WINDOWS

    def send_mid(w):
        levels = (2 * w + 1, (2 * w + 2) % LEVELS)
        mids[w] = post(1, w, nn(ahead_s[0], mid_s[levels[0]]) + nn(ahead_s[1], mid_s[levels[1]]))

    for w in range(WINDOWS):
        xf, att = window_forward(w, x_a[w * WT : (w + 1) * WT, :], ga, wqa, wka, wva, scaled_s.at[0], None, save_a)
        middle = xf + nn(att, wo)
        mid_s[2 * w] = middle[:72].astype(BF16)
        mid_s[2 * w + 1] = middle[72:].astype(BF16)
        if w == 0:
            loads[1].wait()
            cots = nn(slots_s[...], cot_ref[...]).astype(BF16)
            cots = cots.reshape(4, WINDOWS, SLOT, C)
            recv_s[0, 0] = cots[0]
            for n in range(1, 4):
                send_s[0, n] = cots[n]
        else:
            if w == 1:
                pl.semaphore_wait(barrier, greeted)
                cot_copies = quarters(0, None)
                for copy in cot_copies:
                    copy.start()
            send_mid(w - 1)
    send_mid(WINDOWS - 1)

    order_s[...] = one_hot(TOK, 1, TOK)
    place_s[...] = one_hot(WT, 5, 4 * SLOT)
    back_s[...] = one_hot(4 * SLOT, 6, WT)
    for n in range(2):
        home_s[n] = one_hot(72, 7 + n, 4 * SLOT)
    for n in (6, 7, 8, 9):
        loads[n].wait()
    scaled_s[1] = bias_b[...] * LOG2E

    def label(shape, axis, level):
        at = lax.broadcasted_iota(jnp.int32, shape, axis)
        upper = jnp.where(at >= 72, 1, 0)
        inside = at - 72 * upper
        late = jnp.where(inside >= 36, 1, 0) * jnp.where(lat == lats - 1, 1, 0)
        return late + 2 * upper if level else late

    for n in range(2):
        same = label((WT, WT), 0, n) == label((WT, WT), 1, n)
        extra_s[n] = jnp.where(same, 0.0, -1e30)

    gb = gain_b[...]
    wob = out_b[...]
    wqb, wkb, wvb = (qkv_b[:, n * C : (n + 1) * C] for n in range(3))

    for copy in cot_copies:
        copy.wait()
    gs = [None] * WINDOWS

    def shifted_forward(w):
        for copy in mids[w]:
            copy.wait()
        x = nn(place_s[...], arrived(1, w)).astype(BF16)
        gs[w] = nn(place_s[...], arrived(0, w)).astype(BF16)
        extra = extra_s.at[w // (WINDOWS - 1)]
        window_forward(w, x, gb, wqb, wkb, wvb, scaled_s.at[1], extra, save_b)

    shifted_forward(0)
    for w in range(WINDOWS):
        if w + 1 < WINDOWS:
            shifted_forward(w + 1)
        d_in = window_backward(w, w == 0, gs[w], gb, wqb, wkb, wvb, wob, save_b, grad_b)
        backs[w] = post(2, w, nn(back_s[...], d_in))

    pack(packed_s.at[1], grad_b)
    sum_b.start_core()

    def take_back(w):
        for copy in backs[w]:
            copy.wait()
        value = arrived(2, w)
        dmid_s[2 * w + 1] = nn(home_s[0], value)
        dmid_s[(2 * w + 2) % LEVELS] = nn(home_s[1], value)

    def regular_back(w, first_one):
        g = jnp.concatenate([dmid_s[2 * w], dmid_s[2 * w + 1]], axis=0).astype(BF16)
        x_a[w * WT : (w + 1) * WT, :] = window_backward(
            w, first_one, g, ga, wqa, wka, wva, wo, save_a, grad_a
        )

    take_back(0)
    take_back(1)
    regular_back(1, True)
    sum_b.start_plane()
    take_back(2)
    regular_back(2, False)
    take_back(3)
    regular_back(3, False)
    regular_back(0, False)
    pack(packed_s.at[0], grad_a)
    sum_a.start_core()
    sum_a.start_plane()
    dtok_ref[...] = nn(order_s[...], x_a[...]).astype(BF16)
    sum_b.start_line()
    sum_a.start_line()
    sum_b.start_back()
    sum_a.start_back()
    sum_b.start_last()
    sum_a.start_last()
    sum_b.finish()
    sum_a.finish()


def unpack_kernel(in_ref, dtok_ref, dtok_out, *outs):
    dtok_out[...] = dtok_ref[...]
    for block in range(2):
        gain, qkv, out, bias = outs[4 * block : 4 * block + 4]
        at = block * 2 * HALF

        def rows(count):
            nonlocal at
            at += count
            return in_ref[at - count : at, :].astype(F32)

        gq, gk, gv, go = (rows(C) for _ in range(4))
        one, two = rows(C), rows(C)
        qkv[...] = jnp.concatenate(
            [gq, one[:, :64], gk, one[:, 64:], gv, two[:, :64]], axis=1
        )
        out[...] = jnp.concatenate([go, two[:, 64:]], axis=1)
        main = [rows(WT) for _ in range(HEADS)]
        tails = rows(WT)
        for h in range(HEADS):
            bias[h] = jnp.concatenate([main[h], tails[:, 16 * h : 16 * h + 16]], axis=1)
        last = rows(16)
        gain[...] = jnp.concatenate([last[0:1, :], last[1:2, :64]], axis=1)


def saves():
    return (
        pltpu.VMEM((TOK, C), F32),
        pltpu.VMEM((TOK, 1), F32),
        pltpu.VMEM((TOK, C), BF16),
        pltpu.VMEM((TOK, C), BF16),
        pltpu.VMEM((TOK, C), BF16),
        pltpu.VMEM((TOK, C), BF16),
        pltpu.VMEM((WINDOWS, HEADS * WT, WT), BF16),
        pltpu.VMEM((TOK, C), BF16),
    )


def rooms():
    return (
        pltpu.VMEM((WINDOWS, HEADS * WT, WT), F32),
        pltpu.VMEM((WINDOWS, HEADS * WT, WT), BF16),
    )


def totals():
    return (
        pltpu.VMEM((C, C), F32),
        pltpu.VMEM((C, C), F32),
        pltpu.VMEM((C, C), F32),
        pltpu.VMEM((C, C), F32),
        pltpu.VMEM((HEADS, WT, WT), F32),
        pltpu.VMEM((1, C), F32),
    )


def parts(lons):
    piece = (PIECE, 128)
    return (
        (pltpu.VMEM((SPOTS,) + piece, BF16),) * 3
        + (pltpu.VMEM((lons,) + piece, BF16),)
        + (pltpu.SemaphoreType.DMA((SPOTS,)),) * 4
        + (pltpu.SemaphoreType.DMA((lons,)),) * 2
        + (pltpu.SemaphoreType.DMA((SPOTS,)),) * 4
    )


def run_layer(lats, lons, *args):
    return pl.pallas_call(
        functools.partial(layer_kernel, lats, lons, Sum),
        out_shape=(
            pltpu.VMEM((TOK, C), BF16),
            pltpu.VMEM((2, 2, SPOTS, PIECE, 128), BF16),
        ),
        in_specs=[pl.BlockSpec(memory_space=pl.ANY)] * 11,
        out_specs=(pl.BlockSpec(memory_space=pltpu.VMEM),) * 2,
        scratch_shapes=[
            tuple(pltpu.VMEM(arg.shape, arg.dtype) for arg in args),
            pltpu.SemaphoreType.DMA((11,)),
            pltpu.VMEM((2, HEADS, WT, WT), F32),
            rooms(),
            saves(),
            saves(),
            totals(),
            totals(),
            pltpu.VMEM((TOK, TOK), BF16),
            pltpu.VMEM((16 * SLOT, TOK), BF16),
            pltpu.VMEM((2, 4 * SLOT, 72), BF16),
            pltpu.VMEM((WT, 4 * SLOT), BF16),
            pltpu.VMEM((4 * SLOT, WT), BF16),
            pltpu.VMEM((2, 72, 4 * SLOT), BF16),
            pltpu.VMEM((2, WT, WT), F32),
            pltpu.VMEM((TOK, C), BF16),
            pltpu.VMEM((LEVELS, 72, C), BF16),
            pltpu.VMEM((LEVELS, 72, C), F32),
            pltpu.VMEM((3, 4, WINDOWS, SLOT, C), BF16),
            pltpu.VMEM((3, 4, WINDOWS, SLOT, C), BF16),
            pltpu.SemaphoreType.DMA((27,)),
            pltpu.SemaphoreType.DMA((27,)),
            pltpu.VMEM((2, 2, SPOTS, PIECE, 128), BF16),
            parts(lons),
            parts(lons),
        ],
        compiler_params=pltpu.CompilerParams(
            collective_id=0, has_side_effects=True, vmem_limit_bytes=VMEM_LIMIT
        ),
        name="layer",
    )(*args)


def run_unpack(summed, d_tokens):
    block = (
        jax.ShapeDtypeStruct((1, C), F32),
        jax.ShapeDtypeStruct((C, 3 * C), F32),
        jax.ShapeDtypeStruct((C, C), F32),
        jax.ShapeDtypeStruct((HEADS, WT, WT), F32),
    )
    return pl.pallas_call(
        unpack_kernel,
        out_shape=(jax.ShapeDtypeStruct((TOK, C), BF16),) + block + block,
        in_specs=[pl.BlockSpec(memory_space=pltpu.VMEM)] * 2,
        out_specs=(pl.BlockSpec(memory_space=pltpu.VMEM),) * 9,
        compiler_params=pltpu.CompilerParams(vmem_limit_bytes=UNPACK_LIMIT),
        name="unpack",
    )(summed, d_tokens)


def solution(mesh):
    lats, lons = mesh.shape["lat"], mesh.shape["lon"]
    route = routes()

    def stored(grid):
        return grid.transpose(0, 2, 3, 1, 4).reshape(TOK, C)

    def local(tokens, cotangent, gain_a, qkv_a, out_a, bias_a, gain_b, qkv_b, out_b, bias_b):
        d_tokens, summed = run_layer(
            lats,
            lons,
            stored(tokens),
            stored(cotangent),
            gain_a.reshape(1, C),
            qkv_a,
            out_a,
            bias_a,
            gain_b.reshape(1, C),
            qkv_b,
            out_b,
            bias_b,
            jnp.asarray(route),
        )
        d_tokens, ga, qa, oa, ba, gb, qb, ob, bb = run_unpack(
            summed.reshape(4 * HALF, 128), d_tokens
        )
        d_tokens = d_tokens.reshape(1, 6, 12, LEVELS, C).transpose(0, 3, 1, 2, 4)
        return (
            d_tokens,
            ga.reshape(C),
            qa,
            oa,
            ba,
            gb.reshape(C),
            qb,
            ob,
            bb,
        )

    grid = P("rep", None, "lat", "lon", None)
    return jax.shard_map(
        local,
        mesh=mesh,
        in_specs=(grid, grid) + (P(),) * 8,
        out_specs=(grid,) + (P(),) * 8,
        check_vma=False,
    )
```
